128 devices in a mesh: gx: 16 (over x, z_lo, core), gy: 8 (over y, z_hi).
Axes of the slice: x: 4, y: 4, z: 4 (z_hi: 2, z_lo: 2; z = z_hi * 2 + z_lo), core: 2. Of those that a mesh axis runs over, the one named last changes fastest.
Arguments:
- fine_input: float32 [64, 64, 128, 256], P(None, 'gx', 'gy'), may hold values from -34 to 34
- weights: float32 [27, 128, 64], replicated, may hold values from -0.15625 to 0.15625
- norm_gain: float32 [128], P(('gx', 'gy')), may hold values from 0.5 to 2
- norm_shift: float32 [128], P(('gx', 'gy')), may hold values from -3 to 3
- cotangent: float32 [128, 32, 64, 128], P(('gx', 'gy')), may hold values from -6 to 6
Outputs:
- activated: float32 [128, 32, 64, 128], P(('gx', 'gy'))
- grad_input: float32 [64, 64, 128, 256], P(None, 'gx', 'gy')
- grad_weights: float32 [27, 128, 64], replicated
- grad_gain: float32 [128], P(('gx', 'gy'))
- grad_shift: float32 [128], P(('gx', 'gy'))
The draws below stay inside these ranges and needn't reach their ends.
All inputs are finite; a program needn't handle non-finite values.
Results may differ from the reference program's by a relative error of at most 0.00026.
Values sent between devices are 32-bit elements; how exact they have to be, the bound alone decides.
A program may use at most 128 MiB of HBM per device.

```python
import math
import jax
import jax.numpy as jnp
from jax import lax

CI = 64
CO = 128
KERN = 27
NZ = 256
NX = 64
NY = 128
MX = 32
MY = 64
MZ = 128


def draw_fine_input(key, part):
    key = jax.random.fold_in(key, 7)
    keys = jax.random.split(key, 4)
    top = math.log(10.0) / 3.0
    chan_scale = jnp.exp(jax.random.uniform(keys[0], (CI, 1, 1, 1), jnp.float32, 0.0, top))
    x_scale = jnp.exp(jax.random.uniform(keys[1], (1, NX, 1, 1), jnp.float32, 0.0, top))
    y_scale = jnp.exp(jax.random.uniform(keys[2], (1, 1, NY, 1), jnp.float32, 0.0, top))
    noise = jnp.clip(jax.random.normal(keys[3], (CI, NX, NY, NZ), jnp.float32), -3.0, 3.0)
    return (noise * chan_scale * x_scale * y_scale).astype(jnp.float32)


def shard_levels(key, shape, cuts, smallest, largest):
    level = 1.0
    for dim, shards_of in cuts:
        steps = jax.random.uniform(jax.random.fold_in(jax.random.fold_in(key, 6), dim), (shards_of,), jnp.float32, smallest / len(cuts), largest / len(cuts))
        level = level * jnp.repeat(jnp.exp(steps), shape[dim] // shards_of).reshape((-1,) + (1,) * (len(shape) - 1 - dim))
    return level


def bell_draw(stream_key, extent, scale, reach, pieces=(), kind=jnp.bfloat16):
    result = jax.random.normal(stream_key, extent, jnp.float32) * scale
    if len(pieces) > 0:
        result = shard_levels(stream_key, extent, pieces, -0.22, 0.18) * result
    return jnp.clip(result, min=-reach, max=reach).astype(kind)


def setup_inputs(seed: int = 0) -> dict:
    streams_of = jax.random.split(jax.random.key(seed), 6)
    return {
        "fine_input": draw_fine_input(jax.random.fold_in(streams_of[5], 71), 0),
        "weights": bell_draw(streams_of[1], (KERN, CO, CI), (27 * CI) ** -0.5, 0.15625, (), jnp.float32),
        "norm_gain": jnp.clip(jnp.exp(math.log(2.0) - 1.3862944 * jax.random.uniform(streams_of[2], (CO,), jnp.float32) ** shard_levels(streams_of[2], (CO,), ((0, 128),), -0.2, 0.2)), 0.5, 2.0),
        "norm_shift": bell_draw(streams_of[3], (CO,), 0.5, 3.0, ((0, 128),), jnp.float32),
        "cotangent": bell_draw(streams_of[4], (CO, MX, MY, MZ), 1.0, 6.0, ((0, 128),), jnp.float32),
    }


epsilon = 1e-05
highest = lax.Precision.HIGHEST

def strided_window(padded, off_x, off_y, off_z, coarse_x, coarse_y, coarse_z):
    channels = padded.shape[0]
    return lax.slice(padded, (0, off_x, off_y, off_z), (channels, off_x + 2 * coarse_x - 1, off_y + 2 * coarse_y - 1, off_z + 2 * coarse_z - 1), (1, 2, 2, 2))

def forward_conv(fine, weights):
    coarse_x, coarse_y, coarse_z = (fine.shape[1] // 2, fine.shape[2] // 2, fine.shape[3] // 2)
    padded = jnp.pad(fine, ((0, 0), (1, 0), (1, 0), (1, 0)))
    summed = jnp.zeros((weights.shape[1], coarse_x, coarse_y, coarse_z), jnp.float32)
    for off_x in range(3):
        for off_y in range(3):
            for off_z in range(3):
                window = strided_window(padded, off_x, off_y, off_z, coarse_x, coarse_y, coarse_z)
                summed = summed + jnp.einsum('oc,cxyz->oxyz', weights[(off_x * 3 + off_y) * 3 + off_z], window, precision=highest)
    return summed

def reference(fine_input, weights, norm_gain, norm_shift, cotangent):
    conv = forward_conv(fine_input, weights)
    average = lax.optimization_barrier(jnp.mean(conv, axis=(1, 2, 3), keepdims=True))
    centred = conv - average
    spread = lax.optimization_barrier(jnp.mean(centred * centred, axis=(1, 2, 3), keepdims=True))
    inv_std = 1.0 / jnp.sqrt(spread + epsilon)
    normed = centred * inv_std
    gain_col = norm_gain[:, None, None, None]
    pre = gain_col * normed + norm_shift[:, None, None, None]
    sig = jax.nn.sigmoid(pre)
    activated = pre * sig
    grad_pre = cotangent * sig * (1.0 + pre * (1.0 - sig))
    rescale = 1.0 / math.sqrt(MX * MY * MZ)
    grad_gain = lax.optimization_barrier(jnp.sum(grad_pre * normed, axis=(1, 2, 3))) * rescale
    grad_shift = lax.optimization_barrier(jnp.sum(grad_pre, axis=(1, 2, 3))) * rescale
    grad_norm = gain_col * grad_pre
    grad_conv = inv_std * (grad_norm - lax.optimization_barrier(jnp.mean(grad_norm, axis=(1, 2, 3), keepdims=True)) - normed * lax.optimization_barrier(jnp.mean(grad_norm * normed, axis=(1, 2, 3), keepdims=True)))
    unused, pullback = jax.vjp(forward_conv, fine_input, weights)
    grad_input, raw_w = pullback(grad_conv)
    return (activated, grad_input, raw_w * rescale, grad_gain, grad_shift)
```

```python
import functools
import math

import jax
import jax.numpy as jnp
from jax import lax
from jax.experimental import pallas as pl
from jax.experimental.pallas import tpu as pltpu
from jax.sharding import PartitionSpec as P

MESH = pl.DeviceIdType.MESH
F32 = jnp.float32
BF16 = jnp.bfloat16
GX, GY, N_DEV = 16, 8, 128
CI, CO = 64, 128
CELLS = 32 * 64 * 128
OWN_CELLS = CELLS // N_DEV
RESCALE = 1.0 / math.sqrt(CELLS)
EPSILON = 1e-5
SLICE_OWNERS = 27 * CI // 16


def dot(a, b):
    return jnp.dot(a, b, preferred_element_type=F32)


def dot_nt(a, b):
    return lax.dot_general(a, b, (((1,), (1,)), ((), ())), preferred_element_type=F32)


def high_low(value):
    high = value.astype(BF16)
    return high, (value - high.astype(F32)).astype(BF16)


def rows_to_columns(rows):
    return jnp.concatenate([rows, jnp.zeros((120, 128), F32)], axis=0).T


def kernel(
    fine, wts, gain, shift, cot, act_out, gin_out, gw_out, gg_out, gs_out,
    fine_v, w_v, cot_v, x_hi, x_lo, even_t, odd_t, wf_e, wf_o, wb, conv, conv_t, rim_x, rim_y, rim_c,
    g_f, g_w, g_i, o_acc, out_v, act_v, stat, stat_x, stat_y, wg, wg_in, wg_all,
    local_sem, out_sem, cot_send, cot_recv, rim_send, rim_recv, stat_send, stat_recv,
    act_send, act_recv, g_send, g_recv, wr_send, wr_recv, wa_send, wa_recv,
):
    gx, gy = lax.axis_index("gx"), lax.axis_index("gy")
    me = gx * GY + gy

    def at(lin):
        return (lin // GY, lax.rem(lin, GY))

    def remote(src, dst, send, recv, device):
        return pltpu.make_async_remote_copy(
            src_ref=src, dst_ref=dst, send_sem=send, recv_sem=recv,
            device_id=device, device_id_type=MESH,
        )

    fine_in = [
        pltpu.make_async_copy(fine.at[:, x], fine_v.at[x], local_sem.at[x]) for x in (3, 2, 1, 0)
    ]
    for copy in fine_in:
        copy.start()
    w_in = pltpu.make_async_copy(wts, w_v, local_sem.at[4])
    w_in.start()
    my_cells = (pl.ds(2 * gx, 2), pl.ds(pl.multiple_of(8 * gy, 8), 8), slice(None))
    cot_own = pltpu.make_async_copy(cot.at[(0,) + my_cells], cot_v.at[me], local_sem.at[5])
    cot_own.start()

    barrier = pltpu.get_barrier_semaphore()

    def greet(k, carry):
        pl.semaphore_signal(
            barrier, inc=1, device_id=at(lax.rem(me + k, N_DEV)), device_id_type=MESH
        )
        return carry

    lax.fori_loop(1, N_DEV, greet, 0)

    row = lax.broadcasted_iota(jnp.int32, (256, 256), 0)
    col = lax.broadcasted_iota(jnp.int32, (256, 256), 1)
    split = jnp.where(
        row == jnp.where(col < 128, 2 * col, 2 * (col - 128) + 1), 1.0, 0.0
    ).astype(BF16)
    merge = jnp.where(
        col == jnp.where(row < 128, 2 * row, 2 * (row - 128) + 1), 1.0, 0.0
    ).astype(BF16)
    lane = lax.broadcasted_iota(jnp.int32, (64, 128), 1)

    w_in.wait()
    for b in range(3):
        flat = jnp.concatenate([w_v[(a * 3 + b) * 3 + c] for a in range(3) for c in range(3)], axis=1)
        high, low = high_low(flat)
        if b == 1:
            wf_e[0:128], wf_e[128:256] = high, low
        else:
            at_row = 0 if b == 2 else 128
            wf_o[at_row : at_row + 128] = high
            wf_o[256 + at_row : 384 + at_row] = low

    pl.semaphore_wait(barrier, N_DEV - 1)

    def send_cot(k, carry):
        to = lax.rem(me + k, N_DEV)
        tx, ty = at(to)
        src = cot.at[0, pl.ds(2 * tx, 2), pl.ds(pl.multiple_of(8 * ty, 8), 8), :]
        remote(src, cot_v.at[me], cot_send, cot_recv, (tx, ty)).start()
        return carry

    lax.fori_loop(1, N_DEV, send_cot, 0)

    def split_slab(x):
        high, low = high_low(fine_v[x].reshape(CI * 16, 256))
        for part, dst in ((high, x_hi), (low, x_lo)):
            both = dot(part, split)
            even_t[...] = both[:, :128]
            odd_t[...] = both[:, 128:]

            def one_row(y, carry, dst=dst):
                half, cell = lax.rem(y, 2), y // 2
                even = even_t[pl.ds(y, CI, stride=16), :]
                odd = odd_t[pl.ds(y, CI, stride=16), :]
                before = jnp.where(lane == 0, 0.0, pltpu.roll(odd, 1, 1))
                lanes = pl.ds(pl.multiple_of(cell * 128, 128), 128)
                dst[half, x * 192 : x * 192 + 64, lanes] = before.astype(BF16)
                dst[half, x * 192 + 64 : x * 192 + 128, lanes] = even.astype(BF16)
                dst[half, x * 192 + 128 : x * 192 + 192, lanes] = odd.astype(BF16)
                return carry

            lax.fori_loop(0, 16, one_row, 0)

    def forward(mx):
        x0, x1 = ((0, 2), (1, 4), (3, 4))[mx]
        a0 = (1, 0, 0)[mx]
        rows = slice(x0 * 192, x1 * 192)
        depth = (x1 - x0) * 192
        cols = slice(a0 * 192, a0 * 192 + depth)
        conv[mx, :, 0:128] = jnp.zeros((CO, 128), F32)

        def chunk(n, carry):
            here = pl.ds(pl.multiple_of(n * 256, 256), 256)
            e_hi, e_lo = x_hi[0, rows, here], x_lo[0, rows, here]
            o_hi, o_lo = x_hi[1, rows, here], x_lo[1, rows, here]
            e = dot(wf_e[:, cols], e_hi)
            e = e[:128] + e[128:] + dot(wf_e[0:128, cols], e_lo)
            o = dot(wf_o[:, cols], o_hi)
            o = o[:256] + o[256:] + dot(wf_o[0:256, cols], o_lo)
            e = e + o[:128]
            first = pl.ds(pl.multiple_of(n * 256, 256), 128)
            second = pl.ds(pl.multiple_of(n * 256 + 128, 128), 128)
            conv[mx, :, first] += e[:, :128]
            conv[mx, :, second] = e[:, 128:] + o[128:, :128]
            conv[mx, :, pl.ds(pl.multiple_of(n * 256 + 256, 256), 128)] = o[128:, 128:]
            return carry

        lax.fori_loop(0, 4, chunk, 0)

    right = (lax.rem(gx + 1, GX), gy)
    up = (gx, lax.rem(gy + 1, GY))
    right_up = (lax.rem(gx + 1, GX), lax.rem(gy + 1, GY))
    left = (lax.rem(gx + GX - 1, GX), gy)
    down = (gx, lax.rem(gy + GY - 1, GY))
    left_down = (lax.rem(gx + GX - 1, GX), lax.rem(gy + GY - 1, GY))

    fine_in[0].wait()
    split_slab(3)
    forward(2)
    rims = [
        remote(conv.at[2, :, pl.ds(0, 1024)], rim_x, rim_send.at[0], rim_recv.at[0], right),
        remote(conv.at[2, :, pl.ds(1024, 128)], rim_c, rim_send.at[1], rim_recv.at[1], right_up),
    ]
    rims[0].start()
    rims[1].start()
    for i, x in ((1, 2), (2, 1), (3, 0)):
        fine_in[i].wait()
        split_slab(x)
    forward(1)
    forward(0)
    rims.append(
        remote(conv.at[pl.ds(0, 2), :, pl.ds(1024, 128)], rim_y, rim_send.at[2], rim_recv.at[2], up)
    )
    rims[2].start()

    for tap in range(9):
        turned = [w_v[tap * 3 + c].T for c in range(3)]
        for half, (now, later) in enumerate(((turned[1], None), (turned[2], turned[0]))):
            rows = slice(tap * 128 + half * 64, tap * 128 + half * 64 + 64)
            for k, block in enumerate((now, later)):
                if block is None:
                    high = low = jnp.zeros((64, 128), BF16)
                else:
                    high, low = high_low(block)
                wb[rows, k * 128 : k * 128 + 128] = high
                wb[rows, 256 + k * 128 : 384 + k * 128] = high
                wb[rows, 512 + k * 128 : 640 + k * 128] = low

    for copy in rims:
        copy.wait()
    has_left = jnp.where(gx > 0, 1.0, 0.0)
    has_down = jnp.where(gy > 0, 1.0, 0.0)
    conv[0, :, 0:1024] += rim_x[...] * has_left
    conv[0, :, 0:128] += rim_c[...] * (has_left * has_down)
    for mx in range(2):
        conv[mx, :, 0:128] += rim_y[mx] * has_down

    own = [conv[mx, :, 128 * my : 128 * my + 128] for mx in range(2) for my in range(8)]
    average = jnp.sum(functools.reduce(jnp.add, own), axis=1, keepdims=True) * (1.0 / OWN_CELLS)
    spread = jnp.sum(
        functools.reduce(jnp.add, [(v - average) * (v - average) for v in own]), axis=1, keepdims=True
    )
    wide = lax.broadcasted_iota(jnp.int32, (128, 128), 1)
    stat[0] = jnp.where(wide == 0, average, jnp.where(wide == 1, spread, 0.0)).T[0:8]
    one_row = lax.broadcasted_iota(jnp.int32, (1, 128), 1)
    mine = one_row == me
    stat[0, 2:3] = jnp.where(mine, gain[0], 0.0)
    stat[0, 3:4] = jnp.where(mine, shift[0], 0.0)

    def exchange(k, combine):
        def to_x(d, carry):
            t = lax.rem(gx + d, GX)
            remote(stat.at[2 * k], stat_x.at[k, gx], stat_send.at[2 * k], stat_recv.at[2 * k], (t, gy)).start()
            return carry

        lax.fori_loop(1, GX, to_x, 0)
        stat_x[k, pl.ds(gx, 1)] = stat[pl.ds(2 * k, 1)]
        everyone = stat_x.at[k, pl.ds(0, GX - 1)]
        remote(everyone, everyone, stat_send.at[2 * k], stat_recv.at[2 * k], right).wait()
        stat[2 * k + 1] = combine(stat_x[k], GX, OWN_CELLS)

        def to_y(d, carry):
            t = lax.rem(gy + d, GY)
            remote(stat.at[2 * k + 1], stat_y.at[k, gy], stat_send.at[2 * k + 1], stat_recv.at[2 * k + 1], (gx, t)).start()
            return carry

        lax.fori_loop(1, GY, to_y, 0)
        stat_y[k, pl.ds(gy, 1)] = stat[pl.ds(2 * k + 1, 1)]
        everyone = stat_y.at[k, pl.ds(0, GY - 1)]
        remote(everyone, everyone, stat_send.at[2 * k + 1], stat_recv.at[2 * k + 1], up).wait()
        return combine(stat_y[k], GY, OWN_CELLS * GX)

    def combine_moments(parts, count, cells):
        total = jnp.sum(parts, axis=0)
        mean = total[0:1] * (1.0 / count)
        away = functools.reduce(
            jnp.add, [(parts[i, 0:1] - mean) * (parts[i, 0:1] - mean) for i in range(count)]
        )
        return jnp.concatenate([mean, total[1:2] + cells * away, total[2:4], jnp.zeros((4, 128), F32)], axis=0)

    def combine_sums(parts, count, cells):
        return jnp.sum(parts, axis=0)

    moments = exchange(0, combine_moments)
    inv_row = 1.0 / jnp.sqrt(moments[1:2] * (1.0 / CELLS) + EPSILON)
    rows = jnp.concatenate([moments[0:1], inv_row, moments[2:4], jnp.zeros((4, 128), F32)], axis=0)
    columns = rows_to_columns(rows)
    average, inv_std = columns[:, 0:1], columns[:, 1:2]
    gain_col, shift_col = columns[:, 2:3], columns[:, 3:4]

    cot_own.wait()
    everyone = cot_v.at[pl.ds(0, N_DEV - 1)]
    remote(everyone, everyone, cot_send, cot_recv, right).wait()
    cot_rows = cot_v.reshape(CO * 16, 128)
    conv_rows = conv_t.reshape(CO * 16, 128)

    sums = jnp.zeros((128, 128), F32), jnp.zeros((128, 128), F32)
    for mx in range(2):

        def one_cell(my, carry, mx=mx):
            s0, s1 = carry
            lanes = pl.ds(pl.multiple_of(my * 128, 128), 128)
            value = conv[mx, :, lanes]
            normed = (value - average) * inv_std
            pre = gain_col * normed + shift_col
            sig = 1.0 / (1.0 + jnp.exp(-pre))
            conv_rows[pl.ds(mx * 8 + my, 128, stride=16), :] = pre * sig
            grad = cot_rows[pl.ds(mx * 8 + my, 128, stride=16), :] * sig * (1.0 + pre * (1.0 - sig))
            g_f[mx, :, lanes] = grad
            return s0 + grad, s1 + grad * normed

        sums = lax.fori_loop(0, 8, one_cell, sums)
    stat[2] = jnp.concatenate(
        [jnp.sum(s.T, axis=0, keepdims=True) for s in sums] + [jnp.zeros((6, 128), F32)], axis=0
    )
    totals = exchange(1, combine_sums)
    gs_out[...] = jnp.sum(jnp.where(mine, totals[0:1], 0.0), axis=1, keepdims=True) * RESCALE
    gg_out[...] = jnp.sum(jnp.where(mine, totals[1:2], 0.0), axis=1, keepdims=True) * RESCALE
    columns2 = rows_to_columns(totals)
    mean_g = gain_col * columns2[:, 0:1] * (1.0 / CELLS)
    mean_gn = gain_col * columns2[:, 1:2] * (1.0 / CELLS)

    def place(mx, lanes, value):
        high, low = high_low(value)
        g_w[mx, 0:128, lanes] = high
        g_w[mx, 128:256, lanes] = low
        g_i[mx, 0:128, lanes] = high
        g_i[mx, 256:384, lanes] = low
        g_i[mx, 512:640, lanes] = high
        moved = jnp.where(wide == 127, 0.0, pltpu.roll(value, 127, 1))
        high, low = high_low(moved)
        g_i[mx, 128:256, lanes] = high
        g_i[mx, 384:512, lanes] = low
        g_i[mx, 640:768, lanes] = high

    for mx in range(2):

        def finish(my, carry, mx=mx):
            lanes = pl.ds(pl.multiple_of(my * 128, 128), 128)
            normed = (conv[mx, :, lanes] - average) * inv_std
            value = inv_std * (gain_col * g_f[mx, :, lanes] - mean_g - normed * mean_gn)
            g_f[mx, :, lanes] = value
            place(mx, lanes, value)
            return carry

        lax.fori_loop(0, 8, finish, 0)

    g_rims = [
        remote(g_f.at[0, :, pl.ds(0, 1024)], g_f.at[2, :, pl.ds(0, 1024)], g_send.at[0], g_recv.at[0], left),
        remote(g_f.at[pl.ds(0, 2), :, pl.ds(0, 128)], g_f.at[pl.ds(0, 2), :, pl.ds(1024, 128)], g_send.at[1], g_recv.at[1], down),
        remote(g_f.at[0, :, pl.ds(0, 128)], g_f.at[2, :, pl.ds(1024, 128)], g_send.at[2], g_recv.at[2], left_down),
    ]
    for copy in g_rims:
        copy.start()

    def send_act(k, carry):
        to = lax.rem(me + k, N_DEV)
        remote(conv_t.at[to], act_v.at[my_cells], act_send, act_recv, at(to)).start()
        return carry

    lax.fori_loop(1, N_DEV, send_act, 0)
    act_own = pltpu.make_async_copy(conv_t.at[me], act_v.at[my_cells], local_sem.at[6])
    act_own.start()

    for copy in g_rims:
        copy.wait()
    has_right = jnp.where(gx < GX - 1, 1.0, 0.0)
    has_up = jnp.where(gy < GY - 1, 1.0, 0.0)

    def finish_x(my, carry):
        lanes = pl.ds(pl.multiple_of(my * 128, 128), 128)
        place(2, lanes, g_f[2, :, lanes] * has_right)
        return carry

    lax.fori_loop(0, 8, finish_x, 0)
    for mx, there in ((0, has_up), (1, has_up), (2, has_up * has_right)):
        place(mx, slice(1024, 1152), g_f[mx, :, 1024:1152] * there)

    for a in range(3):
        for b in range(3):
            half = 0 if b == 1 else 1
            first_lane = 128 if b == 0 else 0
            total = jnp.zeros((192, 128), F32)
            for x, mx in ((1, 1), (3, 2)) if a == 0 else ((a - 1, 0), (a + 1, 1)):
                rows = slice(x * 192, x * 192 + 192)
                g_here = g_w[mx, :, first_lane : first_lane + 1024]
                both = dot_nt(x_hi[half, rows, :], g_here)
                total += both[:, :128] + both[:, 128:] + dot_nt(x_lo[half, rows, :], g_here[:128])
            tap = (a * 3 + b) * 3
            wg[tap * 64 : tap * 64 + 192] = total

    def send_part(k, carry):
        to = lax.rem(me + k, N_DEV)

        @pl.when(to < SLICE_OWNERS)
        def _():
            src = wg.at[pl.ds(pl.multiple_of(to * 16, 16), 16)]
            remote(src, wg_in.at[me], wr_send, wr_recv, at(to)).start()

        return carry

    lax.fori_loop(1, N_DEV, send_part, 0)

    def add_to(x, half, lanes, value, fresh):
        if fresh:
            o_acc[x, half, :, lanes] = value
        else:
            o_acc[x, half, :, lanes] += value

    for mx in range(3):
        taps = [a for a in range(3) if 0 <= 2 * mx - 1 + a <= 3]
        top, bottom = taps[0] * 384, taps[-1] * 384 + 384

        for a in taps:
            rows = slice(a * 384, a * 384 + 128)
            value = dot(wb[rows, :], g_i[mx, :, 1024:1152])
            add_to(2 * mx - 1 + a, 1, slice(896, 1024), value, a > 0)

        def chunk(n, carry, mx=mx, taps=taps, top=top, bottom=bottom):
            n = 3 - n
            here = pl.ds(pl.multiple_of(n * 256, 256), 256)
            terms = dot(wb[top:bottom, :], g_i[mx, :, here])
            first = pl.ds(pl.multiple_of(n * 256, 256), 128)
            for a in taps:
                x = 2 * mx - 1 + a
                block = terms[a * 384 - top : a * 384 - top + 384]
                add_to(x, 0, here, block[128:256], a > 0)
                value = block[256:384]
                lanes2 = pl.ds(pl.multiple_of(n * 256 + 128, 128), 128)
                o_acc[x, 1, :, lanes2] += value[:, 128:]
                add_to(x, 1, first, value[:, :128] + block[0:128, 128:], a > 0)

                @pl.when(n > 0)
                def _(x=x, block=block, a=a):
                    add_to(x, 1, pl.ds(pl.multiple_of(n * 256 - 128, 128), 128), block[0:128, :128], a > 0)

            return carry

        lax.fori_loop(0, 4, chunk, 0)

    copies = []
    for x in range(4):
        slot = x % 2
        if x >= 2:
            for copy in copies[2 * (x - 2) : 2 * (x - 2) + 2]:
                copy.wait()
        for half in range(2):
            blocks = [
                jnp.concatenate(
                    [o_acc[x, half, 0:64, 128 * my : 128 * my + 128], o_acc[x, half, 64:128, 128 * my : 128 * my + 128]],
                    axis=1,
                )
                for my in range(8)
            ]
            high, low = high_low(jnp.concatenate(blocks, axis=0))
            merged = dot(high, merge) + dot(low, merge)
            for my in range(8):
                for z in range(2):
                    out_v[slot, z, pl.ds(2 * my + half, 64, stride=16), :] = merged[
                        64 * my : 64 * my + 64, 128 * z : 128 * z + 128
                    ]
        for z in range(2):
            copy = pltpu.make_async_copy(
                out_v.at[slot, z].reshape(CI, 16, 128),
                gin_out.at[:, x, :, pl.ds(128 * z, 128)],
                out_sem.at[slot, z],
            )
            copy.start()
            copies.append(copy)

    @pl.when(me < SLICE_OWNERS)
    def _():
        wg_in[pl.ds(me, 1)] = wg[pl.ds(pl.multiple_of(me * 16, 16), 16)][None]
        everyone = wg_in.at[pl.ds(0, N_DEV - 1)]
        remote(everyone, everyone, wr_send, wr_recv, right).wait_recv()
        wg_all[pl.ds(pl.multiple_of(me * 16, 16), 16)] = jnp.sum(wg_in[...], axis=0) * RESCALE

        def send_slice(k, carry):
            to = lax.rem(me + k, N_DEV)
            src = wg_all.at[pl.ds(pl.multiple_of(me * 16, 16), 16)]
            remote(src, src, wa_send, wa_recv, at(to)).start()
            return carry

        lax.fori_loop(1, N_DEV, send_slice, 0)
        some = wg.at[pl.ds(0, 16 * (SLICE_OWNERS - 1))]
        remote(some, some, wr_send, wr_recv, right).wait_send()
        everyone = wg_in.at[pl.ds(0, N_DEV - 1)]
        remote(everyone, everyone, wa_send, wa_recv, right).wait_send()
        some = wg_all.at[pl.ds(0, 16 * (SLICE_OWNERS - 1))]
        remote(some, some, wa_send, wa_recv, right).wait_recv()

    @pl.when(me >= SLICE_OWNERS)
    def _():
        remote(wg, wg, wr_send, wr_recv, right).wait_send()
        remote(wg_all, wg_all, wa_send, wa_recv, right).wait_recv()

    for tap in range(27):
        gw_out[tap] = wg_all[tap * 64 : tap * 64 + 64].T

    act_own.wait()
    everyone = conv_t.at[pl.ds(0, N_DEV - 1)]
    remote(everyone, everyone, act_send, act_recv, right).wait()
    act_copy = pltpu.make_async_copy(act_v, act_out.at[0], local_sem.at[7])
    act_copy.start()
    act_copy.wait()
    for copy in copies[4:]:
        copy.wait()


def local(fine_input, weights, norm_gain, norm_shift, cotangent):
    any_space = pl.BlockSpec(memory_space=pl.ANY)
    vmem = pl.BlockSpec(memory_space=pltpu.VMEM)
    smem = pl.BlockSpec(memory_space=pltpu.SMEM)
    dma = pltpu.SemaphoreType.DMA
    activated, grad_input, grad_weights, grad_gain, grad_shift = pl.pallas_call(
        kernel,
        out_shape=(
            jax.ShapeDtypeStruct((1, 32, 64, 128), F32),
            jax.ShapeDtypeStruct((CI, 4, 16, 256), F32),
            jax.ShapeDtypeStruct((27, CO, CI), F32),
            jax.ShapeDtypeStruct((1, 1), F32),
            jax.ShapeDtypeStruct((1, 1), F32),
        ),
        in_specs=[any_space, any_space, smem, smem, any_space],
        out_specs=(any_space, any_space, vmem, vmem, vmem),
        scratch_shapes=[
            pltpu.VMEM((4, CI, 16, 256), F32),
            pltpu.VMEM((27, CO, CI), F32),
            pltpu.VMEM((CO, 2, 8, 128), F32),
            pltpu.VMEM((2, 768, 1024), BF16),
            pltpu.VMEM((2, 768, 1024), BF16),
            pltpu.VMEM((1024, 128), F32),
            pltpu.VMEM((1024, 128), F32),
            pltpu.VMEM((256, 576), BF16),
            pltpu.VMEM((512, 576), BF16),
            pltpu.VMEM((1152, 768), BF16),
            pltpu.VMEM((3, CO, 1152), F32),
            pltpu.VMEM((CO, 2, 8, 128), F32),
            pltpu.VMEM((CO, 1024), F32),
            pltpu.VMEM((2, CO, 128), F32),
            pltpu.VMEM((CO, 128), F32),
            pltpu.VMEM((3, CO, 1152), F32),
            pltpu.VMEM((3, 256, 1152), BF16),
            pltpu.VMEM((3, 768, 1152), BF16),
            pltpu.VMEM((4, 2, 128, 1024), F32),
            pltpu.VMEM((2, 2, 1024, 128), F32),
            pltpu.VMEM((32, 64, 128), F32),
            pltpu.VMEM((4, 8, 128), F32),
            pltpu.VMEM((2, GX, 8, 128), F32),
            pltpu.VMEM((2, GY, 8, 128), F32),
            pltpu.VMEM((27 * CI, 128), F32),
            pltpu.VMEM((N_DEV, 16, 128), F32),
            pltpu.VMEM((27 * CI, 128), F32),
            dma((8,)),
            dma((2, 2)),
            dma,
            dma,
            dma((3,)),
            dma((3,)),
            dma((4,)),
            dma((4,)),
            dma,
            dma,
            dma((3,)),
            dma((3,)),
            dma,
            dma,
            dma,
            dma,
        ],
        compiler_params=pltpu.CompilerParams(
            collective_id=0, has_side_effects=True, vmem_limit_bytes=60 << 20
        ),
    )(fine_input, weights, norm_gain, norm_shift, cotangent)
    return activated, grad_input, grad_weights, grad_gain.reshape(1), grad_shift.reshape(1)


def solution(mesh):
    placed = (
        P(None, "gx", "gy", None),
        P(),
        P(("gx", "gy")),
        P(("gx", "gy")),
        P(("gx", "gy"), None, None, None),
    )
    return jax.shard_map(
        local,
        mesh=mesh,
        in_specs=placed,
        out_specs=(
            P(("gx", "gy"), None, None, None),
            P(None, "gx", "gy", None),
            P(),
            P(("gx", "gy")),
            P(("gx", "gy")),
        ),
        check_vma=False,
    )
```

```python
import functools
import math

import jax
import jax.numpy as jnp
from jax import lax
from jax.experimental import pallas as pl
from jax.experimental.pallas import tpu as pltpu
from jax.sharding import PartitionSpec as P

MESH = pl.DeviceIdType.MESH
F32 = jnp.float32
BF16 = jnp.bfloat16
GX, GY, N_DEV = 16, 8, 128
CI, CO = 64, 128
CELLS = 32 * 64 * 128
OWN_CELLS = CELLS // N_DEV
RESCALE = 1.0 / math.sqrt(CELLS)
EPSILON = 1e-5
N_CHIP = N_DEV // 2
HALF = 27 * CI // 2
OWNERS = HALF // 16
ACT_CUTS = ((1, 32), (32, 64), (64, 96), (96, 128))


def dot(a, b):
    return jnp.dot(a, b, preferred_element_type=F32)


def dot_nt(a, b):
    return lax.dot_general(a, b, (((1,), (1,)), ((), ())), preferred_element_type=F32)


def high_low(value):
    high = value.astype(BF16)
    return high, (value - high.astype(F32)).astype(BF16)


def rows_to_columns(rows):
    return jnp.concatenate([rows, jnp.zeros((120, 128), F32)], axis=0).T


def kernel(
    fine, wts, gain, shift, cot, act_out, gin_out, gw_out, gg_out, gs_out,
    fine_v, w_v, cot_v, x_hi, x_lo, even_t, odd_t, wf_e, wf_o, wb, conv, conv_t, rim_out, rim_x, rim_y, rim_c,
    g_f, g_w, g_i, o_acc, out_v, act_v, stat, stat_x, stat_y, wg, wg_pair, wg_half, wg_in, wg_all,
    local_sem, out_sem, cot_send, cot_recv, rim_send, rim_recv, stat_send, stat_recv,
    act_send, act_recv, g_send, g_recv, wr_send, wr_recv, wa_send, wa_recv, pair_send, pair_recv,
):
    gx, gy = lax.axis_index("gx"), lax.axis_index("gy")
    me = gx * GY + gy

    def at(lin):
        return (lin // GY, lax.rem(lin, GY))

    def remote(src, dst, send, recv, device):
        return pltpu.make_async_remote_copy(
            src_ref=src, dst_ref=dst, send_sem=send, recv_sem=recv,
            device_id=device, device_id_type=MESH,
        )

    fine_in = [
        pltpu.make_async_copy(fine.at[:, x], fine_v.at[x], local_sem.at[x]) for x in (3, 2, 1, 0)
    ]
    for copy in fine_in:
        copy.start()
    w_in = pltpu.make_async_copy(wts, w_v, local_sem.at[4])
    w_in.start()
    my_cells = (pl.ds(2 * gx, 2), pl.ds(pl.multiple_of(8 * gy, 8), 8), slice(None))
    cot_own = pltpu.make_async_copy(cot.at[(0,) + my_cells], cot_v.at[me], local_sem.at[5])
    cot_own.start()

    barrier = pltpu.get_barrier_semaphore()

    def greet(k, carry):
        pl.semaphore_signal(
            barrier, inc=1, device_id=at(lax.rem(me + k, N_DEV)), device_id_type=MESH
        )
        return carry

    lax.fori_loop(1, N_DEV, greet, 0)

    row = lax.broadcasted_iota(jnp.int32, (256, 256), 0)
    col = lax.broadcasted_iota(jnp.int32, (256, 256), 1)
    split = jnp.where(
        row == jnp.where(col < 128, 2 * col, 2 * (col - 128) + 1), 1.0, 0.0
    ).astype(BF16)
    merge = jnp.where(
        col == jnp.where(row < 128, 2 * row, 2 * (row - 128) + 1), 1.0, 0.0
    ).astype(BF16)
    lane = lax.broadcasted_iota(jnp.int32, (64, 128), 1)

    w_in.wait()
    for b in range(3):
        flat = jnp.concatenate([w_v[(a * 3 + b) * 3 + c] for a in range(3) for c in range(3)], axis=0)
        high, low = high_low(flat.T)
        if b == 1:
            wf_e[0:128], wf_e[128:256] = high, low
        else:
            at_row = 0 if b == 2 else 128
            wf_o[at_row : at_row + 128] = high
            wf_o[256 + at_row : 384 + at_row] = low

    def send_cot(k, carry):
        to = lax.rem(me + k, N_DEV)
        tx, ty = at(to)
        src = cot.at[0, pl.ds(2 * tx, 2), pl.ds(pl.multiple_of(8 * ty, 8), 8), :]
        remote(src, cot_v.at[me], cot_send, cot_recv, (tx, ty)).start()
        return carry

    right = (lax.rem(gx + 1, GX), gy)
    up = (gx, lax.rem(gy + 1, GY))
    right_up = (lax.rem(gx + 1, GX), lax.rem(gy + 1, GY))
    left = (lax.rem(gx + GX - 1, GX), gy)
    down = (gx, lax.rem(gy + GY - 1, GY))
    left_down = (lax.rem(gx + GX - 1, GX), lax.rem(gy + GY - 1, GY))

    def exchange_start(k, stage):
        index, parts = 2 * k + stage, (stat_x, stat_y)[stage]
        place, count = ((gx, GX), (gy, GY))[stage]

        def send(d, carry):
            to = lax.rem(place + d, count)
            device = ((to, gy), (gx, to))[stage]
            remote(stat.at[index], parts.at[k, place], stat_send.at[index], stat_recv.at[index], device).start()
            return carry

        lax.fori_loop(1, count, send, 0)
        parts[k, pl.ds(place, 1)] = stat[pl.ds(index, 1)]

    def exchange_wait(k, stage):
        index, parts = 2 * k + stage, (stat_x, stat_y)[stage]
        everyone = parts.at[k, pl.ds(0, (GX, GY)[stage] - 1)]
        remote(everyone, everyone, stat_send.at[index], stat_recv.at[index], (right, up)[stage]).wait()

    def split_slab(x):
        high, low = high_low(fine_v[x].reshape(CI * 16, 256))
        for part, dst in ((high, x_hi), (low, x_lo)):
            both = dot(part, split)
            even_t[...] = both[:, :128]
            odd_t[...] = both[:, 128:]

            for y in range(16):
                half, lanes = y % 2, slice(y // 2 * 128, y // 2 * 128 + 128)
                even = even_t[pl.ds(y, CI, stride=16), :]
                odd = odd_t[pl.ds(y, CI, stride=16), :]
                before = jnp.where(lane == 0, 0.0, pltpu.roll(odd, 1, 1))
                dst[half, x * 192 : x * 192 + 64, lanes] = before.astype(BF16)
                dst[half, x * 192 + 64 : x * 192 + 128, lanes] = even.astype(BF16)
                dst[half, x * 192 + 128 : x * 192 + 192, lanes] = odd.astype(BF16)

    def operands(mx):
        x0, x1 = ((0, 2), (1, 4), (3, 4))[mx]
        a0 = (1, 0, 0)[mx]
        depth = (x1 - x0) * 192
        return slice(x0 * 192, x1 * 192), slice(a0 * 192, a0 * 192 + depth)

    def forward_rim(mx):
        rows, cols = operands(mx)
        value = dot(wf_o[:, cols], x_hi[1, rows, 896:1024])
        return value[128:256] + value[384:512] + dot(wf_o[128:256, cols], x_lo[1, rows, 896:1024])

    def forward(mx):
        rows, cols = operands(mx)
        conv[mx, :, 0:128] = jnp.zeros((CO, 128), F32)

        def chunk(n, carry):
            here = pl.ds(pl.multiple_of(n * 256, 256), 256)
            e_hi, e_lo = x_hi[0, rows, here], x_lo[0, rows, here]
            o_hi, o_lo = x_hi[1, rows, here], x_lo[1, rows, here]
            e = dot(wf_e[:, cols], e_hi)
            e = e[:128] + e[128:] + dot(wf_e[0:128, cols], e_lo)
            o = dot(wf_o[:, cols], o_hi)
            o = o[:256] + o[256:] + dot(wf_o[0:256, cols], o_lo)
            e = e + o[:128]
            conv[mx, :, pl.ds(pl.multiple_of(n * 256, 256), 128)] += e[:, :128]
            conv[mx, :, pl.ds(pl.multiple_of(n * 256 + 128, 128), 128)] = e[:, 128:] + o[128:, :128]
            conv[mx, :, pl.ds(pl.multiple_of(n * 256 + 256, 256), 128)] = o[128:, 128:]
            return carry

        lax.fori_loop(0, 4, chunk, 0)

    fine_in[0].wait()
    split_slab(3)
    forward(2)
    pl.semaphore_wait(barrier, N_DEV - 1)
    rims = [
        remote(conv.at[2, :, pl.ds(0, 1024)], rim_x, rim_send.at[0], rim_recv.at[0], right),
        remote(conv.at[2, :, pl.ds(1024, 128)], rim_c, rim_send.at[1], rim_recv.at[1], right_up),
    ]
    rims[0].start()
    rims[1].start()
    one_row = lax.broadcasted_iota(jnp.int32, (1, 128), 1)
    mine = one_row == me
    stat[4] = jnp.concatenate([jnp.where(mine, gain[0], 0.0), jnp.where(mine, shift[0], 0.0)], axis=0)
    exchange_start(2, 0)
    lax.fori_loop(1, N_DEV, send_cot, 0)
    for i, x in ((1, 2), (2, 1), (3, 0)):
        fine_in[i].wait()
        split_slab(x)
    for mx in range(2):
        rim_out[mx] = forward_rim(mx)
    rims.append(remote(rim_out, rim_y, rim_send.at[2], rim_recv.at[2], up))
    rims[2].start()
    forward(1)
    forward(0)

    for tap in range(9):
        turned = [w_v[tap * 3 + c] for c in range(3)]
        for half, (now, later) in enumerate(((turned[1], None), (turned[2], turned[0]))):
            rows = slice(tap * 128 + half * 64, tap * 128 + half * 64 + 64)
            for k, block in enumerate((now, later)):
                if block is None:
                    high = low = jnp.zeros((64, 128), BF16)
                else:
                    high, low = high_low(block)
                wb[rows, k * 128 : k * 128 + 128] = high
                wb[rows, 256 + k * 128 : 384 + k * 128] = high
                wb[rows, 512 + k * 128 : 640 + k * 128] = low

    exchange_wait(2, 0)
    stat[5] = jnp.sum(stat_x[2], axis=0)
    exchange_start(2, 1)
    for copy in rims:
        copy.wait()
    has_left = jnp.where(gx > 0, 1.0, 0.0)
    has_down = jnp.where(gy > 0, 1.0, 0.0)
    conv[0, :, 0:1024] += rim_x[...] * has_left
    conv[0, :, 0:128] += rim_c[...] * (has_left * has_down)
    for mx in range(2):
        conv[mx, :, 0:128] += rim_y[mx] * has_down

    conv_rows = conv_t.reshape(CO * 16, 128)
    own = [conv[mx, :, 128 * my : 128 * my + 128] for mx in range(2) for my in range(8)]
    average = jnp.sum(functools.reduce(jnp.add, own), axis=1, keepdims=True) * (1.0 / OWN_CELLS)
    spread = jnp.sum(
        functools.reduce(jnp.add, [(v - average) * (v - average) for v in own]), axis=1, keepdims=True
    )
    wide = lax.broadcasted_iota(jnp.int32, (128, 128), 1)
    stat[0] = jnp.where(wide == 0, average, jnp.where(wide == 1, spread, 0.0)).T[0:2]
    for row_of in range(16):
        conv_rows[pl.ds(row_of, 128, stride=16), :] = conv[row_of // 8, :, row_of % 8 * 128 : row_of % 8 * 128 + 128]
    act_own = pltpu.make_async_copy(conv_t.at[me], act_v.at[my_cells], local_sem.at[6])
    act_own.start()

    def send_act(k, carry):
        to = lax.rem(me + k, N_DEV)
        remote(conv_t.at[to], act_v.at[my_cells], act_send, act_recv, at(to)).start()
        return carry

    def combine_moments(parts, cells):
        count = parts.shape[0]
        total = jnp.sum(parts, axis=0)
        mean = total[0:1] * (1.0 / count)
        away = parts[:, 0:1] - mean[None]
        return jnp.concatenate([mean, total[1:2] + cells * jnp.sum(away * away, axis=0)], axis=0)

    exchange_start(0, 0)
    lax.fori_loop(*ACT_CUTS[0], send_act, 0)
    exchange_wait(0, 0)
    stat[1] = combine_moments(stat_x[0], OWN_CELLS)
    exchange_start(0, 1)
    lax.fori_loop(*ACT_CUTS[1], send_act, 0)
    exchange_wait(0, 1)
    moments = combine_moments(stat_y[0], OWN_CELLS * GX)
    exchange_wait(2, 1)
    scales = jnp.sum(stat_y[2], axis=0)
    inv_row = 1.0 / jnp.sqrt(moments[1:2] * (1.0 / CELLS) + EPSILON)
    rows = jnp.concatenate([moments[0:1], inv_row, scales, jnp.zeros((4, 128), F32)], axis=0)
    own_average, own_inv_std = (
        jnp.sum(jnp.where(mine, r, 0.0), axis=1, keepdims=True) for r in (moments[0:1], inv_row)
    )
    columns = rows_to_columns(rows)
    average, inv_std = columns[:, 0:1], columns[:, 1:2]
    gain_col, shift_col = columns[:, 2:3], columns[:, 3:4]

    cot_own.wait()
    everyone = cot_v.at[pl.ds(0, N_DEV - 1)]
    remote(everyone, everyone, cot_send, cot_recv, right).wait()
    cot_rows = cot_v.reshape(CO * 16, 128)
    sums = jnp.zeros((128, 128), F32), jnp.zeros((128, 128), F32)
    for mx in range(2):

        def one_cell(my, carry, mx=mx):
            s0, s1 = carry
            lanes = pl.ds(pl.multiple_of(my * 128, 128), 128)
            value = conv[mx, :, lanes]
            normed = (value - average) * inv_std
            pre = gain_col * normed + shift_col
            sig = 1.0 / (1.0 + jnp.exp(-pre))
            grad = cot_rows[pl.ds(mx * 8 + my, 128, stride=16), :] * sig * (1.0 + pre * (1.0 - sig))
            g_f[mx, :, lanes] = grad
            return s0 + grad, s1 + grad * normed

        sums = lax.fori_loop(0, 8, one_cell, sums, unroll=4)
    stat[2] = jnp.concatenate([jnp.sum(s.T, axis=0, keepdims=True) for s in sums], axis=0)
    exchange_start(1, 0)
    lax.fori_loop(*ACT_CUTS[2], send_act, 0)
    exchange_wait(1, 0)
    stat[3] = jnp.sum(stat_x[1], axis=0)
    exchange_start(1, 1)
    lax.fori_loop(*ACT_CUTS[3], send_act, 0)
    exchange_wait(1, 1)
    totals = jnp.sum(stat_y[1], axis=0)
    gs_out[...] = jnp.sum(jnp.where(mine, totals[0:1], 0.0), axis=1, keepdims=True) * RESCALE
    gg_out[...] = jnp.sum(jnp.where(mine, totals[1:2], 0.0), axis=1, keepdims=True) * RESCALE
    columns2 = rows_to_columns(jnp.concatenate([totals, jnp.zeros((6, 128), F32)], axis=0))
    mean_g = gain_col * columns2[:, 0:1] * (1.0 / CELLS)
    mean_gn = gain_col * columns2[:, 1:2] * (1.0 / CELLS)

    def place(mx, lanes, value):
        high, low = high_low(value)
        g_w[mx, 0:128, lanes] = high
        g_w[mx, 128:256, lanes] = low
        g_i[mx, 0:128, lanes] = high
        g_i[mx, 256:384, lanes] = low
        g_i[mx, 512:640, lanes] = high
        moved = jnp.where(wide == 127, 0.0, pltpu.roll(value, 127, 1))
        high, low = high_low(moved)
        g_i[mx, 128:256, lanes] = high
        g_i[mx, 384:512, lanes] = low
        g_i[mx, 640:768, lanes] = high

    def finish_row(mx):
        def finish(my, carry):
            lanes = pl.ds(pl.multiple_of(my * 128, 128), 128)
            normed = (conv[mx, :, lanes] - average) * inv_std
            value = inv_std * (gain_col * g_f[mx, :, lanes] - mean_g - normed * mean_gn)
            g_f[mx, :, lanes] = value
            place(mx, lanes, value)
            return carry

        lax.fori_loop(0, 8, finish, 0, unroll=4)

    finish_row(0)
    g_rims = [
        remote(g_f.at[0, :, pl.ds(0, 1024)], g_f.at[2, :, pl.ds(0, 1024)], g_send.at[0], g_recv.at[0], left),
        remote(g_f.at[pl.ds(0, 2), :, pl.ds(0, 128)], g_f.at[pl.ds(0, 2), :, pl.ds(1024, 128)], g_send.at[1], g_recv.at[1], down),
        remote(g_f.at[0, :, pl.ds(0, 128)], g_f.at[2, :, pl.ds(1024, 128)], g_send.at[2], g_recv.at[2], left_down),
    ]
    g_rims[0].start()
    g_rims[2].start()
    finish_row(1)
    g_rims[1].start()

    def weight_terms(mx, b, x_lanes, g_lanes, fresh=False):
        half = 0 if b == 1 else 1
        rows, cols = operands(mx)
        g_here = g_w[mx, :, g_lanes]
        both = dot_nt(x_hi[half, rows, x_lanes], g_here)
        value = both[:, :128] + both[:, 128:] + dot_nt(x_lo[half, rows, x_lanes], g_here[:128])
        target = slice(b * 576 + cols.start, b * 576 + cols.stop)
        if fresh:
            wg[target] = value
        else:
            wg[target] += value

    def add_to(x, half, lanes, value, fresh):
        if fresh:
            o_acc[x, half, :, lanes] = value
        else:
            o_acc[x, half, :, lanes] += value

    def input_terms(mx):
        taps = [a for a in range(3) if 0 <= 2 * mx - 1 + a <= 3]
        top, bottom = taps[0] * 384, taps[-1] * 384 + 384

        def chunk(n, carry):
            here = pl.ds(pl.multiple_of(n * 256, 256), 256)
            first = pl.ds(pl.multiple_of(n * 256, 256), 128)
            second = pl.ds(pl.multiple_of(n * 256 + 128, 128), 128)
            terms = dot(wb[top:bottom, :], g_i[mx, :, here])
            for a in taps:
                x = 2 * mx - 1 + a
                block = terms[a * 384 - top : a * 384 - top + 384]
                add_to(x, 0, here, block[128:256], a > 0)
                add_to(x, 1, first, block[256:384, :128] + block[0:128, 128:], a > 0)
                add_to(x, 1, second, block[256:384, 128:], a > 0)

                @pl.when(n > 0)
                def _(x=x, block=block):
                    before = pl.ds(pl.multiple_of(n * 256 - 128, 128), 128)
                    o_acc[x, 1, :, before] += block[0:128, :128]

            return carry

        lax.fori_loop(0, 4, chunk, 0)

    def input_terms_rim(mx):
        for a in range(3):
            x = 2 * mx - 1 + a
            if 0 <= x <= 3:
                value = dot(wb[a * 384 : a * 384 + 128, :], g_i[mx, :, 1024:1152])
                o_acc[x, 1, :, 896:1024] += value

    everything = slice(0, 1024)
    for mx in (1, 0):
        weight_terms(mx, 0, slice(0, 896), slice(128, 1024), mx == 1)
        weight_terms(mx, 1, everything, everything, mx == 1)
        weight_terms(mx, 2, everything, everything, mx == 1)
    input_terms(0)
    input_terms(1)
    for copy in g_rims:
        copy.wait()
    has_right = jnp.where(gx < GX - 1, 1.0, 0.0)
    has_up = jnp.where(gy < GY - 1, 1.0, 0.0)

    def finish_x(my, carry):
        lanes = pl.ds(pl.multiple_of(my * 128, 128), 128)
        place(2, lanes, g_f[2, :, lanes] * has_right)
        return carry

    lax.fori_loop(0, 8, finish_x, 0, unroll=4)
    for mx, there in ((0, has_up), (1, has_up), (2, has_up * has_right)):
        place(mx, slice(1024, 1152), g_f[mx, :, 1024:1152] * there)
    for mx in range(2):
        weight_terms(mx, 0, slice(896, 1024), slice(1024, 1152))
    weight_terms(2, 0, everything, slice(128, 1152))
    weight_terms(2, 1, everything, everything)
    weight_terms(2, 2, everything, everything)

    core, chip = lax.rem(gx, 2), (gx // 2) * GY + gy
    pair_device = (gx + 1 - 2 * core, gy)
    other_half = pl.ds(pl.multiple_of((1 - core) * HALF, HALF), HALF)
    own_half = pl.ds(pl.multiple_of(core * HALF, HALF), HALF)
    pair = remote(wg.at[other_half], wg_pair, pair_send.at[0], pair_recv.at[0], pair_device)
    pair.start()

    def chip_device(index):
        return (2 * (index // GY) + core, lax.rem(index, GY))

    def slice_of(index):
        return pl.ds(pl.multiple_of(index * 16, 16), 16)

    pair.wait()
    wg_half[...] = wg[own_half] + wg_pair[...]

    def send_part(k, carry):
        to = lax.rem(chip + k, N_CHIP)

        @pl.when(to < OWNERS)
        def _():
            remote(wg_half.at[slice_of(to)], wg_in.at[chip], wr_send, wr_recv, chip_device(to)).start()

        return carry

    lax.fori_loop(1, N_CHIP, send_part, 0)
    input_terms(2)
    for mx in range(3):
        input_terms_rim(mx)
    copies = []
    for x in range(4):
        slot = x % 2
        if x >= 2:
            for copy in copies[2 * (x - 2) : 2 * (x - 2) + 2]:
                copy.wait()
        for half in range(2):
            blocks = [
                jnp.concatenate(
                    [o_acc[x, half, 0:64, 128 * my : 128 * my + 128], o_acc[x, half, 64:128, 128 * my : 128 * my + 128]],
                    axis=1,
                )
                for my in range(8)
            ]
            high, low = high_low(jnp.concatenate(blocks, axis=0))
            merged = dot(high, merge) + dot(low, merge)
            for my in range(8):
                for z in range(2):
                    out_v[slot, z, pl.ds(2 * my + half, 64, stride=16), :] = merged[
                        64 * my : 64 * my + 64, 128 * z : 128 * z + 128
                    ]
        for z in range(2):
            copy = pltpu.make_async_copy(
                out_v.at[slot, z].reshape(CI, 16, 128),
                gin_out.at[:, x, :, pl.ds(128 * z, 128)],
                out_sem.at[slot, z],
            )
            copy.start()
            copies.append(copy)

    @pl.when(chip < OWNERS)
    def _():
        wg_in[pl.ds(chip, 1)] = wg_half[slice_of(chip)][None]
        everyone = wg_in.at[pl.ds(0, N_CHIP - 1)]
        remote(everyone, everyone, wr_send, wr_recv, right).wait_recv()
        own_slice = pl.ds(pl.multiple_of(core * HALF + chip * 16, 16), 16)
        wg_all[own_slice] = jnp.sum(wg_in[...], axis=0) * RESCALE

        def send_slice(k, carry):
            to = lax.rem(chip + k, N_CHIP)
            src = wg_all.at[own_slice]
            remote(src, src, wa_send, wa_recv, chip_device(to)).start()
            return carry

        lax.fori_loop(1, N_CHIP, send_slice, 0)
        some = wg_half.at[pl.ds(0, 16 * (OWNERS - 1))]
        remote(some, some, wr_send, wr_recv, right).wait_send()
        remote(everyone, everyone, wa_send, wa_recv, right).wait_send()
        some = wg_all.at[pl.ds(0, 16 * (OWNERS - 1))]
        remote(some, some, wa_send, wa_recv, right).wait_recv()

    @pl.when(chip >= OWNERS)
    def _():
        remote(wg_half, wg_half, wr_send, wr_recv, right).wait_send()
        some = wg_all.at[pl.ds(0, HALF)]
        remote(some, some, wa_send, wa_recv, right).wait_recv()

    done = wg_all.at[own_half]
    pair = remote(done, done, pair_send.at[1], pair_recv.at[1], pair_device)
    pair.start()
    act_own.wait()
    everyone = conv_t.at[pl.ds(0, N_DEV - 1)]
    remote(everyone, everyone, act_send, act_recv, right).wait()
    own_scale = own_inv_std * gain[0]

    def activate(i, carry):
        here = pl.ds(i * 4, 4)
        pre = (act_v[here] - own_average[None]) * own_scale[None] + shift[0]
        act_v[here] = pre / (1.0 + jnp.exp(-pre))
        return carry

    lax.fori_loop(0, 8, activate, 0)
    act_copy = pltpu.make_async_copy(act_v, act_out, local_sem.at[7])
    act_copy.start()
    pair.wait()
    for a in range(3):
        for b in range(3):
            rows = slice((b * 3 + a) * 192, (b * 3 + a) * 192 + 192)
            gw_out[(a * 3 + b) * 3 : (a * 3 + b) * 3 + 3] = wg_all[rows].reshape(3, CI, CO)
    act_copy.wait()
    for copy in copies[4:]:
        copy.wait()


def hand_over(*refs):
    sources, targets, buffers, sem = refs[:3], refs[3:6], refs[6:9], refs[9]
    reads, writes = [], []
    for source, target, buffer, pieces in zip(sources, targets, buffers, (2, 8, 1)):
        size = source.shape[0] // pieces
        for piece in range(pieces):
            here = pl.ds(piece * size, size)
            k = len(reads)
            reads.append(pltpu.make_async_copy(source.at[here], buffer.at[here], sem.at[0, k]))
            writes.append(pltpu.make_async_copy(buffer.at[here], target.at[here], sem.at[1, k]))
    for read in reads:
        read.start()
    for read, write in zip(reads, writes):
        read.wait()
        write.start()
    for write in writes:
        write.wait()


def local(fine_input, weights, norm_gain, norm_shift, cotangent):
    any_space = pl.BlockSpec(memory_space=pl.ANY)
    vmem = pl.BlockSpec(memory_space=pltpu.VMEM)
    smem = pl.BlockSpec(memory_space=pltpu.SMEM)
    dma = pltpu.SemaphoreType.DMA
    activated, grad_input, grad_weights, grad_gain, grad_shift = pl.pallas_call(
        kernel,
        out_shape=(
            jax.ShapeDtypeStruct((32, 64, 128), F32),
            jax.ShapeDtypeStruct((CI, 4, 16, 256), F32),
            jax.ShapeDtypeStruct((27, CI, CO), F32),
            jax.ShapeDtypeStruct((1, 1), F32),
            jax.ShapeDtypeStruct((1, 1), F32),
        ),
        in_specs=[any_space, any_space, smem, smem, any_space],
        out_specs=(any_space, any_space, vmem, vmem, vmem),
        scratch_shapes=[
            pltpu.VMEM((4, CI, 16, 256), F32),
            pltpu.VMEM((27, CI, CO), F32),
            pltpu.VMEM((CO, 2, 8, 128), F32),
            pltpu.VMEM((2, 768, 1024), BF16),
            pltpu.VMEM((2, 768, 1024), BF16),
            pltpu.VMEM((1024, 128), F32),
            pltpu.VMEM((1024, 128), F32),
            pltpu.VMEM((256, 576), BF16),
            pltpu.VMEM((512, 576), BF16),
            pltpu.VMEM((1152, 768), BF16),
            pltpu.VMEM((3, CO, 1152), F32),
            pltpu.VMEM((CO, 2, 8, 128), F32),
            pltpu.VMEM((2, CO, 128), F32),
            pltpu.VMEM((CO, 1024), F32),
            pltpu.VMEM((2, CO, 128), F32),
            pltpu.VMEM((CO, 128), F32),
            pltpu.VMEM((3, CO, 1152), F32),
            pltpu.VMEM((3, 256, 1152), BF16),
            pltpu.VMEM((3, 768, 1152), BF16),
            pltpu.VMEM((4, 2, 128, 1024), F32),
            pltpu.VMEM((2, 2, 1024, 128), F32),
            pltpu.VMEM((32, 64, 128), F32),
            pltpu.VMEM((6, 2, 128), F32),
            pltpu.VMEM((3, GX, 2, 128), F32),
            pltpu.VMEM((3, GY, 2, 128), F32),
            pltpu.VMEM((27 * CI, 128), F32),
            pltpu.VMEM((HALF, 128), F32),
            pltpu.VMEM((HALF, 128), F32),
            pltpu.VMEM((N_CHIP, 16, 128), F32),
            pltpu.VMEM((27 * CI, 128), F32),
            dma((8,)),
            dma((2, 2)),
            dma,
            dma,
            dma((3,)),
            dma((3,)),
            dma((6,)),
            dma((6,)),
            dma,
            dma,
            dma((3,)),
            dma((3,)),
            dma,
            dma,
            dma,
            dma,
            dma((2,)),
            dma((2,)),
        ],
        compiler_params=pltpu.CompilerParams(
            collective_id=0, has_side_effects=True, vmem_limit_bytes=60 << 20
        ),
    )(fine_input, weights.transpose(0, 2, 1), norm_gain, norm_shift, cotangent)
    activated, grad_input, grad_weights = pl.pallas_call(
        hand_over,
        out_shape=(
            jax.ShapeDtypeStruct((32, 64, 128), F32),
            jax.ShapeDtypeStruct((CI, 4, 16, 256), F32),
            jax.ShapeDtypeStruct((27, CI, CO), F32),
        ),
        in_specs=[any_space] * 3,
        out_specs=(any_space,) * 3,
        scratch_shapes=[
            pltpu.VMEM((32, 64, 128), F32),
            pltpu.VMEM((CI, 4, 16, 256), F32),
            pltpu.VMEM((27, CI, CO), F32),
            dma((2, 11)),
        ],
        compiler_params=pltpu.CompilerParams(vmem_limit_bytes=60 << 20),
    )(activated, grad_input, grad_weights)
    activated, grad_weights = activated[None], grad_weights.transpose(0, 2, 1)
    return activated, grad_input, grad_weights, grad_gain.reshape(1), grad_shift.reshape(1)


def solution(mesh):
    placed = (
        P(None, "gx", "gy", None),
        P(),
        P(("gx", "gy")),
        P(("gx", "gy")),
        P(("gx", "gy"), None, None, None),
    )
    return jax.shard_map(
        local,
        mesh=mesh,
        in_specs=placed,
        out_specs=(
            P(("gx", "gy"), None, None, None),
            P(None, "gx", "gy", None),
            P(),
            P(("gx", "gy")),
            P(("gx", "gy")),
        ),
        check_vma=False,
    )
```

```python
import functools
import math

import jax
import jax.numpy as jnp
from jax import lax
from jax.experimental import pallas as pl
from jax.experimental.pallas import tpu as pltpu
from jax.sharding import PartitionSpec as P

MESH = pl.DeviceIdType.MESH
F32 = jnp.float32
BF16 = jnp.bfloat16
GX, GY, N_DEV = 16, 8, 128
CI, CO = 64, 128
CELLS = 32 * 64 * 128
RESCALE = 1.0 / math.sqrt(CELLS)
EPSILON = 1e-5
N_CHIP = N_DEV // 2
HALF = 27 * CI // 2
OWNERS = HALF // 16
FIRST = (16, 8, 0)
PARTS = ((0, 8), (8, 8), (16, 11))
GROUPS = ((0, 576), (1152, 288))
CUT = 36


def dot(a, b):
    return jnp.dot(a, b, preferred_element_type=F32)


def dot_nt(a, b):
    return lax.dot_general(a, b, (((1,), (1,)), ((), ())), preferred_element_type=F32)


def high_low(value):
    high = value.astype(BF16)
    return high, (value - high.astype(F32)).astype(BF16)


def rows_to_columns(rows):
    return jnp.concatenate([rows, jnp.zeros((120, 128), F32)], axis=0).T


def kernel(
    fine, wts, gain, shift, cot, act_out, gin_out, gw_out, gg_out, gs_out,
    fine_v, w_v, cot_v, x_hi, x_lo, even_t, odd_t, wf_e, wf_o, wb,
    conv, pair_x, cells_out, cells_in, whole, grad_out, grad_in, g_w, g_i, o_acc, out_v, act_v,
    wg, wg_pair, wg_half, wg_in, wg_all,
    local_sem, out_sem, conv_send, conv_recv, grad_send, grad_recv, wr_send, wr_recv, wa_send, wa_recv,
    pair_send, pair_recv,
):
    gx, gy = lax.axis_index("gx"), lax.axis_index("gy")
    me = gx * GY + gy
    core, chip = lax.rem(gx, 2), (gx // 2) * GY + gy
    pair_device = (gx + 1 - 2 * core, gy)
    right = (lax.rem(gx + 1, GX), gy)

    def at(lin):
        return (lin // GY, lax.rem(lin, GY))

    def remote(src, dst, send, recv, device):
        return pltpu.make_async_remote_copy(
            src_ref=src, dst_ref=dst, send_sem=send, recv_sem=recv,
            device_id=device, device_id_type=MESH,
        )

    fine_in = [
        pltpu.make_async_copy(fine.at[:, x], fine_v.at[x], local_sem.at[x]) for x in (3, 2, 1, 0)
    ]
    for copy in fine_in:
        copy.start()
    w_in = pltpu.make_async_copy(wts, w_v, local_sem.at[4])
    w_in.start()
    cot_in = pltpu.make_async_copy(cot.at[0], cot_v, local_sem.at[5])
    cot_in.start()

    barrier = pltpu.get_barrier_semaphore()

    def greet(k, carry):
        pl.semaphore_signal(
            barrier, inc=1, device_id=at(lax.rem(me + k, N_DEV)), device_id_type=MESH
        )
        return carry

    lax.fori_loop(1, N_DEV, greet, 0)

    row = lax.broadcasted_iota(jnp.int32, (256, 256), 0)
    col = lax.broadcasted_iota(jnp.int32, (256, 256), 1)
    split = jnp.where(
        row == jnp.where(col < 128, 2 * col, 2 * (col - 128) + 1), 1.0, 0.0
    ).astype(BF16)
    merge_z = jnp.where(
        col == jnp.where(row < 128, 2 * row, 2 * (row - 128) + 1), 1.0, 0.0
    ).astype(BF16)
    lane = lax.broadcasted_iota(jnp.int32, (64, 128), 1)

    w_in.wait()
    for b in range(3):
        flat = jnp.concatenate([w_v[(a * 3 + b) * 3 + c] for a in range(3) for c in range(3)], axis=0)
        high, low = high_low(flat.T)
        if b == 1:
            wf_e[0:128], wf_e[128:256] = high, low
        else:
            at_row = 0 if b == 2 else 128
            wf_o[at_row : at_row + 128] = high
            wf_o[256 + at_row : 384 + at_row] = low

    def split_slab(x):
        high, low = high_low(fine_v[x].reshape(CI * 16, 256))
        for part, dst in ((high, x_hi), (low, x_lo)):
            both = dot(part, split)
            even_t[...] = both[:, :128]
            odd_t[...] = both[:, 128:]
            for y in range(16):
                half, lanes = y % 2, slice(y // 2 * 128, y // 2 * 128 + 128)
                even = even_t[pl.ds(y, CI, stride=16), :]
                odd = odd_t[pl.ds(y, CI, stride=16), :]
                before = jnp.where(lane == 0, 0.0, pltpu.roll(odd, 1, 1))
                for c, value in enumerate((before, even, odd)):
                    rows = slice(x * 192 + c * 64, x * 192 + c * 64 + 64)
                    dst[half, rows, lanes] = value.astype(BF16)

    def operands(mx):
        x0, x1 = ((0, 2), (1, 4), (3, 4))[mx]
        a0 = (1, 0, 0)[mx]
        depth = (x1 - x0) * 192
        return slice(x0 * 192, x1 * 192), slice(a0 * 192, a0 * 192 + depth)

    def forward_rim(mx):
        rows, cols = operands(mx)
        value = dot(wf_o[:, cols], x_hi[1, rows, 896:1024])
        return value[128:256] + value[384:512] + dot(wf_o[128:256, cols], x_lo[1, rows, 896:1024])

    def forward(mx):
        rows, cols = operands(mx)
        target = conv.at[mx]
        target[:, 0:128] = jnp.zeros((CO, 128), F32)

        def chunk(n, carry):
            here = pl.ds(pl.multiple_of(n * 256, 256), 256)
            e_hi, e_lo = x_hi[0, rows, here], x_lo[0, rows, here]
            o_hi, o_lo = x_hi[1, rows, here], x_lo[1, rows, here]
            e = dot(wf_e[:, cols], e_hi)
            e = e[:128] + e[128:] + dot(wf_e[0:128, cols], e_lo)
            o = dot(wf_o[:, cols], o_hi)
            o = o[:256] + o[256:] + dot(wf_o[0:256, cols], o_lo)
            e = e + o[:128]
            target[:, pl.ds(pl.multiple_of(n * 256, 256), 128)] += e[:, :128]
            target[:, pl.ds(pl.multiple_of(n * 256 + 128, 128), 128)] = e[:, 128:] + o[128:, :128]

            target[:, pl.ds(pl.multiple_of(n * 256 + 256, 256), 128)] = o[128:, 128:]
            return carry

        lax.fori_loop(0, 4, chunk, 0)

    out_rows = cells_out.reshape(CO * 32, 128)

    def lanes_of(my):
        return slice(my * 128, my * 128 + 128)

    def store_rows(mx):
        for my in range(8):
            out_rows[pl.ds(FIRST[mx] + my, 128, stride=32), :] = conv[mx, :, lanes_of(my)]
        out_rows[pl.ds(24 + mx, 128, stride=32), :] = conv[mx, :, lanes_of(8)]

    def send_cells(part):
        start, rows = PARTS[part]

        def send(k, carry):
            to = lax.rem(me + k, N_DEV)
            src, dst = (ref.at[i, pl.ds(start, rows)] for ref, i in ((cells_out, to), (cells_in, me)))
            remote(src, dst, conv_send.at[part], conv_recv.at[part], at(to)).start()
            return carry

        lax.fori_loop(1, N_DEV, send, 0)

    fine_in[0].wait()
    split_slab(3)
    forward(2)
    store_rows(2)
    pl.semaphore_wait(barrier, N_DEV - 1)
    to_pair = remote(conv.at[2, :, pl.ds(0, 1024)], pair_x, pair_send.at[4], pair_recv.at[4], pair_device)

    @pl.when(core == 0)
    def _():
        to_pair.start()

    @pl.when(core == 1)
    def _():
        send_cells(0)

    for i, x in ((1, 2), (2, 1)):
        fine_in[i].wait()
        split_slab(x)
    forward(1)
    store_rows(1)
    send_cells(1)
    fine_in[3].wait()
    split_slab(0)
    forward(0)

    @pl.when(core == 0)
    def _():
        to_pair.wait_send()

    @pl.when(core == 1)
    def _():
        to_pair.wait_recv()
        conv[0, :, 0:1024] += pair_x[...]

    store_rows(0)
    send_cells(2)
    cells_in[pl.ds(me, 1)] = cells_out[pl.ds(me, 1)]

    for tap in range(9):
        turned = [w_v[tap * 3 + c] for c in range(3)]
        for half, (now, later) in enumerate(((turned[1], None), (turned[2], turned[0]))):
            rows = slice(tap * 128 + half * 64, tap * 128 + half * 64 + 64)
            for k, block in enumerate((now, later)):
                if block is None:
                    high = low = jnp.zeros((64, 128), BF16)
                else:
                    high, low = high_low(block)
                wb[rows, k * 128 : k * 128 + 128] = high
                wb[rows, 256 + k * 128 : 384 + k * 128] = high
                wb[rows, 512 + k * 128 : 640 + k * 128] = low

    cot_in.wait()
    for part, (start, rows) in enumerate(PARTS):
        if part > 0:
            moved = cells_out.at[pl.ds(0, N_DEV - 1), pl.ds(0, rows)]
            remote(moved, moved, conv_send.at[part], conv_recv.at[part], right).wait()
        else:
            for which in range(2):

                @pl.when(core == which)
                def _(which=which):
                    arrived = cells_in.at[pl.ds(0, N_CHIP - which), pl.ds(0, 8)]
                    remote(arrived, arrived, conv_send.at[0], conv_recv.at[0], right).wait_recv()
                    if which == 1:
                        sent = cells_out.at[pl.ds(0, N_DEV - 1), pl.ds(0, 8)]
                        remote(sent, sent, conv_send.at[0], conv_recv.at[0], right).wait_send()

    first = lax.broadcasted_iota(jnp.int32, (8, 128), 0) == 0

    def device(x, y):
        return x * GY + y

    total = jnp.zeros((8, 128), F32)
    for x in range(GX):
        for y in range(GY):
            for half in range(2):
                tile = cells_in[device(x, y), FIRST[half] : FIRST[half] + 8]
                if y > 0:
                    edge = cells_in[device(x, y - 1), 24 + half : 25 + half]
                    if half == 0 and x > 0:
                        edge += cells_in[device(x - 1, y - 1), 26:27]
                    tile += jnp.where(first, edge, 0.0)
                if half == 0 and x % 2 == 0 and x > 0:
                    tile += cells_in[device(x - 1, y), 0:8]
                whole[2 * x + half, 8 * y : 8 * y + 8] = tile
                total += tile

    def everything_in(value):
        return jnp.sum(jnp.sum(value, axis=1, keepdims=True), axis=0, keepdims=True)

    average = everything_in(total) * (1.0 / CELLS)

    def moment(i, carry):
        away = whole[i] - average
        return carry + jnp.sum((away * away).reshape(8, 8, 128), axis=0)

    spread = everything_in(lax.fori_loop(0, 32, moment, jnp.zeros((8, 128), F32), unroll=4)) * (1.0 / CELLS)
    inv_std = 1.0 / jnp.sqrt(spread + EPSILON)
    own_gain, own_shift = gain[0], shift[0]

    def activate(i, carry):
        s0, s1 = carry
        normed = (whole[i] - average) * inv_std
        pre = own_gain * normed + own_shift
        sig = 1.0 / (1.0 + jnp.exp(-pre))
        act_v[i] = pre * sig
        grad = cot_v[i] * sig * (1.0 + pre * (1.0 - sig))
        cot_v[i] = grad
        whole[i] = normed
        return s0 + jnp.sum(grad.reshape(8, 8, 128), axis=0), s1 + jnp.sum((grad * normed).reshape(8, 8, 128), axis=0)

    sums = lax.fori_loop(0, 32, activate, (jnp.zeros((8, 128), F32), jnp.zeros((8, 128), F32)), unroll=2)
    sum_g, sum_gn = everything_in(sums[0]), everything_in(sums[1])
    gs_out[...] = sum_g * RESCALE
    gg_out[...] = sum_gn * RESCALE
    mean_g, mean_gn = own_gain * sum_g * (1.0 / CELLS), own_gain * sum_gn * (1.0 / CELLS)

    def finish(i, carry):
        whole[i] = inv_std * (own_gain * cot_v[i] - mean_g - whole[i] * mean_gn)
        return carry

    lax.fori_loop(0, 32, finish, 0, unroll=4)
    act_copy = pltpu.make_async_copy(act_v, act_out, local_sem.at[7])
    act_copy.start()
    for x in range(GX):
        for y in range(GY):
            to = device(x, y)
            tiles = pl.ds(8 * y, 8)
            for half in range(2):
                grad_out[to, FIRST[half] : FIRST[half] + 8] = whole[2 * x + half, tiles]
            if x % 2 == 1:
                grad_out[to, 0:8] = whole[2 * x + 2, tiles] if x < GX - 1 else jnp.zeros((8, 128), F32)
            for k in range(3):
                inside = y < GY - 1 and (k < 2 or x < GX - 1)
                grad_out[to, 24 + k : 25 + k] = (
                    whole[2 * x + k, 8 * y + 8 : 8 * y + 9] if inside else jnp.zeros((1, 128), F32)
                )

    grad_in[pl.ds(me, 1)] = grad_out[pl.ds(me, 1)]

    def grad_copy(part, to):
        start, rows = PARTS[part]
        src, dst = (ref.at[i, pl.ds(start, rows)] for ref, i in ((grad_out, to), (grad_in, me)))
        return remote(src, dst, grad_send.at[part], grad_recv.at[part], at(to))

    for part in (2, 1):

        def send(k, carry, part=part):
            grad_copy(part, lax.rem(me + k, N_DEV)).start()
            return carry

        lax.fori_loop(1, N_DEV, send, 0)

    def send_next(k, carry):
        other = lax.rem(chip + k, N_CHIP)
        grad_copy(0, (2 * (other // GY) + 1) * GY + lax.rem(other, GY)).start()
        return carry

    @pl.when(core == 0)
    def _():
        send_next(0, 0)

    lax.fori_loop(1, N_CHIP, send_next, 0)

    def grad_wait(part):
        arrived = grad_in.at[pl.ds(0, N_DEV - 1), pl.ds(0, PARTS[part][1])]
        remote(arrived, arrived, grad_send.at[part], grad_recv.at[part], right).wait_recv()

    wide = lax.broadcasted_iota(jnp.int32, (128, 128), 1)
    grad_rows = grad_in.reshape(CO * 32, 128)

    def place(row, mx, lanes):
        value = grad_rows[pl.ds(row, 128, stride=32), :]
        high, low = high_low(value)
        g_w[mx, 0:128, lanes] = high
        g_w[mx, 128:256, lanes] = low
        g_i[mx, 0:128, lanes] = high
        g_i[mx, 256:384, lanes] = low
        g_i[mx, 512:640, lanes] = high
        moved = jnp.where(wide == 127, 0.0, pltpu.roll(value, 127, 1))
        high, low = high_low(moved)
        g_i[mx, 128:256, lanes] = high
        g_i[mx, 384:512, lanes] = low
        g_i[mx, 640:768, lanes] = high

    def place_rows(mx):
        for my in range(8):
            place(FIRST[mx] + my, mx, lanes_of(my))

    def weight_terms(mx):
        x_rows, cols = operands(mx)
        for b in range(3):
            half = 0 if b == 1 else 1
            here = g_w[mx, :, slice(128, 1152) if b == 0 else slice(0, 1024)]
            both = dot_nt(x_hi[half, x_rows, :], here)
            value = both[:, :128] + both[:, 128:] + dot_nt(x_lo[half, x_rows, :], here[:128])
            for k in range(value.shape[0] // 192):
                a = cols.start // 192 + k
                into = slice((a + 2) % 3 * 576 + b * 192, (a + 2) % 3 * 576 + b * 192 + 192)
                if mx == 0 or (mx == 1 and a == 0):
                    wg[into] = value[192 * k : 192 * k + 192]
                else:
                    wg[into] += value[192 * k : 192 * k + 192]

    def add_to(x, half, lanes, value, fresh):
        if fresh:
            o_acc[x, half, :, lanes] = value
        else:
            o_acc[x, half, :, lanes] += value

    def input_terms(mx):
        taps = [a for a in range(3) if 0 <= 2 * mx - 1 + a <= 3]
        top, bottom = taps[0] * 384, taps[-1] * 384 + 384

        def chunk(n, carry):
            here = pl.ds(pl.multiple_of(n * 256, 256), 256)
            first = pl.ds(pl.multiple_of(n * 256, 256), 128)
            second = pl.ds(pl.multiple_of(n * 256 + 128, 128), 128)
            terms = dot(wb[top:bottom, :], g_i[mx, :, here])
            for a in taps:
                x = 2 * mx - 1 + a
                block = terms[a * 384 - top : a * 384 - top + 384]
                add_to(x, 0, here, block[128:256], a > 0)
                add_to(x, 1, first, block[256:384, :128] + block[0:128, 128:], a > 0)
                add_to(x, 1, second, block[256:384, 128:], a > 0)

                @pl.when(n > 0)
                def _(x=x, block=block):
                    before = pl.ds(pl.multiple_of(n * 256 - 128, 128), 128)
                    o_acc[x, 1, :, before] += block[0:128, :128]

            return carry

        lax.fori_loop(0, 4, chunk, 0)

    def input_terms_rim(mx):
        for a in range(3):
            x = 2 * mx - 1 + a
            if 0 <= x <= 3:
                value = dot(wb[a * 384 : a * 384 + 128, :], g_i[mx, :, 1024:1152])
                o_acc[x, 1, :, 896:1024] += value

    def merge(x):
        slot = x % 2
        if x >= 2:
            for copy in copies[2 * (x - 2) : 2 * (x - 2) + 2]:
                copy.wait()
        for half in range(2):
            blocks = [
                jnp.concatenate([o_acc[x, half, 0:64, lanes_of(my)], o_acc[x, half, 64:128, lanes_of(my)]], axis=1)
                for my in range(8)
            ]
            high, low = high_low(jnp.concatenate(blocks, axis=0))
            merged = dot(high, merge_z) + dot(low, merge_z)
            for my in range(8):
                for z in range(2):
                    out_v[slot, z, pl.ds(2 * my + half, 64, stride=16), :] = merged[
                        64 * my : 64 * my + 64, 128 * z : 128 * z + 128
                    ]
        for z in range(2):
            copy = pltpu.make_async_copy(
                out_v.at[slot, z].reshape(CI, 16, 128),
                gin_out.at[:, x, :, pl.ds(128 * z, 128)],
                out_sem.at[slot, z],
            )
            copy.start()
            copies.append(copy)

    def start_pair(group):
        first, size = GROUPS[group]
        there = wg.at[pl.ds(pl.multiple_of(first + (1 - core) * size, 16), size)]
        copy = remote(there, wg_pair.at[pl.ds(first // 2, size)], pair_send.at[group], pair_recv.at[group], pair_device)
        copy.start()
        return copy

    def chip_device(index):
        return (2 * (index // GY) + core, lax.rem(index, GY))

    def slice_of(index):
        return pl.ds(pl.multiple_of(index * 16, 16), 16)

    def share_out(group, copy):
        first, size = GROUPS[group]
        copy.wait()
        here = wg[pl.ds(pl.multiple_of(first + core * size, 16), size)]
        half = slice(first // 2, first // 2 + size)
        wg_half[half] = here + wg_pair[half]
        owners = (first // 32, (first // 2 + size) // 16)

        def send(k, carry):
            to = lax.rem(chip + k, N_CHIP)

            @pl.when((to >= owners[0]) & (to < owners[1]))
            def _():
                remote(wg_half.at[slice_of(to)], wg_in.at[chip], wr_send, wr_recv, chip_device(to)).start()

            return carry

        lax.fori_loop(1, N_CHIP, send, 0)

    copies = []
    grad_wait(2)
    from_pair = remote(grad_in.at[:, pl.ds(16, 8)], grad_in.at[:, pl.ds(0, 8)], pair_send.at[5], pair_recv.at[5], pair_device)

    @pl.when(core == 1)
    def _():
        from_pair.start()

    place_rows(0)
    for mx in range(3):
        place(24 + mx, mx, lanes_of(8))
    weight_terms(0)
    input_terms(0)
    input_terms_rim(0)
    grad_wait(1)
    place_rows(1)
    weight_terms(1)
    pair_0 = start_pair(0)
    @pl.when(core == 0)
    def _():
        from_pair.wait_recv()

    @pl.when(core == 1)
    def _():
        grad_wait(0)

    place_rows(2)
    weight_terms(2)
    pair_1 = start_pair(1)
    share_out(0, pair_0)
    share_out(1, pair_1)
    input_terms(1)
    input_terms_rim(1)
    input_terms(2)
    input_terms_rim(2)
    own_slice = pl.ds(pl.multiple_of(chip * 16 + jnp.where(chip < CUT, core * 576, 576 + core * 288), 16), 16)

    @pl.when(chip < OWNERS)
    def _():
        wg_in[pl.ds(chip, 1)] = wg_half[slice_of(chip)][None]
        everyone = wg_in.at[pl.ds(0, N_CHIP - 1)]
        remote(everyone, everyone, wr_send, wr_recv, right).wait_recv()
        wg_all[own_slice] = jnp.sum(wg_in[...], axis=0) * RESCALE

    for group in range(2):

        @pl.when((chip < CUT) if group == 0 else (chip >= CUT) & (chip < OWNERS))
        def _(group=group):
            def send_slice(k, carry):
                src = wg_all.at[own_slice]
                to = chip_device(lax.rem(chip + k, N_CHIP))
                remote(src, src, wa_send, wa_recv.at[group], to).start()
                return carry

            lax.fori_loop(1, N_CHIP, send_slice, 0)

    for x in range(4):
        merge(x)
    @pl.when(chip < OWNERS)
    def _():
        some = wg_half.at[pl.ds(0, 16 * (OWNERS - 1))]
        remote(some, some, wr_send, wr_recv, right).wait_send()
        everyone = wg_in.at[pl.ds(0, N_CHIP - 1)]
        remote(everyone, everyone, wa_send, wa_recv.at[0], right).wait_send()

    @pl.when(chip >= OWNERS)
    def _():
        remote(wg_half, wg_half, wr_send, wr_recv, right).wait_send()

    last = []
    for group, (low, high) in enumerate(((0, CUT), (CUT, OWNERS))):
        inside = (chip >= low) & (chip < high)
        for missing in range(2):

            @pl.when(inside if missing else jnp.logical_not(inside))
            def _(group=group, rows=(high - low - missing) * 16):
                some = wg_all.at[pl.ds(0, rows)]
                remote(some, some, wa_send, wa_recv.at[group], right).wait_recv()

        first, size = GROUPS[group]
        done = wg_all.at[pl.ds(pl.multiple_of(first + core * size, 16), size)]
        last.append(remote(done, done, pair_send.at[2 + group], pair_recv.at[2 + group], pair_device))
        last[-1].start()
    for copy in last:
        copy.wait()
    for a in range(3):
        for b in range(3):
            rows = slice((a + 2) % 3 * 576 + b * 192, (a + 2) % 3 * 576 + b * 192 + 192)
            gw_out[(a * 3 + b) * 3 : (a * 3 + b) * 3 + 3] = wg_all[rows].reshape(3, CI, CO)
    for part in (2, 1):
        sent = grad_out.at[pl.ds(0, N_DEV - 1), pl.ds(0, PARTS[part][1])]
        remote(sent, sent, grad_send.at[part], grad_recv.at[part], right).wait_send()
    for which in range(2):

        @pl.when(core == which)
        def _(which=which):
            sent = grad_out.at[pl.ds(0, N_CHIP - which), pl.ds(0, 8)]
            remote(sent, sent, grad_send.at[0], grad_recv.at[0], right).wait_send()
            if which == 1:
                from_pair.wait_send()

    act_copy.wait()
    for copy in copies[4:]:
        copy.wait()


def hand_over(*refs):
    sources, targets, buffers, sem = refs[:3], refs[3:6], refs[6:9], refs[9]
    reads, writes = [], []
    for source, target, buffer, pieces in zip(sources, targets, buffers, (2, 8, 1)):
        size = source.shape[0] // pieces
        for piece in range(pieces):
            here = pl.ds(piece * size, size)
            k = len(reads)
            reads.append(pltpu.make_async_copy(source.at[here], buffer.at[here], sem.at[0, k]))
            writes.append(pltpu.make_async_copy(buffer.at[here], target.at[here], sem.at[1, k]))
    for read in reads:
        read.start()
    for read, write in zip(reads, writes):
        read.wait()
        write.start()
    for write in writes:
        write.wait()


def local(fine_input, weights, norm_gain, norm_shift, cotangent):
    any_space = pl.BlockSpec(memory_space=pl.ANY)
    vmem = pl.BlockSpec(memory_space=pltpu.VMEM)
    smem = pl.BlockSpec(memory_space=pltpu.SMEM)
    dma = pltpu.SemaphoreType.DMA
    activated, grad_input, grad_weights, grad_gain, grad_shift = pl.pallas_call(
        kernel,
        out_shape=(
            jax.ShapeDtypeStruct((32, 64, 128), F32),
            jax.ShapeDtypeStruct((CI, 4, 16, 256), F32),
            jax.ShapeDtypeStruct((27, CI, CO), F32),
            jax.ShapeDtypeStruct((1, 1), F32),
            jax.ShapeDtypeStruct((1, 1), F32),
        ),
        in_specs=[any_space, any_space, smem, smem, any_space],
        out_specs=(any_space, any_space, vmem, vmem, vmem),
        scratch_shapes=[
            pltpu.VMEM((4, CI, 16, 256), F32),
            pltpu.VMEM((27, CI, CO), F32),
            pltpu.VMEM((32, 64, 128), F32),
            pltpu.VMEM((2, 768, 1024), BF16),
            pltpu.VMEM((2, 768, 1024), BF16),
            pltpu.VMEM((1024, 128), F32),
            pltpu.VMEM((1024, 128), F32),
            pltpu.VMEM((256, 576), BF16),
            pltpu.VMEM((512, 576), BF16),
            pltpu.VMEM((1152, 768), BF16),
            pltpu.VMEM((3, CO, 1152), F32),
            pltpu.VMEM((CO, 1024), F32),
            pltpu.VMEM((N_DEV, 32, 128), F32),
            pltpu.VMEM((N_DEV, 32, 128), F32),
            pltpu.VMEM((32, 64, 128), F32),
            pltpu.VMEM((N_DEV, 32, 128), F32),
            pltpu.VMEM((N_DEV, 32, 128), F32),
            pltpu.VMEM((3, 256, 1152), BF16),
            pltpu.VMEM((3, 768, 1152), BF16),
            pltpu.VMEM((4, 2, 128, 1024), F32),
            pltpu.VMEM((2, 2, 1024, 128), F32),
            pltpu.VMEM((32, 64, 128), F32),
            pltpu.VMEM((27 * CI, 128), F32),
            pltpu.VMEM((HALF, 128), F32),
            pltpu.VMEM((HALF, 128), F32),
            pltpu.VMEM((N_CHIP, 16, 128), F32),
            pltpu.VMEM((27 * CI, 128), F32),
            dma((8,)),
            dma((2, 2)),
            dma((3,)),
            dma((3,)),
            dma((3,)),
            dma((3,)),
            dma,
            dma,
            dma,
            dma((2,)),
            dma((6,)),
            dma((6,)),
        ],
        compiler_params=pltpu.CompilerParams(
            collective_id=0, has_side_effects=True, vmem_limit_bytes=60 << 20
        ),
    )(fine_input, weights.transpose(0, 2, 1), norm_gain, norm_shift, cotangent)
    activated, grad_input, grad_weights = pl.pallas_call(
        hand_over,
        out_shape=(
            jax.ShapeDtypeStruct((32, 64, 128), F32),
            jax.ShapeDtypeStruct((CI, 4, 16, 256), F32),
            jax.ShapeDtypeStruct((27, CI, CO), F32),
        ),
        in_specs=[any_space] * 3,
        out_specs=(any_space,) * 3,
        scratch_shapes=[
            pltpu.VMEM((32, 64, 128), F32),
            pltpu.VMEM((CI, 4, 16, 256), F32),
            pltpu.VMEM((27, CI, CO), F32),
            dma((2, 11)),
        ],
        compiler_params=pltpu.CompilerParams(vmem_limit_bytes=60 << 20),
    )(activated, grad_input, grad_weights)
    activated, grad_weights = activated[None], grad_weights.transpose(0, 2, 1)
    return activated, grad_input, grad_weights, grad_gain.reshape(1), grad_shift.reshape(1)


def solution(mesh):
    placed = (
        P(None, "gx", "gy", None),
        P(),
        P(("gx", "gy")),
        P(("gx", "gy")),
        P(("gx", "gy"), None, None, None),
    )
    return jax.shard_map(
        local,
        mesh=mesh,
        in_specs=placed,
        out_specs=(
            P(("gx", "gy"), None, None, None),
            P(None, "gx", "gy", None),
            P(),
            P(("gx", "gy")),
            P(("gx", "gy")),
        ),
        check_vma=False,
    )
```

```python
import functools
import math

import jax
import jax.numpy as jnp
from jax import lax
from jax.experimental import pallas as pl
from jax.experimental.pallas import tpu as pltpu
from jax.sharding import PartitionSpec as P

MESH = pl.DeviceIdType.MESH
F32 = jnp.float32
BF16 = jnp.bfloat16
GX, GY, N_DEV = 16, 8, 128
CI, CO = 64, 128
CELLS = 32 * 64 * 128
RESCALE = 1.0 / math.sqrt(CELLS)
EPSILON = 1e-5
N_CHIP = N_DEV // 2
HALF = 27 * CI // 2
OWNERS = HALF // 16
FIRST = (16, 8, 0)
PARTS = ((0, 8), (8, 8), (16, 11))
GROUPS = ((0, 576), (1152, 288))
CUT = 36


def dot(a, b):
    return jnp.dot(a, b, preferred_element_type=F32)


def dot_nt(a, b):
    return lax.dot_general(a, b, (((1,), (1,)), ((), ())), preferred_element_type=F32)


def high_low(value):
    high = value.astype(BF16)
    return high, (value - high.astype(F32)).astype(BF16)


def kernel(
    fine, wts, gain, shift, cot, act_out, gin_out, gw_out, gg_out, gs_out,
    fine_v, w_v, cot_v, x_hi, x_lo, even_t, odd_t, wf_e, wf_o, wb,
    conv, pair_x, cells_out, cells_in, whole, grad_out, grad_in, g_w, g_i, o_acc, out_v,
    wg, wg_pair, wg_half, wg_in, wg_all,
    local_sem, out_sem, conv_send, conv_recv, grad_send, grad_recv, wr_send, wr_recv, wa_send, wa_recv,
    pair_send, pair_recv, row_sem,
):
    gx, gy = lax.axis_index("gx"), lax.axis_index("gy")
    me = gx * GY + gy
    core, chip = lax.rem(gx, 2), (gx // 2) * GY + gy
    pair_device = (gx + 1 - 2 * core, gy)
    right = (lax.rem(gx + 1, GX), gy)

    def at(lin):
        return (lin // GY, lax.rem(lin, GY))

    def remote(src, dst, send, recv, device):
        return pltpu.make_async_remote_copy(
            src_ref=src, dst_ref=dst, send_sem=send, recv_sem=recv,
            device_id=device, device_id_type=MESH,
        )

    fine_in = [
        pltpu.make_async_copy(fine.at[:, x], fine_v.at[x], local_sem.at[x]) for x in (3, 2, 1, 0)
    ]
    w_in = pltpu.make_async_copy(wts, w_v, local_sem.at[4])
    cot_in = pltpu.make_async_copy(cot.at[0], cot_v, local_sem.at[5])
    for copy in (w_in, *fine_in, cot_in):
        copy.start()

    barrier = pltpu.get_barrier_semaphore()

    def greet(sem, sizes):
        for count, device in zip(sizes, (lambda k: (lax.rem(gx + k, GX), gy), lambda k: (gx, lax.rem(gy + k, GY)))):

            def one(k, carry, device=device):
                pl.semaphore_signal(sem, inc=1, device_id=device(k), device_id_type=MESH)
                return carry

            lax.fori_loop(1, count, one, 0)

    greet(barrier, (GX, GY))

    row = lax.broadcasted_iota(jnp.int32, (256, 256), 0)
    col = lax.broadcasted_iota(jnp.int32, (256, 256), 1)
    split = jnp.where(
        row == jnp.where(col < 128, 2 * col, 2 * (col - 128) + 1), 1.0, 0.0
    ).astype(BF16)
    merge_z = jnp.where(
        col == jnp.where(row < 128, 2 * row, 2 * (row - 128) + 1), 1.0, 0.0
    ).astype(BF16)
    lane = lax.broadcasted_iota(jnp.int32, (64, 128), 1)

    w_in.wait()
    for b in range(3):
        flat = jnp.concatenate([w_v[(a * 3 + b) * 3 + c] for a in range(3) for c in range(3)], axis=0)
        high, low = high_low(flat.T)
        if b == 1:
            wf_e[0:128], wf_e[128:256] = high, low
        else:
            at_row = 0 if b == 2 else 128
            wf_o[at_row : at_row + 128] = high
            wf_o[256 + at_row : 384 + at_row] = low

    def split_slab(x):
        high, low = high_low(fine_v[x].reshape(CI * 16, 256))
        for part, dst in ((high, x_hi), (low, x_lo)):
            both = dot(part, split)
            even_t[...] = both[:, :128]
            odd_t[...] = both[:, 128:]
            for y in range(16):
                half, lanes = y % 2, slice(y // 2 * 128, y // 2 * 128 + 128)
                even = even_t[pl.ds(y, CI, stride=16), :]
                odd = odd_t[pl.ds(y, CI, stride=16), :]
                before = jnp.where(lane == 0, 0.0, pltpu.roll(odd, 1, 1))
                for c, value in enumerate((before, even, odd)):
                    rows = slice(x * 192 + c * 64, x * 192 + c * 64 + 64)
                    dst[half, rows, lanes] = value.astype(BF16)

    def operands(mx):
        x0, x1 = ((0, 2), (1, 4), (3, 4))[mx]
        a0 = (1, 0, 0)[mx]
        depth = (x1 - x0) * 192
        return slice(x0 * 192, x1 * 192), slice(a0 * 192, a0 * 192 + depth)

    def forward_rim(mx):
        rows, cols = operands(mx)
        value = dot(wf_o[:, cols], x_hi[1, rows, 896:1024])
        return value[128:256] + value[384:512] + dot(wf_o[128:256, cols], x_lo[1, rows, 896:1024])

    def forward(mx):
        rows, cols = operands(mx)
        target = conv.at[mx]
        target[:, 0:128] = jnp.zeros((CO, 128), F32)

        def chunk(n, carry):
            here = pl.ds(pl.multiple_of(n * 256, 256), 256)
            e_hi, e_lo = x_hi[0, rows, here], x_lo[0, rows, here]
            o_hi, o_lo = x_hi[1, rows, here], x_lo[1, rows, here]
            e = dot(wf_e[:, cols], e_hi)
            e = e[:128] + e[128:] + dot(wf_e[0:128, cols], e_lo)
            o = dot(wf_o[:, cols], o_hi)
            o = o[:256] + o[256:] + dot(wf_o[0:256, cols], o_lo)
            e = e + o[:128]
            target[:, pl.ds(pl.multiple_of(n * 256, 256), 128)] += e[:, :128]
            target[:, pl.ds(pl.multiple_of(n * 256 + 128, 128), 128)] = e[:, 128:] + o[128:, :128]

            target[:, pl.ds(pl.multiple_of(n * 256 + 256, 256), 128)] = o[128:, 128:]
            return carry

        lax.fori_loop(0, 4, chunk, 0)

    out_rows = cells_out.reshape(CO * 32, 128)

    def lanes_of(my):
        return slice(my * 128, my * 128 + 128)

    def store_rows(mx):
        for my in range(8):
            out_rows[pl.ds(FIRST[mx] + my, 128, stride=32), :] = conv[mx, :, lanes_of(my)]
        out_rows[pl.ds(24 + mx, 128, stride=32), :] = conv[mx, :, lanes_of(8)]

    def send_cells(part):
        start, rows = PARTS[part]

        def send(k, carry):
            to = lax.rem(me + k, N_DEV)
            src, dst = (ref.at[i, pl.ds(start, rows)] for ref, i in ((cells_out, to), (cells_in, me)))
            remote(src, dst, conv_send.at[part], conv_recv.at[part], at(to)).start()
            return carry

        lax.fori_loop(2, N_DEV, send, send(1, 0), unroll=6)

    fine_in[0].wait()
    split_slab(3)
    pl.semaphore_wait(barrier, GX + GY - 2)
    greet(row_sem, (GX,))
    forward(2)
    store_rows(2)
    pl.semaphore_wait(row_sem, GX - 1)
    to_pair = remote(conv.at[2, :, pl.ds(0, 1024)], pair_x, pair_send.at[4], pair_recv.at[4], pair_device)

    @pl.when(core == 0)
    def _():
        to_pair.start()

    @pl.when(core == 1)
    def _():
        send_cells(0)

    for i, x in ((1, 2), (2, 1)):
        fine_in[i].wait()
        split_slab(x)
    forward(1)
    store_rows(1)
    send_cells(1)
    fine_in[3].wait()
    split_slab(0)
    forward(0)

    @pl.when(core == 0)
    def _():
        to_pair.wait_send()

    @pl.when(core == 1)
    def _():
        to_pair.wait_recv()
        conv[0, :, 0:1024] += pair_x[...]

    store_rows(0)
    send_cells(2)
    cells_in[pl.ds(me, 1)] = cells_out[pl.ds(me, 1)]

    for tap in range(9):
        turned = [w_v[tap * 3 + c] for c in range(3)]
        for half, (now, later) in enumerate(((turned[1], None), (turned[2], turned[0]))):
            rows = slice(tap * 128 + half * 64, tap * 128 + half * 64 + 64)
            for k, block in enumerate((now, later)):
                if block is None:
                    high = low = jnp.zeros((64, 128), BF16)
                else:
                    high, low = high_low(block)
                wb[rows, k * 128 : k * 128 + 128] = high
                wb[rows, 256 + k * 128 : 384 + k * 128] = high
                wb[rows, 512 + k * 128 : 640 + k * 128] = low

    cot_in.wait()
    for part, (start, rows) in enumerate(PARTS):
        if part > 0:
            moved = cells_out.at[pl.ds(0, N_DEV - 1), pl.ds(0, rows)]
            remote(moved, moved, conv_send.at[part], conv_recv.at[part], right).wait()
        else:
            for which in range(2):

                @pl.when(core == which)
                def _(which=which):
                    arrived = cells_in.at[pl.ds(0, N_CHIP - which), pl.ds(0, 8)]
                    remote(arrived, arrived, conv_send.at[0], conv_recv.at[0], right).wait_recv()
                    if which == 1:
                        sent = cells_out.at[pl.ds(0, N_DEV - 1), pl.ds(0, 8)]
                        remote(sent, sent, conv_send.at[0], conv_recv.at[0], right).wait_send()

    first = lax.broadcasted_iota(jnp.int32, (8, 128), 0) == 0

    def device(x, y):
        return x * GY + y

    total = jnp.zeros((8, 128), F32)
    for x in range(GX):
        for y in range(GY):
            for half in range(2):
                tile = cells_in[device(x, y), FIRST[half] : FIRST[half] + 8]
                if y > 0:
                    edge = cells_in[device(x, y - 1), 24 + half : 25 + half]
                    if half == 0 and x > 0:
                        edge += cells_in[device(x - 1, y - 1), 26:27]
                    tile += jnp.where(first, edge, 0.0)
                if half == 0 and x % 2 == 0 and x > 0:
                    tile += cells_in[device(x - 1, y), 0:8]
                whole[2 * x + half, 8 * y : 8 * y + 8] = tile
                total += tile

    def everything_in(value):
        return jnp.sum(jnp.sum(value, axis=1, keepdims=True), axis=0, keepdims=True)

    average = everything_in(total) * (1.0 / CELLS)

    def moment(i, carry):
        away = whole[i] - average
        return carry + jnp.sum((away * away).reshape(8, 8, 128), axis=0)

    spread = everything_in(lax.fori_loop(0, 32, moment, jnp.zeros((8, 128), F32), unroll=4)) * (1.0 / CELLS)
    inv_std = 1.0 / jnp.sqrt(spread + EPSILON)
    own_gain, own_shift = gain[0], shift[0]

    def activate(i, carry):
        s0, s1 = carry
        normed = (whole[i] - average) * inv_std
        pre = own_gain * normed + own_shift
        sig = 1.0 / (1.0 + jnp.exp(-pre))
        act_out[i] = pre * sig
        grad = cot_v[i] * sig * (1.0 + pre * (1.0 - sig))
        cot_v[i] = grad
        whole[i] = normed
        return s0 + jnp.sum(grad.reshape(8, 8, 128), axis=0), s1 + jnp.sum((grad * normed).reshape(8, 8, 128), axis=0)

    sums = lax.fori_loop(0, 32, activate, (jnp.zeros((8, 128), F32), jnp.zeros((8, 128), F32)), unroll=2)
    sum_g, sum_gn = everything_in(sums[0]), everything_in(sums[1])
    gs_out[...] = sum_g * RESCALE
    gg_out[...] = sum_gn * RESCALE
    mean_g, mean_gn = own_gain * sum_g * (1.0 / CELLS), own_gain * sum_gn * (1.0 / CELLS)

    def finish(i, carry):
        whole[i] = inv_std * (own_gain * cot_v[i] - mean_g - whole[i] * mean_gn)
        return carry

    lax.fori_loop(0, 32, finish, 0, unroll=4)
    for x in range(GX):
        for y in range(GY):
            to = device(x, y)
            tiles = pl.ds(8 * y, 8)
            for half in range(2):
                grad_out[to, FIRST[half] : FIRST[half] + 8] = whole[2 * x + half, tiles]
            if x % 2 == 1:
                grad_out[to, 0:8] = whole[2 * x + 2, tiles] if x < GX - 1 else jnp.zeros((8, 128), F32)
            for k in range(3):
                inside = y < GY - 1 and (k < 2 or x < GX - 1)
                grad_out[to, 24 + k : 25 + k] = (
                    whole[2 * x + k, 8 * y + 8 : 8 * y + 9] if inside else jnp.zeros((1, 128), F32)
                )

    grad_in[pl.ds(me, 1)] = grad_out[pl.ds(me, 1)]

    def grad_copy(part, to):
        start, rows = PARTS[part]
        src, dst = (ref.at[i, pl.ds(start, rows)] for ref, i in ((grad_out, to), (grad_in, me)))
        return remote(src, dst, grad_send.at[part], grad_recv.at[part], at(to))

    for part in (2, 1):

        def send(k, carry, part=part):
            grad_copy(part, lax.rem(me + k, N_DEV)).start()
            return carry

        lax.fori_loop(2, N_DEV, send, send(1, 0), unroll=6)

    def send_next(k, carry):
        other = lax.rem(chip + k, N_CHIP)
        grad_copy(0, (2 * (other // GY) + 1) * GY + lax.rem(other, GY)).start()
        return carry

    @pl.when(core == 0)
    def _():
        send_next(0, 0)

    lax.fori_loop(1, N_CHIP, send_next, 0)

    def grad_wait(part):
        arrived = grad_in.at[pl.ds(0, N_DEV - 1), pl.ds(0, PARTS[part][1])]
        remote(arrived, arrived, grad_send.at[part], grad_recv.at[part], right).wait_recv()

    wide = lax.broadcasted_iota(jnp.int32, (128, 128), 1)
    grad_rows = grad_in.reshape(CO * 32, 128)

    def place(row, mx, lanes):
        value = grad_rows[pl.ds(row, 128, stride=32), :]
        high, low = high_low(value)
        g_w[mx, 0:128, lanes] = high
        g_w[mx, 128:256, lanes] = low
        g_i[mx, 0:128, lanes] = high
        g_i[mx, 256:384, lanes] = low
        g_i[mx, 512:640, lanes] = high
        moved = jnp.where(wide == 127, 0.0, pltpu.roll(value, 127, 1))
        high, low = high_low(moved)
        g_i[mx, 128:256, lanes] = high
        g_i[mx, 384:512, lanes] = low
        g_i[mx, 640:768, lanes] = high

    def place_rows(mx):
        for my in range(8):
            place(FIRST[mx] + my, mx, lanes_of(my))

    def weight_terms(mx):
        x_rows, cols = operands(mx)
        for b in range(3):
            half = 0 if b == 1 else 1
            here = g_w[mx, :, slice(128, 1152) if b == 0 else slice(0, 1024)]
            both = dot_nt(x_hi[half, x_rows, :], here)
            value = both[:, :128] + both[:, 128:] + dot_nt(x_lo[half, x_rows, :], here[:128])
            for k in range(value.shape[0] // 192):
                a = cols.start // 192 + k
                into = slice((a + 2) % 3 * 576 + b * 192, (a + 2) % 3 * 576 + b * 192 + 192)
                if mx == 0 or (mx == 1 and a == 0):
                    wg[into] = value[192 * k : 192 * k + 192]
                else:
                    wg[into] += value[192 * k : 192 * k + 192]

    def add_to(x, half, lanes, value, fresh):
        if fresh:
            o_acc[x, half, :, lanes] = value
        else:
            o_acc[x, half, :, lanes] += value

    def input_terms(mx):
        taps = [a for a in range(3) if 0 <= 2 * mx - 1 + a <= 3]
        top, bottom = taps[0] * 384, taps[-1] * 384 + 384

        def chunk(n, carry):
            here = pl.ds(pl.multiple_of(n * 256, 256), 256)
            first = pl.ds(pl.multiple_of(n * 256, 256), 128)
            second = pl.ds(pl.multiple_of(n * 256 + 128, 128), 128)
            terms = dot(wb[top:bottom, :], g_i[mx, :, here])
            for a in taps:
                x = 2 * mx - 1 + a
                block = terms[a * 384 - top : a * 384 - top + 384]
                add_to(x, 0, here, block[128:256], a > 0)
                add_to(x, 1, first, block[256:384, :128] + block[0:128, 128:], a > 0)
                add_to(x, 1, second, block[256:384, 128:], a > 0)

                @pl.when(n > 0)
                def _(x=x, block=block):
                    before = pl.ds(pl.multiple_of(n * 256 - 128, 128), 128)
                    o_acc[x, 1, :, before] += block[0:128, :128]

            return carry

        lax.fori_loop(0, 4, chunk, 0)

    def input_terms_rim(mx):
        for a in range(3):
            x = 2 * mx - 1 + a
            if 0 <= x <= 3:
                value = dot(wb[a * 384 : a * 384 + 128, :], g_i[mx, :, 1024:1152])
                o_acc[x, 1, :, 896:1024] += value

    def merge(x):
        slot = x % 2
        if x >= 2:
            for copy in copies[2 * (x - 2) : 2 * (x - 2) + 2]:
                copy.wait()
        for half in range(2):
            blocks = [
                jnp.concatenate([o_acc[x, half, 0:64, lanes_of(my)], o_acc[x, half, 64:128, lanes_of(my)]], axis=1)
                for my in range(8)
            ]
            high, low = high_low(jnp.concatenate(blocks, axis=0))
            merged = dot(high, merge_z) + dot(low, merge_z)
            for my in range(8):
                for z in range(2):
                    out_v[slot, z, pl.ds(2 * my + half, 64, stride=16), :] = merged[
                        64 * my : 64 * my + 64, 128 * z : 128 * z + 128
                    ]
        for z in range(2):
            copy = pltpu.make_async_copy(
                out_v.at[slot, z].reshape(CI, 16, 128),
                gin_out.at[:, x, :, pl.ds(128 * z, 128)],
                out_sem.at[slot, z],
            )
            copy.start()
            copies.append(copy)

    def start_pair(group):
        first, size = GROUPS[group]
        there = wg.at[pl.ds(pl.multiple_of(first + (1 - core) * size, 16), size)]
        copy = remote(there, wg_pair.at[pl.ds(first // 2, size)], pair_send.at[group], pair_recv.at[group], pair_device)
        copy.start()
        return copy

    def chip_device(index):
        return (2 * (index // GY) + core, lax.rem(index, GY))

    def slice_of(index):
        return pl.ds(pl.multiple_of(index * 16, 16), 16)

    def share_out(group, copy):
        first, size = GROUPS[group]
        copy.wait()
        here = wg[pl.ds(pl.multiple_of(first + core * size, 16), size)]
        half = slice(first // 2, first // 2 + size)
        wg_half[half] = here + wg_pair[half]
        owners = (first // 32, (first // 2 + size) // 16)

        def send(k, carry):
            to = lax.rem(chip + k, N_CHIP)

            @pl.when((to >= owners[0]) & (to < owners[1]))
            def _():
                remote(wg_half.at[slice_of(to)], wg_in.at[chip], wr_send, wr_recv, chip_device(to)).start()

            return carry

        lax.fori_loop(1, N_CHIP, send, 0)

    copies = []
    grad_wait(2)
    from_pair = remote(grad_in.at[:, pl.ds(16, 8)], grad_in.at[:, pl.ds(0, 8)], pair_send.at[5], pair_recv.at[5], pair_device)

    @pl.when(core == 1)
    def _():
        from_pair.start()

    place_rows(0)
    for mx in range(3):
        place(24 + mx, mx, lanes_of(8))
    weight_terms(0)
    input_terms(0)
    input_terms_rim(0)
    grad_wait(1)
    place_rows(1)
    weight_terms(1)
    pair_0 = start_pair(0)
    @pl.when(core == 0)
    def _():
        from_pair.wait_recv()

    @pl.when(core == 1)
    def _():
        grad_wait(0)

    place_rows(2)
    weight_terms(2)
    pair_1 = start_pair(1)
    share_out(0, pair_0)
    share_out(1, pair_1)
    input_terms(1)
    input_terms_rim(1)
    input_terms(2)
    input_terms_rim(2)
    own_slice = pl.ds(pl.multiple_of(chip * 16 + jnp.where(chip < CUT, core * 576, 576 + core * 288), 16), 16)

    @pl.when(chip < OWNERS)
    def _():
        wg_in[pl.ds(chip, 1)] = wg_half[slice_of(chip)][None]
        everyone = wg_in.at[pl.ds(0, N_CHIP - 1)]
        remote(everyone, everyone, wr_send, wr_recv, right).wait_recv()
        wg_all[own_slice] = jnp.sum(wg_in[...], axis=0) * RESCALE

    for group in range(2):

        @pl.when((chip < CUT) if group == 0 else (chip >= CUT) & (chip < OWNERS))
        def _(group=group):
            def send_slice(k, carry):
                src = wg_all.at[own_slice]
                to = chip_device(lax.rem(chip + k, N_CHIP))
                remote(src, src, wa_send, wa_recv.at[group], to).start()
                return carry

            lax.fori_loop(1, N_CHIP, send_slice, 0)

    for x in range(4):
        merge(x)
    @pl.when(chip < OWNERS)
    def _():
        some = wg_half.at[pl.ds(0, 16 * (OWNERS - 1))]
        remote(some, some, wr_send, wr_recv, right).wait_send()
        everyone = wg_in.at[pl.ds(0, N_CHIP - 1)]
        remote(everyone, everyone, wa_send, wa_recv.at[0], right).wait_send()

    @pl.when(chip >= OWNERS)
    def _():
        remote(wg_half, wg_half, wr_send, wr_recv, right).wait_send()

    last = []
    for group, (low, high) in enumerate(((0, CUT), (CUT, OWNERS))):
        inside = (chip >= low) & (chip < high)
        for missing in range(2):

            @pl.when(inside if missing else jnp.logical_not(inside))
            def _(group=group, rows=(high - low - missing) * 16):
                some = wg_all.at[pl.ds(0, rows)]
                remote(some, some, wa_send, wa_recv.at[group], right).wait_recv()

        first, size = GROUPS[group]
        done = wg_all.at[pl.ds(pl.multiple_of(first + core * size, 16), size)]
        last.append(remote(done, done, pair_send.at[2 + group], pair_recv.at[2 + group], pair_device))
        last[-1].start()
    for copy in last:
        copy.wait()
    for a in range(3):
        for b in range(3):
            rows = slice((a + 2) % 3 * 576 + b * 192, (a + 2) % 3 * 576 + b * 192 + 192)
            gw_out[(a * 3 + b) * 3 : (a * 3 + b) * 3 + 3] = wg_all[rows].reshape(3, CI, CO)
    for part in (2, 1):
        sent = grad_out.at[pl.ds(0, N_DEV - 1), pl.ds(0, PARTS[part][1])]
        remote(sent, sent, grad_send.at[part], grad_recv.at[part], right).wait_send()
    for which in range(2):

        @pl.when(core == which)
        def _(which=which):
            sent = grad_out.at[pl.ds(0, N_CHIP - which), pl.ds(0, 8)]
            remote(sent, sent, grad_send.at[0], grad_recv.at[0], right).wait_send()
            if which == 1:
                from_pair.wait_send()

    for copy in copies[4:]:
        copy.wait()


def local(fine_input, weights, norm_gain, norm_shift, cotangent):
    any_space = pl.BlockSpec(memory_space=pl.ANY)
    vmem = pl.BlockSpec(memory_space=pltpu.VMEM)
    smem = pl.BlockSpec(memory_space=pltpu.SMEM)
    dma = pltpu.SemaphoreType.DMA
    activated, grad_input, grad_weights, grad_gain, grad_shift = pl.pallas_call(
        kernel,
        out_shape=(
            pltpu.VMEM((32, 64, 128), F32),
            pltpu.VMEM((CI, 4, 16, 256), F32),
            pltpu.VMEM((27, CI, CO), F32),
            jax.ShapeDtypeStruct((1, 1), F32),
            jax.ShapeDtypeStruct((1, 1), F32),
        ),
        in_specs=[any_space, any_space, smem, smem, any_space],
        out_specs=(vmem,) * 5,
        scratch_shapes=[
            pltpu.VMEM((4, CI, 16, 256), F32),
            pltpu.VMEM((27, CI, CO), F32),
            pltpu.VMEM((32, 64, 128), F32),
            pltpu.VMEM((2, 768, 1024), BF16),
            pltpu.VMEM((2, 768, 1024), BF16),
            pltpu.VMEM((1024, 128), F32),
            pltpu.VMEM((1024, 128), F32),
            pltpu.VMEM((256, 576), BF16),
            pltpu.VMEM((512, 576), BF16),
            pltpu.VMEM((1152, 768), BF16),
            pltpu.VMEM((3, CO, 1152), F32),
            pltpu.VMEM((CO, 1024), F32),
            pltpu.VMEM((N_DEV, 32, 128), F32),
            pltpu.VMEM((N_DEV, 32, 128), F32),
            pltpu.VMEM((32, 64, 128), F32),
            pltpu.VMEM((N_DEV, 32, 128), F32),
            pltpu.VMEM((N_DEV, 32, 128), F32),
            pltpu.VMEM((3, 256, 1152), BF16),
            pltpu.VMEM((3, 768, 1152), BF16),
            pltpu.VMEM((4, 2, 128, 1024), F32),
            pltpu.VMEM((2, 2, 1024, 128), F32),
            pltpu.VMEM((27 * CI, 128), F32),
            pltpu.VMEM((HALF, 128), F32),
            pltpu.VMEM((HALF, 128), F32),
            pltpu.VMEM((N_CHIP, 16, 128), F32),
            pltpu.VMEM((27 * CI, 128), F32),
            dma((8,)),
            dma((2, 2)),
            dma((3,)),
            dma((3,)),
            dma((3,)),
            dma((3,)),
            dma,
            dma,
            dma,
            dma((2,)),
            dma((6,)),
            dma((6,)),
            pltpu.SemaphoreType.REGULAR,
        ],
        compiler_params=pltpu.CompilerParams(
            collective_id=0, has_side_effects=True, vmem_limit_bytes=50 << 20
        ),
    )(fine_input, weights.transpose(0, 2, 1), norm_gain, norm_shift, cotangent)
    activated, grad_weights = activated[None], grad_weights.transpose(0, 2, 1)
    return activated, grad_input, grad_weights, grad_gain.reshape(1), grad_shift.reshape(1)


def solution(mesh):
    placed = (
        P(None, "gx", "gy", None),
        P(),
        P(("gx", "gy")),
        P(("gx", "gy")),
        P(("gx", "gy"), None, None, None),
    )
    return jax.shard_map(
        local,
        mesh=mesh,
        in_specs=placed,
        out_specs=(
            P(("gx", "gy"), None, None, None),
            P(None, "gx", "gy", None),
            P(),
            P(("gx", "gy")),
            P(("gx", "gy")),
        ),
        check_vma=False,
    )
```

```python
import functools
import math

import jax
import jax.numpy as jnp
from jax import lax
from jax.experimental import pallas as pl
from jax.experimental.pallas import tpu as pltpu
from jax.sharding import PartitionSpec as P

MESH = pl.DeviceIdType.MESH
F32 = jnp.float32
BF16 = jnp.bfloat16
GX, GY, N_DEV = 16, 8, 128
CI, CO = 64, 128
CELLS = 32 * 64 * 128
RESCALE = 1.0 / math.sqrt(CELLS)
EPSILON = 1e-5
N_CHIP = N_DEV // 2
HALF = 27 * CI // 2
OWNERS = HALF // 16
FIRST = (16, 8, 0)
PARTS = ((0, 8), (8, 8), (16, 11))
GROUPS = ((576, 576), (0, 288))
HALVES = (0, 576)
CUT = 36


def dot(a, b):
    return jnp.dot(a, b, preferred_element_type=F32)


def dot_nt(a, b):
    return lax.dot_general(a, b, (((1,), (1,)), ((), ())), preferred_element_type=F32)


def high_low(value):
    high = value.astype(BF16)
    return high, (value - high.astype(F32)).astype(BF16)


def kernel(
    fine, wts, gain, shift, cot, act_out, gin_out, gw_out, gg_out, gs_out,
    fine_v, w_v, cot_v, x_hi, x_lo, even_t, odd_t, wf_e, wf_o, wb,
    conv, pair_x, cells_out, cells_in, whole, grad_out, grad_in, g_w, g_i, o_acc, out_v,
    wg, wg_pair, wg_half, wg_in,
    local_sem, out_sem, conv_send, conv_recv, grad_send, grad_recv, wr_send, wr_recv, wa_send, wa_recv,
    pair_send, pair_recv, row_sem,
):
    gx, gy = lax.axis_index("gx"), lax.axis_index("gy")
    me = gx * GY + gy
    core, chip = lax.rem(gx, 2), (gx // 2) * GY + gy
    pair_device = (gx + 1 - 2 * core, gy)
    right = (lax.rem(gx + 1, GX), gy)

    def at(lin):
        return (lin // GY, lax.rem(lin, GY))

    def remote(src, dst, send, recv, device):
        return pltpu.make_async_remote_copy(
            src_ref=src, dst_ref=dst, send_sem=send, recv_sem=recv,
            device_id=device, device_id_type=MESH,
        )

    fine_in = [
        pltpu.make_async_copy(fine.at[:, x], fine_v.at[x], local_sem.at[x]) for x in (3, 2, 1, 0)
    ]
    w_in = pltpu.make_async_copy(wts, w_v, local_sem.at[4])
    cot_in = pltpu.make_async_copy(cot.at[0], cot_v, local_sem.at[5])
    for copy in (w_in, *fine_in, cot_in):
        copy.start()

    barrier = pltpu.get_barrier_semaphore()

    def greet(sem, sizes):
        for count, device in zip(sizes, (lambda k: (lax.rem(gx + k, GX), gy), lambda k: (gx, lax.rem(gy + k, GY)))):

            def one(k, carry, device=device):
                pl.semaphore_signal(sem, inc=1, device_id=device(k), device_id_type=MESH)
                return carry

            lax.fori_loop(1, count, one, 0)

    greet(barrier, (GX, GY))

    row = lax.broadcasted_iota(jnp.int32, (256, 256), 0)
    col = lax.broadcasted_iota(jnp.int32, (256, 256), 1)
    split = jnp.where(
        row == jnp.where(col < 128, 2 * col, 2 * (col - 128) + 1), 1.0, 0.0
    ).astype(BF16)
    merge_z = jnp.where(
        col == jnp.where(row < 128, 2 * row, 2 * (row - 128) + 1), 1.0, 0.0
    ).astype(BF16)
    lane = lax.broadcasted_iota(jnp.int32, (64, 128), 1)

    w_in.wait()
    for b in range(3):
        flat = jnp.concatenate([w_v[(a * 3 + b) * 3 + c] for a in range(3) for c in range(3)], axis=0)
        high, low = high_low(flat.T)
        if b == 1:
            wf_e[0:128], wf_e[128:256] = high, low
        else:
            at_row = 0 if b == 2 else 128
            wf_o[at_row : at_row + 128] = high
            wf_o[256 + at_row : 384 + at_row] = low

    def split_slab(x):
        high, low = high_low(fine_v[x].reshape(CI * 16, 256))
        for part, dst in ((high, x_hi), (low, x_lo)):
            both = dot(part, split)
            even_t[...] = both[:, :128]
            odd_t[...] = both[:, 128:]
            for y in range(16):
                half, lanes = y % 2, slice(y // 2 * 128, y // 2 * 128 + 128)
                even = even_t[pl.ds(y, CI, stride=16), :]
                odd = odd_t[pl.ds(y, CI, stride=16), :]
                before = jnp.where(lane == 0, 0.0, pltpu.roll(odd, 1, 1))
                for c, value in enumerate((before, even, odd)):
                    rows = slice(x * 192 + c * 64, x * 192 + c * 64 + 64)
                    dst[half, rows, lanes] = value.astype(BF16)

    def operands(mx):
        x0, x1 = ((0, 2), (1, 4), (3, 4))[mx]
        a0 = (1, 0, 0)[mx]
        depth = (x1 - x0) * 192
        return slice(x0 * 192, x1 * 192), slice(a0 * 192, a0 * 192 + depth)

    def forward_rim(mx):
        rows, cols = operands(mx)
        value = dot(wf_o[:, cols], x_hi[1, rows, 896:1024])
        return value[128:256] + value[384:512] + dot(wf_o[128:256, cols], x_lo[1, rows, 896:1024])

    def forward(mx):
        rows, cols = operands(mx)
        target = conv.at[mx]
        target[:, 0:128] = jnp.zeros((CO, 128), F32)

        def chunk(n, carry):
            here = pl.ds(pl.multiple_of(n * 256, 256), 256)
            e_hi, e_lo = x_hi[0, rows, here], x_lo[0, rows, here]
            o_hi, o_lo = x_hi[1, rows, here], x_lo[1, rows, here]
            e = dot(wf_e[:, cols], e_hi)
            e = e[:128] + e[128:] + dot(wf_e[0:128, cols], e_lo)
            o = dot(wf_o[:, cols], o_hi)
            o = o[:256] + o[256:] + dot(wf_o[0:256, cols], o_lo)
            e = e + o[:128]
            target[:, pl.ds(pl.multiple_of(n * 256, 256), 128)] += e[:, :128]
            target[:, pl.ds(pl.multiple_of(n * 256 + 128, 128), 128)] = e[:, 128:] + o[128:, :128]

            target[:, pl.ds(pl.multiple_of(n * 256 + 256, 256), 128)] = o[128:, 128:]
            return carry

        lax.fori_loop(0, 4, chunk, 0)

    out_rows = cells_out.reshape(CO * 32, 128)

    def lanes_of(my):
        return slice(my * 128, my * 128 + 128)

    def store_rows(mx):
        for my in range(8):
            out_rows[pl.ds(FIRST[mx] + my, 128, stride=32), :] = conv[mx, :, lanes_of(my)]
        out_rows[pl.ds(24 + mx, 128, stride=32), :] = conv[mx, :, lanes_of(8)]

    def send_cells(part):
        start, rows = PARTS[part]

        def send(k, carry):
            to = lax.rem(me + k, N_DEV)
            src, dst = (ref.at[i, pl.ds(start, rows)] for ref, i in ((cells_out, to), (cells_in, me)))
            remote(src, dst, conv_send.at[part], conv_recv.at[part], at(to)).start()
            return carry

        lax.fori_loop(2, N_DEV, send, send(1, 0), unroll=6)

    fine_in[0].wait()
    split_slab(3)
    pl.semaphore_wait(barrier, GX + GY - 2)
    greet(row_sem, (GX,))
    forward(2)
    store_rows(2)
    pl.semaphore_wait(row_sem, GX - 1)
    to_pair = remote(conv.at[2, :, pl.ds(0, 1024)], pair_x, pair_send.at[4], pair_recv.at[4], pair_device)

    @pl.when(core == 0)
    def _():
        to_pair.start()

    @pl.when(core == 1)
    def _():
        send_cells(0)

    for i, x in ((1, 2), (2, 1)):
        fine_in[i].wait()
        split_slab(x)
    forward(1)
    store_rows(1)
    send_cells(1)
    fine_in[3].wait()
    split_slab(0)
    forward(0)

    @pl.when(core == 0)
    def _():
        to_pair.wait_send()

    @pl.when(core == 1)
    def _():
        to_pair.wait_recv()
        conv[0, :, 0:1024] += pair_x[...]

    store_rows(0)
    send_cells(2)
    cells_in[pl.ds(me, 1)] = cells_out[pl.ds(me, 1)]

    for tap in range(9):
        turned = [w_v[tap * 3 + c] for c in range(3)]
        for half, (now, later) in enumerate(((turned[1], None), (turned[2], turned[0]))):
            rows = slice(tap * 128 + half * 64, tap * 128 + half * 64 + 64)
            for k, block in enumerate((now, later)):
                if block is None:
                    high = low = jnp.zeros((64, 128), BF16)
                else:
                    high, low = high_low(block)
                wb[rows, k * 128 : k * 128 + 128] = high
                wb[rows, 256 + k * 128 : 384 + k * 128] = high
                wb[rows, 512 + k * 128 : 640 + k * 128] = low

    cot_in.wait()
    for part, (start, rows) in enumerate(PARTS):
        if part > 0:
            moved = cells_out.at[pl.ds(0, N_DEV - 1), pl.ds(0, rows)]
            remote(moved, moved, conv_send.at[part], conv_recv.at[part], right).wait()
        else:
            for which in range(2):

                @pl.when(core == which)
                def _(which=which):
                    arrived = cells_in.at[pl.ds(0, N_CHIP - which), pl.ds(0, 8)]
                    remote(arrived, arrived, conv_send.at[0], conv_recv.at[0], right).wait_recv()
                    if which == 1:
                        sent = cells_out.at[pl.ds(0, N_DEV - 1), pl.ds(0, 8)]
                        remote(sent, sent, conv_send.at[0], conv_recv.at[0], right).wait_send()

    first = lax.broadcasted_iota(jnp.int32, (8, 128), 0) == 0

    def device(x, y):
        return x * GY + y

    total = jnp.zeros((8, 128), F32)
    for x in range(GX):
        for y in range(GY):
            for half in range(2):
                tile = cells_in[device(x, y), FIRST[half] : FIRST[half] + 8]
                if y > 0:
                    edge = cells_in[device(x, y - 1), 24 + half : 25 + half]
                    if half == 0 and x > 0:
                        edge += cells_in[device(x - 1, y - 1), 26:27]
                    tile += jnp.where(first, edge, 0.0)
                if half == 0 and x % 2 == 0 and x > 0:
                    tile += cells_in[device(x - 1, y), 0:8]
                whole[2 * x + half, 8 * y : 8 * y + 8] = tile
                total += tile

    def everything_in(value):
        return jnp.sum(jnp.sum(value, axis=1, keepdims=True), axis=0, keepdims=True)

    average = everything_in(total) * (1.0 / CELLS)

    def moment(i, carry):
        away = whole[i] - average
        return carry + jnp.sum((away * away).reshape(8, 8, 128), axis=0)

    spread = everything_in(lax.fori_loop(0, 32, moment, jnp.zeros((8, 128), F32), unroll=4)) * (1.0 / CELLS)
    inv_std = 1.0 / jnp.sqrt(spread + EPSILON)
    own_gain, own_shift = gain[0], shift[0]

    def activate(i, carry):
        s0, s1 = carry
        normed = (whole[i] - average) * inv_std
        pre = own_gain * normed + own_shift
        sig = 1.0 / (1.0 + jnp.exp(-pre))
        act_out[i] = pre * sig
        grad = cot_v[i] * sig * (1.0 + pre * (1.0 - sig))
        cot_v[i] = grad
        whole[i] = normed
        return s0 + jnp.sum(grad.reshape(8, 8, 128), axis=0), s1 + jnp.sum((grad * normed).reshape(8, 8, 128), axis=0)

    sums = lax.fori_loop(0, 32, activate, (jnp.zeros((8, 128), F32), jnp.zeros((8, 128), F32)), unroll=2)
    sum_g, sum_gn = everything_in(sums[0]), everything_in(sums[1])
    gs_out[...] = sum_g * RESCALE
    gg_out[...] = sum_gn * RESCALE
    mean_g, mean_gn = own_gain * sum_g * (1.0 / CELLS), own_gain * sum_gn * (1.0 / CELLS)

    def finish(i, carry):
        whole[i] = inv_std * (own_gain * cot_v[i] - mean_g - whole[i] * mean_gn)
        return carry

    lax.fori_loop(0, 32, finish, 0, unroll=4)
    for x in range(GX):
        for y in range(GY):
            to = device(x, y)
            tiles = pl.ds(8 * y, 8)
            for half in range(2):
                grad_out[to, FIRST[half] : FIRST[half] + 8] = whole[2 * x + half, tiles]
            if x % 2 == 1:
                grad_out[to, 0:8] = whole[2 * x + 2, tiles] if x < GX - 1 else jnp.zeros((8, 128), F32)
            for k in range(3):
                inside = y < GY - 1 and (k < 2 or x < GX - 1)
                grad_out[to, 24 + k : 25 + k] = (
                    whole[2 * x + k, 8 * y + 8 : 8 * y + 9] if inside else jnp.zeros((1, 128), F32)
                )

    grad_in[pl.ds(me, 1)] = grad_out[pl.ds(me, 1)]

    def grad_copy(part, to):
        start, rows = PARTS[part]
        src, dst = (ref.at[i, pl.ds(start, rows)] for ref, i in ((grad_out, to), (grad_in, me)))
        return remote(src, dst, grad_send.at[part], grad_recv.at[part], at(to))

    for part in (2, 1):

        def send(k, carry, part=part):
            grad_copy(part, lax.rem(me + k, N_DEV)).start()
            return carry

        lax.fori_loop(2, N_DEV, send, send(1, 0), unroll=6)

    def send_next(k, carry):
        other = lax.rem(chip + k, N_CHIP)
        grad_copy(0, (2 * (other // GY) + 1) * GY + lax.rem(other, GY)).start()
        return carry

    @pl.when(core == 0)
    def _():
        send_next(0, 0)

    lax.fori_loop(1, N_CHIP, send_next, 0, unroll=7)

    def grad_wait(part):
        arrived = grad_in.at[pl.ds(0, N_DEV - 1), pl.ds(0, PARTS[part][1])]
        remote(arrived, arrived, grad_send.at[part], grad_recv.at[part], right).wait_recv()

    wide = lax.broadcasted_iota(jnp.int32, (128, 128), 1)
    grad_rows = grad_in.reshape(CO * 32, 128)

    def rows_of(mx):
        yield from ((FIRST[mx] + my, lanes_of(my)) for my in range(8))

    def place_w(mx, rows):
        for row, lanes in rows:
            high, low = high_low(grad_rows[pl.ds(row, 128, stride=32), :])
            g_w[mx, 0:128, lanes] = high
            g_w[mx, 128:256, lanes] = low

    def place_i(mx, rows):
        for row, lanes in rows:
            value = grad_rows[pl.ds(row, 128, stride=32), :]
            for k, part in enumerate((value, jnp.where(wide == 127, 0.0, pltpu.roll(value, 127, 1)))):
                high, low = high_low(part)
                g_i[mx, 128 * k : 128 * k + 128, lanes] = high
                g_i[mx, 256 + 128 * k : 384 + 128 * k, lanes] = low
                g_i[mx, 512 + 128 * k : 640 + 128 * k, lanes] = high

    def weight_terms(mx):
        x_rows, cols = operands(mx)
        for b in range(3):
            half = 0 if b == 1 else 1
            here = g_w[mx, :, slice(128, 1152) if b == 0 else slice(0, 1024)]
            both = dot_nt(x_hi[half, x_rows, :], here)
            value = both[:, :128] + both[:, 128:] + dot_nt(x_lo[half, x_rows, :], here[:128])
            for k in range(value.shape[0] // 192):
                a = cols.start // 192 + k
                into = slice(a * 576 + b * 192, a * 576 + b * 192 + 192)
                if mx == 0 or (mx == 1 and a == 0):
                    wg[into] = value[192 * k : 192 * k + 192]
                else:
                    wg[into] += value[192 * k : 192 * k + 192]

    def add_to(x, half, lanes, value, fresh):
        if fresh:
            o_acc[x, half, :, lanes] = value
        else:
            o_acc[x, half, :, lanes] += value

    def input_terms(mx):
        taps = [a for a in range(3) if 0 <= 2 * mx - 1 + a <= 3]
        top, bottom = taps[0] * 384, taps[-1] * 384 + 384

        def chunk(n, carry):
            here = pl.ds(pl.multiple_of(n * 256, 256), 256)
            first = pl.ds(pl.multiple_of(n * 256, 256), 128)
            second = pl.ds(pl.multiple_of(n * 256 + 128, 128), 128)
            terms = dot(wb[top:bottom, :], g_i[mx, :, here])
            for a in taps:
                x = 2 * mx - 1 + a
                block = terms[a * 384 - top : a * 384 - top + 384]
                add_to(x, 0, here, block[128:256], a > 0)
                add_to(x, 1, first, block[256:384, :128] + block[0:128, 128:], a > 0)
                add_to(x, 1, second, block[256:384, 128:], a > 0)

                @pl.when(n > 0)
                def _(x=x, block=block):
                    before = pl.ds(pl.multiple_of(n * 256 - 128, 128), 128)
                    o_acc[x, 1, :, before] += block[0:128, :128]

            return carry

        lax.fori_loop(0, 4, chunk, 0)

    def input_terms_rim(mx):
        for a in range(3):
            x = 2 * mx - 1 + a
            if 0 <= x <= 3:
                value = dot(wb[a * 384 : a * 384 + 128, :], g_i[mx, :, 1024:1152])
                o_acc[x, 1, :, 896:1024] += value

    def merge(x):
        slot = x % 2
        if x >= 2:
            for copy in copies[2 * (x - 2) : 2 * (x - 2) + 2]:
                copy.wait()
        for half in range(2):
            blocks = [
                jnp.concatenate([o_acc[x, half, 0:64, lanes_of(my)], o_acc[x, half, 64:128, lanes_of(my)]], axis=1)
                for my in range(8)
            ]
            high, low = high_low(jnp.concatenate(blocks, axis=0))
            merged = dot(high, merge_z) + dot(low, merge_z)
            for my in range(8):
                for z in range(2):
                    out_v[slot, z, pl.ds(2 * my + half, 64, stride=16), :] = merged[
                        64 * my : 64 * my + 64, 128 * z : 128 * z + 128
                    ]
        for z in range(2):
            copy = pltpu.make_async_copy(
                out_v.at[slot, z].reshape(CI, 16, 128),
                gin_out.at[:, x, :, pl.ds(128 * z, 128)],
                out_sem.at[slot, z],
            )
            copy.start()
            copies.append(copy)

    def start_pair(group):
        first, size = GROUPS[group]
        there = wg.at[pl.ds(pl.multiple_of(first + (1 - core) * size, 16), size)]
        copy = remote(there, wg_pair.at[pl.ds(HALVES[group], size)], pair_send.at[group], pair_recv.at[group], pair_device)
        copy.start()
        return copy

    def chip_device(index):
        return (2 * (index // GY) + core, lax.rem(index, GY))

    def slice_of(index):
        return pl.ds(pl.multiple_of(index * 16, 16), 16)

    def share_out(group, copy):
        first, size = GROUPS[group]
        copy.wait()
        here = wg[pl.ds(pl.multiple_of(first + core * size, 16), size)]
        half = slice(HALVES[group], HALVES[group] + size)
        wg_half[half] = here + wg_pair[half]
        low, count = HALVES[group] // 16, size // 16

        def send(k, carry):
            to = low + lax.rem(chip + k, count)

            @pl.when(to != chip)
            def _():
                remote(wg_half.at[slice_of(to)], wg_in.at[chip], wr_send, wr_recv, chip_device(to)).start()

            return carry

        lax.fori_loop(0, count, send, 0, unroll=6)

    copies = []
    grad_wait(2)
    from_pair = remote(grad_in.at[:, pl.ds(16, 8)], grad_in.at[:, pl.ds(0, 8)], pair_send.at[5], pair_recv.at[5], pair_device)

    @pl.when(core == 1)
    def _():
        from_pair.start()

    by_y = [(24 + mx, lanes_of(8)) for mx in range(3)]
    place_w(0, rows_of(0))
    for mx in range(3):
        place_w(mx, by_y[mx : mx + 1])
    weight_terms(0)
    for mx in range(3):
        place_i(mx, by_y[mx : mx + 1])
    place_i(0, rows_of(0))
    input_terms(0)
    input_terms_rim(0)
    grad_wait(1)
    place_w(1, rows_of(1))
    weight_terms(1)
    pair_0 = start_pair(0)
    @pl.when(core == 0)
    def _():
        from_pair.wait_recv()

    @pl.when(core == 1)
    def _():
        grad_wait(0)

    place_w(2, rows_of(2))
    weight_terms(2)
    pair_1 = start_pair(1)
    share_out(0, pair_0)
    share_out(1, pair_1)
    place_i(1, rows_of(1))
    input_terms(1)
    input_terms_rim(1)
    place_i(2, rows_of(2))
    input_terms(2)
    input_terms_rim(2)
    own_slice = pl.ds(pl.multiple_of(chip * 16 + jnp.where(chip < CUT, 576 + core * 576, core * 288 - 576), 16), 16)

    @pl.when(chip < OWNERS)
    def _():
        wg_in[pl.ds(chip, 1)] = wg_half[slice_of(chip)][None]
        everyone = wg_in.at[pl.ds(0, N_CHIP - 1)]
        remote(everyone, everyone, wr_send, wr_recv, right).wait_recv()
        gw_out[own_slice] = jnp.sum(wg_in[...], axis=0) * RESCALE

    for group in range(2):

        @pl.when((chip < CUT) if group == 0 else (chip >= CUT) & (chip < OWNERS))
        def _(group=group):
            def send_slice(k, carry):
                src = gw_out.at[own_slice]
                to = chip_device(lax.rem(chip + k, N_CHIP))
                remote(src, src, wa_send, wa_recv.at[group], to).start()
                return carry

            lax.fori_loop(1, N_CHIP, send_slice, 0, unroll=7)

    for x in range(4):
        merge(x)
    @pl.when(chip < OWNERS)
    def _():
        some = wg_half.at[pl.ds(0, 16 * (OWNERS - 1))]
        remote(some, some, wr_send, wr_recv, right).wait_send()
        everyone = wg_in.at[pl.ds(0, N_CHIP - 1)]
        remote(everyone, everyone, wa_send, wa_recv.at[0], right).wait_send()

    @pl.when(chip >= OWNERS)
    def _():
        remote(wg_half, wg_half, wr_send, wr_recv, right).wait_send()

    last = []
    for group, (low, high) in enumerate(((0, CUT), (CUT, OWNERS))):
        inside = (chip >= low) & (chip < high)
        for missing in range(2):

            @pl.when(inside if missing else jnp.logical_not(inside))
            def _(group=group, rows=(high - low - missing) * 16):
                some = gw_out.at[pl.ds(0, rows)]
                remote(some, some, wa_send, wa_recv.at[group], right).wait_recv()

        first, size = GROUPS[group]
        done = gw_out.at[pl.ds(pl.multiple_of(first + core * size, 16), size)]
        last.append(remote(done, done, pair_send.at[2 + group], pair_recv.at[2 + group], pair_device))
        last[-1].start()
    for copy in last:
        copy.wait()
    for part in (2, 1):
        sent = grad_out.at[pl.ds(0, N_DEV - 1), pl.ds(0, PARTS[part][1])]
        remote(sent, sent, grad_send.at[part], grad_recv.at[part], right).wait_send()
    for which in range(2):

        @pl.when(core == which)
        def _(which=which):
            sent = grad_out.at[pl.ds(0, N_CHIP - which), pl.ds(0, 8)]
            remote(sent, sent, grad_send.at[0], grad_recv.at[0], right).wait_send()
            if which == 1:
                from_pair.wait_send()

    for copy in copies[4:]:
        copy.wait()


def hand_over(*refs):
    copies = []
    for source, target, pieces in zip(refs[:3], refs[3:6], (2, 8, 1)):
        size = source.shape[0] // pieces
        for piece in range(pieces):
            here = pl.ds(piece * size, size)
            copies.append(pltpu.make_async_copy(source.at[here], target.at[here], refs[6].at[len(copies)]))
    for copy in copies:
        copy.start()
    for copy in copies:
        copy.wait()


def local(fine_input, weights, norm_gain, norm_shift, cotangent):
    any_space = pl.BlockSpec(memory_space=pl.ANY)
    vmem = pl.BlockSpec(memory_space=pltpu.VMEM)
    smem = pl.BlockSpec(memory_space=pltpu.SMEM)
    dma = pltpu.SemaphoreType.DMA
    activated, grad_input, grad_weights, grad_gain, grad_shift = pl.pallas_call(
        kernel,
        out_shape=(
            pltpu.VMEM((32, 64, 128), F32),
            pltpu.VMEM((CI, 4, 16, 256), F32),
            pltpu.VMEM((27 * CI, CO), F32),
            jax.ShapeDtypeStruct((1, 1), F32),
            jax.ShapeDtypeStruct((1, 1), F32),
        ),
        in_specs=[any_space, any_space, smem, smem, any_space],
        out_specs=(vmem,) * 5,
        scratch_shapes=[
            pltpu.VMEM((4, CI, 16, 256), F32),
            pltpu.VMEM((27, CI, CO), F32),
            pltpu.VMEM((32, 64, 128), F32),
            pltpu.VMEM((2, 768, 1024), BF16),
            pltpu.VMEM((2, 768, 1024), BF16),
            pltpu.VMEM((1024, 128), F32),
            pltpu.VMEM((1024, 128), F32),
            pltpu.VMEM((256, 576), BF16),
            pltpu.VMEM((512, 576), BF16),
            pltpu.VMEM((1152, 768), BF16),
            pltpu.VMEM((3, CO, 1152), F32),
            pltpu.VMEM((CO, 1024), F32),
            pltpu.VMEM((N_DEV, 32, 128), F32),
            pltpu.VMEM((N_DEV, 32, 128), F32),
            pltpu.VMEM((32, 64, 128), F32),
            pltpu.VMEM((N_DEV, 32, 128), F32),
            pltpu.VMEM((N_DEV, 32, 128), F32),
            pltpu.VMEM((3, 256, 1152), BF16),
            pltpu.VMEM((3, 768, 1152), BF16),
            pltpu.VMEM((4, 2, 128, 1024), F32),
            pltpu.VMEM((2, 2, 1024, 128), F32),
            pltpu.VMEM((27 * CI, 128), F32),
            pltpu.VMEM((HALF, 128), F32),
            pltpu.VMEM((HALF, 128), F32),
            pltpu.VMEM((N_CHIP, 16, 128), F32),
            dma((8,)),
            dma((2, 2)),
            dma((3,)),
            dma((3,)),
            dma((3,)),
            dma((3,)),
            dma,
            dma,
            dma,
            dma((2,)),
            dma((6,)),
            dma((6,)),
            pltpu.SemaphoreType.REGULAR,
        ],
        compiler_params=pltpu.CompilerParams(
            collective_id=0, has_side_effects=True, vmem_limit_bytes=50 << 20
        ),
    )(fine_input, weights.transpose(0, 2, 1), norm_gain, norm_shift, cotangent)
    activated, grad_input, grad_weights = pl.pallas_call(
        hand_over,
        out_shape=tuple(jax.ShapeDtypeStruct(v.shape, F32) for v in (activated, grad_input, grad_weights)),
        in_specs=[any_space] * 3,
        out_specs=(any_space,) * 3,
        scratch_shapes=[dma((11,))],
        compiler_params=pltpu.CompilerParams(vmem_limit_bytes=1 << 20),
    )(activated, grad_input, grad_weights)
    activated, grad_weights = activated[None], grad_weights.reshape(27, CI, CO).transpose(0, 2, 1)
    return activated, grad_input, grad_weights, grad_gain.reshape(1), grad_shift.reshape(1)


def solution(mesh):
    placed = (
        P(None, "gx", "gy", None),
        P(),
        P(("gx", "gy")),
        P(("gx", "gy")),
        P(("gx", "gy"), None, None, None),
    )
    return jax.shard_map(
        local,
        mesh=mesh,
        in_specs=placed,
        out_specs=(
            P(("gx", "gy"), None, None, None),
            P(None, "gx", "gy", None),
            P(),
            P(("gx", "gy")),
            P(("gx", "gy")),
        ),
        check_vma=False,
    )
```

```python
import functools
import math

import jax
import jax.numpy as jnp
from jax import lax
from jax.experimental import pallas as pl
from jax.experimental.pallas import tpu as pltpu
from jax.sharding import PartitionSpec as P

MESH = pl.DeviceIdType.MESH
F32 = jnp.float32
BF16 = jnp.bfloat16
GX, GY, N_DEV = 16, 8, 128
CI, CO = 64, 128
CELLS = 32 * 64 * 128
RESCALE = 1.0 / math.sqrt(CELLS)
EPSILON = 1e-5
N_CHIP = N_DEV // 2
HALF = 27 * CI // 2
OWNERS = HALF // 16
FIRST = (16, 8, 0)
PARTS = ((0, 8), (8, 8), (16, 11))
GROUPS = ((576, 576), (0, 288))
HALVES = (0, 576)
CUT = 36


def dot(a, b):
    return jnp.dot(a, b, preferred_element_type=F32)


def dot_nt(a, b):
    return lax.dot_general(a, b, (((1,), (1,)), ((), ())), preferred_element_type=F32)


def high_low(value):
    high = value.astype(BF16)
    return high, (value - high.astype(F32)).astype(BF16)


def kernel(
    fine, wts, gain, shift, cot, act_out, gin_out, gw_out, gg_out, gs_out,
    fine_v, w_v, cot_v, x_hi, x_lo, even_t, odd_t, wf_e, wf_o, wb,
    conv, pair_x, cells_out, cells_in, whole, grad_out, grad_in, g_w, g_i, o_acc, out_v,
    wg, wg_pair, wg_half, wg_in,
    local_sem, out_sem, conv_send, conv_recv, grad_send, grad_recv, wr_send, wr_recv, wa_send, wa_recv,
    pair_send, pair_recv, row_sem,
):
    gx, gy = lax.axis_index("gx"), lax.axis_index("gy")
    me = gx * GY + gy
    core, chip = lax.rem(gx, 2), (gx // 2) * GY + gy
    pair_device = (gx + 1 - 2 * core, gy)
    right = (lax.rem(gx + 1, GX), gy)

    def at(lin):
        return (lin // GY, lax.rem(lin, GY))

    def remote(src, dst, send, recv, device):
        return pltpu.make_async_remote_copy(
            src_ref=src, dst_ref=dst, send_sem=send, recv_sem=recv,
            device_id=device, device_id_type=MESH,
        )

    fine_in = [
        pltpu.make_async_copy(fine.at[:, x], fine_v.at[x], local_sem.at[x]) for x in (3, 2, 1, 0)
    ]
    w_in = pltpu.make_async_copy(wts, w_v, local_sem.at[4])
    cot_in = pltpu.make_async_copy(cot.at[0], cot_v, local_sem.at[5])
    for copy in (w_in, *fine_in, cot_in):
        copy.start()

    barrier = pltpu.get_barrier_semaphore()

    def greet(sem, sizes):
        for count, device in zip(sizes, (lambda k: (lax.rem(gx + k, GX), gy), lambda k: (gx, lax.rem(gy + k, GY)))):

            def one(k, carry, device=device):
                pl.semaphore_signal(sem, inc=1, device_id=device(k), device_id_type=MESH)
                return carry

            lax.fori_loop(1, count, one, 0)

    greet(barrier, (GX, GY))

    row = lax.broadcasted_iota(jnp.int32, (256, 256), 0)
    col = lax.broadcasted_iota(jnp.int32, (256, 256), 1)
    split = jnp.where(
        row == jnp.where(col < 128, 2 * col, 2 * (col - 128) + 1), 1.0, 0.0
    ).astype(BF16)
    merge_z = jnp.where(
        col == jnp.where(row < 128, 2 * row, 2 * (row - 128) + 1), 1.0, 0.0
    ).astype(BF16)
    lane = lax.broadcasted_iota(jnp.int32, (64, 128), 1)

    w_in.wait()
    for b in range(3):
        flat = jnp.concatenate([w_v[(a * 3 + b) * 3 + c] for a in range(3) for c in range(3)], axis=0)
        high, low = high_low(flat.T)
        if b == 1:
            wf_e[0:128], wf_e[128:256] = high, low
        else:
            at_row = 0 if b == 2 else 128
            wf_o[at_row : at_row + 128] = high
            wf_o[256 + at_row : 384 + at_row] = low

    def split_slab(x):
        high, low = high_low(fine_v[x].reshape(CI * 16, 256))
        for part, dst in ((high, x_hi), (low, x_lo)):
            both = dot(part, split)
            even_t[...] = both[:, :128]
            odd_t[...] = both[:, 128:]
            for y in range(16):
                half, lanes = y % 2, slice(y // 2 * 128, y // 2 * 128 + 128)
                even = even_t[pl.ds(y, CI, stride=16), :]
                odd = odd_t[pl.ds(y, CI, stride=16), :]
                before = jnp.where(lane == 0, 0.0, pltpu.roll(odd, 1, 1))
                for c, value in enumerate((before, even, odd)):
                    rows = slice(x * 192 + c * 64, x * 192 + c * 64 + 64)
                    dst[half, rows, lanes] = value.astype(BF16)

    def operands(mx):
        x0, x1 = ((0, 2), (1, 4), (3, 4))[mx]
        a0 = (1, 0, 0)[mx]
        depth = (x1 - x0) * 192
        return slice(x0 * 192, x1 * 192), slice(a0 * 192, a0 * 192 + depth)

    def forward_rim(mx):
        rows, cols = operands(mx)
        value = dot(wf_o[:, cols], x_hi[1, rows, 896:1024])
        return value[128:256] + value[384:512] + dot(wf_o[128:256, cols], x_lo[1, rows, 896:1024])

    def forward(mx):
        rows, cols = operands(mx)
        target = conv.at[mx]
        target[:, 0:128] = jnp.zeros((CO, 128), F32)

        def chunk(n, carry):
            here = pl.ds(pl.multiple_of(n * 256, 256), 256)
            e_hi, e_lo = x_hi[0, rows, here], x_lo[0, rows, here]
            o_hi, o_lo = x_hi[1, rows, here], x_lo[1, rows, here]
            e = dot(wf_e[:, cols], e_hi)
            e = e[:128] + e[128:] + dot(wf_e[0:128, cols], e_lo)
            o = dot(wf_o[:, cols], o_hi)
            o = o[:256] + o[256:] + dot(wf_o[0:256, cols], o_lo)
            e = e + o[:128]
            target[:, pl.ds(pl.multiple_of(n * 256, 256), 128)] += e[:, :128]
            target[:, pl.ds(pl.multiple_of(n * 256 + 128, 128), 128)] = e[:, 128:] + o[128:, :128]

            target[:, pl.ds(pl.multiple_of(n * 256 + 256, 256), 128)] = o[128:, 128:]
            return carry

        lax.fori_loop(0, 4, chunk, 0)

    out_rows = cells_out.reshape(CO * 32, 128)

    def lanes_of(my):
        return slice(my * 128, my * 128 + 128)

    def store_rows(mx):
        for my in range(8):
            out_rows[pl.ds(FIRST[mx] + my, 128, stride=32), :] = conv[mx, :, lanes_of(my)]
        out_rows[pl.ds(24 + mx, 128, stride=32), :] = conv[mx, :, lanes_of(8)]

    def send_cells(part):
        start, rows = PARTS[part]

        def send(k, carry):
            to = lax.rem(me + k + core * (N_DEV - 2 * k), N_DEV)
            src, dst = (ref.at[i, pl.ds(start, rows)] for ref, i in ((cells_out, to), (cells_in, me)))
            remote(src, dst, conv_send.at[part], conv_recv.at[part], at(to)).start()
            return carry

        lax.fori_loop(2, N_DEV, send, send(1, 0), unroll=6)

    fine_in[0].wait()
    split_slab(3)
    pl.semaphore_wait(barrier, GX + GY - 2)
    greet(row_sem, (GX,))
    forward(2)
    store_rows(2)
    pl.semaphore_wait(row_sem, GX - 1)
    to_pair = remote(conv.at[2, :, pl.ds(0, 1024)], pair_x, pair_send.at[4], pair_recv.at[4], pair_device)

    @pl.when(core == 0)
    def _():
        to_pair.start()

    @pl.when(core == 1)
    def _():
        send_cells(0)

    for i, x in ((1, 2), (2, 1)):
        fine_in[i].wait()
        split_slab(x)
    forward(1)
    store_rows(1)
    send_cells(1)
    fine_in[3].wait()
    split_slab(0)
    forward(0)

    @pl.when(core == 0)
    def _():
        to_pair.wait_send()

    @pl.when(core == 1)
    def _():
        to_pair.wait_recv()
        conv[0, :, 0:1024] += pair_x[...]

    store_rows(0)
    send_cells(2)
    cells_in[pl.ds(me, 1)] = cells_out[pl.ds(me, 1)]

    for tap in range(9):
        turned = [w_v[tap * 3 + c] for c in range(3)]
        for half, (now, later) in enumerate(((turned[1], None), (turned[2], turned[0]))):
            rows = slice(tap * 128 + half * 64, tap * 128 + half * 64 + 64)
            for k, block in enumerate((now, later)):
                if block is None:
                    high = low = jnp.zeros((64, 128), BF16)
                else:
                    high, low = high_low(block)
                wb[rows, k * 128 : k * 128 + 128] = high
                wb[rows, 256 + k * 128 : 384 + k * 128] = high
                wb[rows, 512 + k * 128 : 640 + k * 128] = low

    cot_in.wait()
    for part, (start, rows) in enumerate(PARTS):
        if part > 0:
            moved = cells_out.at[pl.ds(0, N_DEV - 1), pl.ds(0, rows)]
            remote(moved, moved, conv_send.at[part], conv_recv.at[part], right).wait()
        else:
            for which in range(2):

                @pl.when(core == which)
                def _(which=which):
                    arrived = cells_in.at[pl.ds(0, N_CHIP - which), pl.ds(0, 8)]
                    remote(arrived, arrived, conv_send.at[0], conv_recv.at[0], right).wait_recv()
                    if which == 1:
                        sent = cells_out.at[pl.ds(0, N_DEV - 1), pl.ds(0, 8)]
                        remote(sent, sent, conv_send.at[0], conv_recv.at[0], right).wait_send()

    first = lax.broadcasted_iota(jnp.int32, (8, 128), 0) == 0

    def device(x, y):
        return x * GY + y

    total = jnp.zeros((8, 128), F32)
    for x in range(GX):
        for y in range(GY):
            for half in range(2):
                tile = cells_in[device(x, y), FIRST[half] : FIRST[half] + 8]
                if y > 0:
                    edge = cells_in[device(x, y - 1), 24 + half : 25 + half]
                    if half == 0 and x > 0:
                        edge += cells_in[device(x - 1, y - 1), 26:27]
                    tile += jnp.where(first, edge, 0.0)
                if half == 0 and x % 2 == 0 and x > 0:
                    tile += cells_in[device(x - 1, y), 0:8]
                whole[2 * x + half, 8 * y : 8 * y + 8] = tile
                total += tile

    def everything_in(value):
        return jnp.sum(jnp.sum(value, axis=1, keepdims=True), axis=0, keepdims=True)

    average = everything_in(total) * (1.0 / CELLS)

    def moment(i, carry):
        away = whole[i] - average
        return carry + jnp.sum((away * away).reshape(8, 8, 128), axis=0)

    spread = everything_in(lax.fori_loop(0, 32, moment, jnp.zeros((8, 128), F32), unroll=4)) * (1.0 / CELLS)
    inv_std = 1.0 / jnp.sqrt(spread + EPSILON)
    own_gain, own_shift = gain[0], shift[0]

    def activate(i, carry):
        s0, s1 = carry
        normed = (whole[i] - average) * inv_std
        pre = own_gain * normed + own_shift
        sig = 1.0 / (1.0 + jnp.exp(-pre))
        act_out[i] = pre * sig
        grad = cot_v[i] * sig * (1.0 + pre * (1.0 - sig))
        cot_v[i] = grad
        whole[i] = normed
        return s0 + jnp.sum(grad.reshape(8, 8, 128), axis=0), s1 + jnp.sum((grad * normed).reshape(8, 8, 128), axis=0)

    sums = lax.fori_loop(0, 32, activate, (jnp.zeros((8, 128), F32), jnp.zeros((8, 128), F32)), unroll=2)
    sum_g, sum_gn = everything_in(sums[0]), everything_in(sums[1])
    gs_out[...] = sum_g * RESCALE
    gg_out[...] = sum_gn * RESCALE
    mean_g, mean_gn = own_gain * sum_g * (1.0 / CELLS), own_gain * sum_gn * (1.0 / CELLS)

    def finish(i, carry):
        whole[i] = inv_std * (own_gain * cot_v[i] - mean_g - whole[i] * mean_gn)
        return carry

    lax.fori_loop(0, 32, finish, 0, unroll=4)
    for x in range(GX):
        for y in range(GY):
            to = device(x, y)
            tiles = pl.ds(8 * y, 8)
            for half in range(2):
                grad_out[to, FIRST[half] : FIRST[half] + 8] = whole[2 * x + half, tiles]
            if x % 2 == 1:
                grad_out[to, 0:8] = whole[2 * x + 2, tiles] if x < GX - 1 else jnp.zeros((8, 128), F32)
            for k in range(3):
                inside = y < GY - 1 and (k < 2 or x < GX - 1)
                grad_out[to, 24 + k : 25 + k] = (
                    whole[2 * x + k, 8 * y + 8 : 8 * y + 9] if inside else jnp.zeros((1, 128), F32)
                )

    grad_in[pl.ds(me, 1)] = grad_out[pl.ds(me, 1)]

    def grad_copy(part, to):
        start, rows = PARTS[part]
        src, dst = (ref.at[i, pl.ds(start, rows)] for ref, i in ((grad_out, to), (grad_in, me)))
        return remote(src, dst, grad_send.at[part], grad_recv.at[part], at(to))

    for part in (2, 1):

        def send(k, carry, part=part):
            grad_copy(part, lax.rem(me + k + core * (N_DEV - 2 * k), N_DEV)).start()
            return carry

        lax.fori_loop(2, N_DEV, send, send(1, 0), unroll=6)

    def send_next(k, carry):
        other = lax.rem(chip + k + core * (N_CHIP - 2 * k), N_CHIP)
        grad_copy(0, (2 * (other // GY) + 1) * GY + lax.rem(other, GY)).start()
        return carry

    @pl.when(core == 0)
    def _():
        send_next(0, 0)

    lax.fori_loop(1, N_CHIP, send_next, 0, unroll=7)

    def grad_wait(part):
        arrived = grad_in.at[pl.ds(0, N_DEV - 1), pl.ds(0, PARTS[part][1])]
        remote(arrived, arrived, grad_send.at[part], grad_recv.at[part], right).wait_recv()

    wide = lax.broadcasted_iota(jnp.int32, (128, 128), 1)
    grad_rows = grad_in.reshape(CO * 32, 128)

    def rows_of(mx):
        yield from ((FIRST[mx] + my, lanes_of(my)) for my in range(8))

    def place_w(mx, rows):
        for row, lanes in rows:
            high, low = high_low(grad_rows[pl.ds(row, 128, stride=32), :])
            g_w[mx, 0:128, lanes] = high
            g_w[mx, 128:256, lanes] = low

    def place_i(mx, rows):
        for row, lanes in rows:
            value = grad_rows[pl.ds(row, 128, stride=32), :]
            for k, part in enumerate((value, jnp.where(wide == 127, 0.0, pltpu.roll(value, 127, 1)))):
                high, low = high_low(part)
                g_i[mx, 128 * k : 128 * k + 128, lanes] = high
                g_i[mx, 256 + 128 * k : 384 + 128 * k, lanes] = low
                g_i[mx, 512 + 128 * k : 640 + 128 * k, lanes] = high

    def weight_terms(mx):
        x_rows, cols = operands(mx)
        for b in range(3):
            half = 0 if b == 1 else 1
            here = g_w[mx, :, slice(128, 1152) if b == 0 else slice(0, 1024)]
            both = dot_nt(x_hi[half, x_rows, :], here)
            value = both[:, :128] + both[:, 128:] + dot_nt(x_lo[half, x_rows, :], here[:128])
            for k in range(value.shape[0] // 192):
                a = cols.start // 192 + k
                into = slice(a * 576 + b * 192, a * 576 + b * 192 + 192)
                if mx == 0 or (mx == 1 and a == 0):
                    wg[into] = value[192 * k : 192 * k + 192]
                else:
                    wg[into] += value[192 * k : 192 * k + 192]

    def add_to(x, half, lanes, value, fresh):
        if fresh:
            o_acc[x, half, :, lanes] = value
        else:
            o_acc[x, half, :, lanes] += value

    def input_terms(mx):
        taps = [a for a in range(3) if 0 <= 2 * mx - 1 + a <= 3]
        top, bottom = taps[0] * 384, taps[-1] * 384 + 384

        def chunk(n, carry):
            here = pl.ds(pl.multiple_of(n * 256, 256), 256)
            first = pl.ds(pl.multiple_of(n * 256, 256), 128)
            second = pl.ds(pl.multiple_of(n * 256 + 128, 128), 128)
            terms = dot(wb[top:bottom, :], g_i[mx, :, here])
            for a in taps:
                x = 2 * mx - 1 + a
                block = terms[a * 384 - top : a * 384 - top + 384]
                add_to(x, 0, here, block[128:256], a > 0)
                add_to(x, 1, first, block[256:384, :128] + block[0:128, 128:], a > 0)
                add_to(x, 1, second, block[256:384, 128:], a > 0)

                @pl.when(n > 0)
                def _(x=x, block=block):
                    before = pl.ds(pl.multiple_of(n * 256 - 128, 128), 128)
                    o_acc[x, 1, :, before] += block[0:128, :128]

            return carry

        lax.fori_loop(0, 4, chunk, 0)

    def input_terms_rim(mx):
        for a in range(3):
            x = 2 * mx - 1 + a
            if 0 <= x <= 3:
                value = dot(wb[a * 384 : a * 384 + 128, :], g_i[mx, :, 1024:1152])
                o_acc[x, 1, :, 896:1024] += value

    def merge(x):
        slot = x % 2
        if x >= 2:
            for copy in copies[2 * (x - 2) : 2 * (x - 2) + 2]:
                copy.wait()
        for half in range(2):
            blocks = [
                jnp.concatenate([o_acc[x, half, 0:64, lanes_of(my)], o_acc[x, half, 64:128, lanes_of(my)]], axis=1)
                for my in range(8)
            ]
            high, low = high_low(jnp.concatenate(blocks, axis=0))
            merged = dot(high, merge_z) + dot(low, merge_z)
            for my in range(8):
                for z in range(2):
                    out_v[slot, z, pl.ds(2 * my + half, 64, stride=16), :] = merged[
                        64 * my : 64 * my + 64, 128 * z : 128 * z + 128
                    ]
        for z in range(2):
            copy = pltpu.make_async_copy(
                out_v.at[slot, z].reshape(CI, 16, 128),
                gin_out.at[:, x, :, pl.ds(128 * z, 128)],
                out_sem.at[slot, z],
            )
            copy.start()
            copies.append(copy)

    def start_pair(group):
        first, size = GROUPS[group]
        there = wg.at[pl.ds(pl.multiple_of(first + (1 - core) * size, 16), size)]
        copy = remote(there, wg_pair.at[pl.ds(HALVES[group], size)], pair_send.at[group], pair_recv.at[group], pair_device)
        copy.start()
        return copy

    def chip_device(index):
        return (2 * (index // GY) + core, lax.rem(index, GY))

    def slice_of(index):
        return pl.ds(pl.multiple_of(index * 16, 16), 16)

    def share_out(group, copy):
        first, size = GROUPS[group]
        copy.wait()
        here = wg[pl.ds(pl.multiple_of(first + core * size, 16), size)]
        half = slice(HALVES[group], HALVES[group] + size)
        wg_half[half] = here + wg_pair[half]
        low, count = HALVES[group] // 16, size // 16

        def send(k, carry):
            to = low + lax.rem(chip + k + core * (count - 2 * k), count)

            @pl.when(to != chip)
            def _():
                remote(wg_half.at[slice_of(to)], wg_in.at[chip], wr_send, wr_recv, chip_device(to)).start()

            return carry

        lax.fori_loop(0, count, send, 0, unroll=6)

    copies = []
    grad_wait(2)
    from_pair = remote(grad_in.at[:, pl.ds(16, 8)], grad_in.at[:, pl.ds(0, 8)], pair_send.at[5], pair_recv.at[5], pair_device)

    @pl.when(core == 1)
    def _():
        from_pair.start()

    by_y = [(24 + mx, lanes_of(8)) for mx in range(3)]
    place_w(0, rows_of(0))
    for mx in range(3):
        place_w(mx, by_y[mx : mx + 1])
    weight_terms(0)
    for mx in range(3):
        place_i(mx, by_y[mx : mx + 1])
    place_i(0, rows_of(0))
    input_terms(0)
    input_terms_rim(0)
    grad_wait(1)
    place_w(1, rows_of(1))
    weight_terms(1)
    pair_0 = start_pair(0)
    @pl.when(core == 0)
    def _():
        from_pair.wait_recv()

    @pl.when(core == 1)
    def _():
        grad_wait(0)

    place_w(2, rows_of(2))
    weight_terms(2)
    pair_1 = start_pair(1)
    share_out(0, pair_0)
    share_out(1, pair_1)
    place_i(1, rows_of(1))
    input_terms(1)
    input_terms_rim(1)
    place_i(2, rows_of(2))
    input_terms(2)
    input_terms_rim(2)
    own_slice = pl.ds(pl.multiple_of(chip * 16 + jnp.where(chip < CUT, 576 + core * 576, core * 288 - 576), 16), 16)

    @pl.when(chip < OWNERS)
    def _():
        wg_in[pl.ds(chip, 1)] = wg_half[slice_of(chip)][None]
        everyone = wg_in.at[pl.ds(0, N_CHIP - 1)]
        remote(everyone, everyone, wr_send, wr_recv, right).wait_recv()
        gw_out[own_slice] = jnp.sum(wg_in[...], axis=0) * RESCALE

    for group in range(2):

        @pl.when((chip < CUT) if group == 0 else (chip >= CUT) & (chip < OWNERS))
        def _(group=group):
            def send_slice(k, carry):
                src = gw_out.at[own_slice]
                to = chip_device(lax.rem(chip + k + core * (N_CHIP - 2 * k), N_CHIP))
                remote(src, src, wa_send, wa_recv.at[group], to).start()
                return carry

            lax.fori_loop(1, N_CHIP, send_slice, 0, unroll=7)

    for x in range(4):
        merge(x)
    @pl.when(chip < OWNERS)
    def _():
        some = wg_half.at[pl.ds(0, 16 * (OWNERS - 1))]
        remote(some, some, wr_send, wr_recv, right).wait_send()
        everyone = wg_in.at[pl.ds(0, N_CHIP - 1)]
        remote(everyone, everyone, wa_send, wa_recv.at[0], right).wait_send()

    @pl.when(chip >= OWNERS)
    def _():
        remote(wg_half, wg_half, wr_send, wr_recv, right).wait_send()

    last = []
    for group, (low, high) in enumerate(((0, CUT), (CUT, OWNERS))):
        inside = (chip >= low) & (chip < high)
        for missing in range(2):

            @pl.when(inside if missing else jnp.logical_not(inside))
            def _(group=group, rows=(high - low - missing) * 16):
                some = gw_out.at[pl.ds(0, rows)]
                remote(some, some, wa_send, wa_recv.at[group], right).wait_recv()

        first, size = GROUPS[group]
        done = gw_out.at[pl.ds(pl.multiple_of(first + core * size, 16), size)]
        last.append(remote(done, done, pair_send.at[2 + group], pair_recv.at[2 + group], pair_device))
        last[-1].start()
    for copy in last:
        copy.wait()
    for part in (2, 1):
        sent = grad_out.at[pl.ds(0, N_DEV - 1), pl.ds(0, PARTS[part][1])]
        remote(sent, sent, grad_send.at[part], grad_recv.at[part], right).wait_send()
    for which in range(2):

        @pl.when(core == which)
        def _(which=which):
            sent = grad_out.at[pl.ds(0, N_CHIP - which), pl.ds(0, 8)]
            remote(sent, sent, grad_send.at[0], grad_recv.at[0], right).wait_send()
            if which == 1:
                from_pair.wait_send()

    for copy in copies[4:]:
        copy.wait()


def hand_over(*refs):
    copies = []
    for source, target, pieces in zip(refs[:3], refs[3:6], (2, 8, 1)):
        size = source.shape[0] // pieces
        for piece in range(pieces):
            here = pl.ds(piece * size, size)
            copies.append(pltpu.make_async_copy(source.at[here], target.at[here], refs[6].at[len(copies)]))
    for copy in copies:
        copy.start()
    for copy in copies:
        copy.wait()


def local(fine_input, weights, norm_gain, norm_shift, cotangent):
    any_space = pl.BlockSpec(memory_space=pl.ANY)
    vmem = pl.BlockSpec(memory_space=pltpu.VMEM)
    smem = pl.BlockSpec(memory_space=pltpu.SMEM)
    dma = pltpu.SemaphoreType.DMA
    activated, grad_input, grad_weights, grad_gain, grad_shift = pl.pallas_call(
        kernel,
        out_shape=(
            pltpu.VMEM((32, 64, 128), F32),
            pltpu.VMEM((CI, 4, 16, 256), F32),
            pltpu.VMEM((27 * CI, CO), F32),
            jax.ShapeDtypeStruct((1, 1), F32),
            jax.ShapeDtypeStruct((1, 1), F32),
        ),
        in_specs=[any_space, any_space, smem, smem, any_space],
        out_specs=(vmem,) * 5,
        scratch_shapes=[
            pltpu.VMEM((4, CI, 16, 256), F32),
            pltpu.VMEM((27, CI, CO), F32),
            pltpu.VMEM((32, 64, 128), F32),
            pltpu.VMEM((2, 768, 1024), BF16),
            pltpu.VMEM((2, 768, 1024), BF16),
            pltpu.VMEM((1024, 128), F32),
            pltpu.VMEM((1024, 128), F32),
            pltpu.VMEM((256, 576), BF16),
            pltpu.VMEM((512, 576), BF16),
            pltpu.VMEM((1152, 768), BF16),
            pltpu.VMEM((3, CO, 1152), F32),
            pltpu.VMEM((CO, 1024), F32),
            pltpu.VMEM((N_DEV, 32, 128), F32),
            pltpu.VMEM((N_DEV, 32, 128), F32),
            pltpu.VMEM((32, 64, 128), F32),
            pltpu.VMEM((N_DEV, 32, 128), F32),
            pltpu.VMEM((N_DEV, 32, 128), F32),
            pltpu.VMEM((3, 256, 1152), BF16),
            pltpu.VMEM((3, 768, 1152), BF16),
            pltpu.VMEM((4, 2, 128, 1024), F32),
            pltpu.VMEM((2, 2, 1024, 128), F32),
            pltpu.VMEM((27 * CI, 128), F32),
            pltpu.VMEM((HALF, 128), F32),
            pltpu.VMEM((HALF, 128), F32),
            pltpu.VMEM((N_CHIP, 16, 128), F32),
            dma((8,)),
            dma((2, 2)),
            dma((3,)),
            dma((3,)),
            dma((3,)),
            dma((3,)),
            dma,
            dma,
            dma,
            dma((2,)),
            dma((6,)),
            dma((6,)),
            pltpu.SemaphoreType.REGULAR,
        ],
        compiler_params=pltpu.CompilerParams(
            collective_id=0, has_side_effects=True, vmem_limit_bytes=50 << 20
        ),
    )(fine_input, weights.transpose(0, 2, 1), norm_gain, norm_shift, cotangent)
    activated, grad_input, grad_weights = pl.pallas_call(
        hand_over,
        out_shape=tuple(jax.ShapeDtypeStruct(v.shape, F32) for v in (activated, grad_input, grad_weights)),
        in_specs=[any_space] * 3,
        out_specs=(any_space,) * 3,
        scratch_shapes=[dma((11,))],
        compiler_params=pltpu.CompilerParams(vmem_limit_bytes=1 << 20),
    )(activated, grad_input, grad_weights)
    activated, grad_weights = activated[None], grad_weights.reshape(27, CI, CO).transpose(0, 2, 1)
    return activated, grad_input, grad_weights, grad_gain.reshape(1), grad_shift.reshape(1)


def solution(mesh):
    placed = (
        P(None, "gx", "gy", None),
        P(),
        P(("gx", "gy")),
        P(("gx", "gy")),
        P(("gx", "gy"), None, None, None),
    )
    return jax.shard_map(
        local,
        mesh=mesh,
        in_specs=placed,
        out_specs=(
            P(("gx", "gy"), None, None, None),
            P(None, "gx", "gy", None),
            P(),
            P(("gx", "gy")),
            P(("gx", "gy")),
        ),
        check_vma=False,
    )
```

```python
import functools
import math

import jax
import jax.numpy as jnp
from jax import lax
from jax.experimental import pallas as pl
from jax.experimental.pallas import tpu as pltpu
from jax.sharding import PartitionSpec as P

MESH = pl.DeviceIdType.MESH
F32 = jnp.float32
BF16 = jnp.bfloat16
GX, GY, N_DEV = 16, 8, 128
CI, CO = 64, 128
CELLS = 32 * 64 * 128
RESCALE = 1.0 / math.sqrt(CELLS)
EPSILON = 1e-5
N_CHIP = N_DEV // 2
HALF = 27 * CI // 2
OWNERS = HALF // 16
FIRST = (16, 8, 0)
PARTS = ((0, 8), (8, 8), (16, 11))
GROUPS = ((576, 576), (0, 288))
HALVES = (0, 576)
CUT = 36


def dot(a, b):
    return jnp.dot(a, b, preferred_element_type=F32)


def dot_nt(a, b):
    return lax.dot_general(a, b, (((1,), (1,)), ((), ())), preferred_element_type=F32)


def high_low(value):
    high = value.astype(BF16)
    return high, (value - high.astype(F32)).astype(BF16)


def kernel(
    fine, wts, gain, shift, cot, act_out, gin_out, gw_out, gg_out, gs_out,
    fine_v, w_v, cot_v, x_hi, x_lo, even_t, odd_t, wf_e, wf_o, wb,
    conv, pair_x, cells_out, cells_in, whole, grad_out, grad_in, g_w, g_i, o_acc, out_v,
    wg, wg_pair, wg_half, wg_in,
    local_sem, out_sem, conv_send, conv_recv, grad_send, grad_recv, wr_send, wr_recv, wa_send, wa_recv,
    pair_send, pair_recv, row_sem,
):
    gx, gy = lax.axis_index("gx"), lax.axis_index("gy")
    me = gx * GY + gy
    core, chip = lax.rem(gx, 2), (gx // 2) * GY + gy
    pair_device = (gx + 1 - 2 * core, gy)
    right = (lax.rem(gx + 1, GX), gy)

    def at(lin):
        return (lin // GY, lax.rem(lin, GY))

    def remote(src, dst, send, recv, device):
        return pltpu.make_async_remote_copy(
            src_ref=src, dst_ref=dst, send_sem=send, recv_sem=recv,
            device_id=device, device_id_type=MESH,
        )

    fine_in = [
        pltpu.make_async_copy(fine.at[:, x], fine_v.at[x], local_sem.at[x]) for x in (3, 2, 1, 0)
    ]
    w_in = pltpu.make_async_copy(wts, w_v, local_sem.at[4])
    cot_in = pltpu.make_async_copy(cot.at[0], cot_v, local_sem.at[5])
    for copy in (w_in, *fine_in, cot_in):
        copy.start()

    barrier = pltpu.get_barrier_semaphore()

    def greet(sem, sizes):
        for count, device in zip(sizes, (lambda k: (lax.rem(gx + k, GX), gy), lambda k: (gx, lax.rem(gy + k, GY)))):

            def one(k, carry, device=device):
                pl.semaphore_signal(sem, inc=1, device_id=device(k), device_id_type=MESH)
                return carry

            lax.fori_loop(1, count, one, 0)

    greet(barrier, (GX, GY))

    row = lax.broadcasted_iota(jnp.int32, (256, 256), 0)
    col = lax.broadcasted_iota(jnp.int32, (256, 256), 1)
    split = jnp.where(
        row == jnp.where(col < 128, 2 * col, 2 * (col - 128) + 1), 1.0, 0.0
    ).astype(BF16)
    merge_z = jnp.where(
        col == jnp.where(row < 128, 2 * row, 2 * (row - 128) + 1), 1.0, 0.0
    ).astype(BF16)
    lane = lax.broadcasted_iota(jnp.int32, (64, 128), 1)

    w_in.wait()
    for b in range(3):
        flat = jnp.concatenate([w_v[(a * 3 + b) * 3 + c] for a in range(3) for c in range(3)], axis=0)
        high, low = high_low(flat.T)
        if b == 1:
            wf_e[0:128], wf_e[128:256] = high, low
        else:
            at_row = 0 if b == 2 else 128
            wf_o[at_row : at_row + 128] = high
            wf_o[256 + at_row : 384 + at_row] = low

    def split_slab(x):
        high, low = high_low(fine_v[x].reshape(CI * 16, 256))
        for part, dst in ((high, x_hi), (low, x_lo)):
            both = dot(part, split)
            even_t[0:1024] = both[:, :128]
            odd_t[0:1024] = both[:, 128:]
            for y in range(16):
                half, lanes = y % 2, slice(y // 2 * 128, y // 2 * 128 + 128)
                even = even_t[pl.ds(y, CI, stride=16), :]
                odd = odd_t[pl.ds(y, CI, stride=16), :]
                before = jnp.where(lane == 0, 0.0, pltpu.roll(odd, 1, 1))
                for c, value in enumerate((before, even, odd)):
                    rows = slice(x * 192 + c * 64, x * 192 + c * 64 + 64)
                    dst[half, rows, lanes] = value.astype(BF16)

    def operands(mx):
        x0, x1 = ((0, 2), (1, 4), (3, 4))[mx]
        a0 = (1, 0, 0)[mx]
        depth = (x1 - x0) * 192
        return slice(x0 * 192, x1 * 192), slice(a0 * 192, a0 * 192 + depth)

    def forward_rim(mx):
        rows, cols = operands(mx)
        value = dot(wf_o[:, cols], x_hi[1, rows, 896:1024])
        return value[128:256] + value[384:512] + dot(wf_o[128:256, cols], x_lo[1, rows, 896:1024])

    def forward(mx):
        rows, cols = operands(mx)
        target = conv.at[mx]
        target[:, 0:128] = jnp.zeros((CO, 128), F32)

        def chunk(n, carry):
            here = pl.ds(pl.multiple_of(n * 256, 256), 256)
            e_hi, e_lo = x_hi[0, rows, here], x_lo[0, rows, here]
            o_hi, o_lo = x_hi[1, rows, here], x_lo[1, rows, here]
            e = dot(wf_e[:, cols], e_hi)
            e = e[:128] + e[128:] + dot(wf_e[0:128, cols], e_lo)
            o = dot(wf_o[:, cols], o_hi)
            o = o[:256] + o[256:] + dot(wf_o[0:256, cols], o_lo)
            e = e + o[:128]
            target[:, pl.ds(pl.multiple_of(n * 256, 256), 128)] += e[:, :128]
            target[:, pl.ds(pl.multiple_of(n * 256 + 128, 128), 128)] = e[:, 128:] + o[128:, :128]

            target[:, pl.ds(pl.multiple_of(n * 256 + 256, 256), 128)] = o[128:, 128:]
            return carry

        lax.fori_loop(0, 4, chunk, 0)

    out_rows = cells_out.reshape((CO + 1) * 32, 128)

    def lanes_of(my):
        return slice(my * 128, my * 128 + 128)

    def store_rows(mx):
        for my in range(8):
            out_rows[pl.ds(FIRST[mx] + my, 128, stride=32), :] = conv[mx, :, lanes_of(my)]
        out_rows[pl.ds(24 + mx, 128, stride=32), :] = conv[mx, :, lanes_of(8)]

    def send_cells(part):
        start, rows = PARTS[part]

        def send(k, carry):
            to = lax.rem(me + k + core * (N_DEV - 2 * k), N_DEV)
            src, dst = (ref.at[i, pl.ds(start, rows)] for ref, i in ((cells_out, to), (cells_in, me)))
            remote(src, dst, conv_send.at[part], conv_recv.at[part], at(to)).start()
            return carry

        lax.fori_loop(2, N_DEV, send, send(1, 0), unroll=6)

    fine_in[0].wait()
    split_slab(3)
    pl.semaphore_wait(barrier, GX + GY - 2)
    greet(row_sem, (GX,))
    forward(2)
    store_rows(2)
    pl.semaphore_wait(row_sem, GX - 1)
    to_pair = remote(conv.at[2, :, pl.ds(0, 1024)], pair_x, pair_send.at[4], pair_recv.at[4], pair_device)

    @pl.when(core == 0)
    def _():
        to_pair.start()

    @pl.when(core == 1)
    def _():
        send_cells(0)

    for i, x in ((1, 2), (2, 1)):
        fine_in[i].wait()
        split_slab(x)
    forward(1)
    store_rows(1)
    send_cells(1)
    fine_in[3].wait()
    split_slab(0)
    forward(0)

    @pl.when(core == 0)
    def _():
        to_pair.wait_send()

    @pl.when(core == 1)
    def _():
        to_pair.wait_recv()
        conv[0, :, 0:1024] += pair_x[...]

    store_rows(0)
    send_cells(2)
    cells_in[pl.ds(me, 1)] = cells_out[pl.ds(me, 1)]

    for tap in range(9):
        turned = [w_v[tap * 3 + c] for c in range(3)]
        for half, (now, later) in enumerate(((turned[1], None), (turned[2], turned[0]))):
            rows = slice(tap * 128 + half * 64, tap * 128 + half * 64 + 64)
            for k, block in enumerate((now, later)):
                if block is None:
                    high = low = jnp.zeros((64, 128), BF16)
                else:
                    high, low = high_low(block)
                wb[rows, k * 128 : k * 128 + 128] = high
                wb[rows, 256 + k * 128 : 384 + k * 128] = high
                wb[rows, 512 + k * 128 : 640 + k * 128] = low

    cot_in.wait()
    for part, (start, rows) in enumerate(PARTS):
        if part > 0:
            moved = cells_out.at[pl.ds(0, N_DEV - 1), pl.ds(0, rows)]
            remote(moved, moved, conv_send.at[part], conv_recv.at[part], right).wait()
        else:
            for which in range(2):

                @pl.when(core == which)
                def _(which=which):
                    arrived = cells_in.at[pl.ds(0, N_CHIP - which), pl.ds(0, 8)]
                    remote(arrived, arrived, conv_send.at[0], conv_recv.at[0], right).wait_recv()
                    if which == 1:
                        sent = cells_out.at[pl.ds(0, N_DEV - 1), pl.ds(0, 8)]
                        remote(sent, sent, conv_send.at[0], conv_recv.at[0], right).wait_send()

    first = lax.broadcasted_iota(jnp.int32, (8, 128), 0) == 0

    def device(x, y):
        return x * GY + y

    total = jnp.zeros((8, 128), F32)
    for x in range(GX):
        for y in range(GY):
            for half in range(2):
                tile = cells_in[device(x, y), FIRST[half] : FIRST[half] + 8]
                if y > 0:
                    edge = cells_in[device(x, y - 1), 24 + half : 25 + half]
                    if half == 0 and x > 0:
                        edge += cells_in[device(x - 1, y - 1), 26:27]
                    tile += jnp.where(first, edge, 0.0)
                if half == 0 and x % 2 == 0 and x > 0:
                    tile += cells_in[device(x - 1, y), 0:8]
                whole[2 * x + half, 8 * y : 8 * y + 8] = tile
                total += tile

    def everything_in(value):
        return jnp.sum(jnp.sum(value, axis=1, keepdims=True), axis=0, keepdims=True)

    average = everything_in(total) * (1.0 / CELLS)

    def moment(i, carry):
        away = whole[i] - average
        return carry + jnp.sum((away * away).reshape(8, 8, 128), axis=0)

    spread = everything_in(lax.fori_loop(0, 32, moment, jnp.zeros((8, 128), F32), unroll=4)) * (1.0 / CELLS)
    inv_std = 1.0 / jnp.sqrt(spread + EPSILON)
    own_gain, own_shift = gain[0], shift[0]

    def activate(i, carry):
        s0, s1 = carry
        normed = (whole[i] - average) * inv_std
        pre = own_gain * normed + own_shift
        sig = 1.0 / (1.0 + jnp.exp(-pre))
        act_out[i] = pre * sig
        grad = cot_v[i] * sig * (1.0 + pre * (1.0 - sig))
        cot_v[i] = grad
        whole[i] = normed
        return s0 + jnp.sum(grad.reshape(8, 8, 128), axis=0), s1 + jnp.sum((grad * normed).reshape(8, 8, 128), axis=0)

    sums = lax.fori_loop(0, 32, activate, (jnp.zeros((8, 128), F32), jnp.zeros((8, 128), F32)), unroll=2)
    sum_g, sum_gn = everything_in(sums[0]), everything_in(sums[1])
    gs_out[...] = sum_g * RESCALE
    gg_out[...] = sum_gn * RESCALE
    mean_g, mean_gn = own_gain * sum_g * (1.0 / CELLS), own_gain * sum_gn * (1.0 / CELLS)

    def finish(i, carry):
        whole[i] = inv_std * (own_gain * cot_v[i] - mean_g - whole[i] * mean_gn)
        return carry

    lax.fori_loop(0, 32, finish, 0, unroll=4)
    for x in range(GX):
        for y in range(GY):
            to = device(x, y)
            tiles = pl.ds(8 * y, 8)
            for half in range(2):
                grad_out[to, FIRST[half] : FIRST[half] + 8] = whole[2 * x + half, tiles]
            if x % 2 == 1:
                grad_out[to, 0:8] = whole[2 * x + 2, tiles] if x < GX - 1 else jnp.zeros((8, 128), F32)
            for k in range(3):
                inside = y < GY - 1 and (k < 2 or x < GX - 1)
                grad_out[to, 24 + k : 25 + k] = (
                    whole[2 * x + k, 8 * y + 8 : 8 * y + 9] if inside else jnp.zeros((1, 128), F32)
                )

    grad_in[pl.ds(me, 1)] = grad_out[pl.ds(me, 1)]

    def grad_copy(part, to):
        start, rows = PARTS[part]
        src, dst = (ref.at[i, pl.ds(start, rows)] for ref, i in ((grad_out, to), (grad_in, me)))
        return remote(src, dst, grad_send.at[part], grad_recv.at[part], at(to))

    for part in (2, 1):

        def send(k, carry, part=part):
            grad_copy(part, lax.rem(me + k + core * (N_DEV - 2 * k), N_DEV)).start()
            return carry

        lax.fori_loop(2, N_DEV, send, send(1, 0), unroll=6)

    def send_next(k, carry):
        other = lax.rem(chip + k + core * (N_CHIP - 2 * k), N_CHIP)
        grad_copy(0, (2 * (other // GY) + 1) * GY + lax.rem(other, GY)).start()
        return carry

    @pl.when(core == 0)
    def _():
        send_next(0, 0)

    lax.fori_loop(1, N_CHIP, send_next, 0, unroll=7)

    def grad_wait(part):
        arrived = grad_in.at[pl.ds(0, N_DEV - 1), pl.ds(0, PARTS[part][1])]
        remote(arrived, arrived, grad_send.at[part], grad_recv.at[part], right).wait_recv()

    wide = lax.broadcasted_iota(jnp.int32, (128, 128), 1)
    grad_rows = grad_in.reshape((CO + 1) * 32, 128)

    def rows_of(mx):
        yield from ((FIRST[mx] + my, lanes_of(my)) for my in range(8))

    def place_w(mx, rows):
        for row, lanes in rows:
            high, low = high_low(grad_rows[pl.ds(row, 128, stride=32), :])
            g_w[mx, 0:128, lanes] = high
            g_w[mx, 128:256, lanes] = low

    def place_i(mx, rows):
        for row, lanes in rows:
            value = grad_rows[pl.ds(row, 128, stride=32), :]
            for k, part in enumerate((value, jnp.where(wide == 127, 0.0, pltpu.roll(value, 127, 1)))):
                high, low = high_low(part)
                g_i[mx, 128 * k : 128 * k + 128, lanes] = high
                g_i[mx, 256 + 128 * k : 384 + 128 * k, lanes] = low
                g_i[mx, 512 + 128 * k : 640 + 128 * k, lanes] = high

    def weight_terms(mx):
        x_rows, cols = operands(mx)
        for b in range(3):
            half = 0 if b == 1 else 1
            here = g_w[mx, :, slice(128, 1152) if b == 0 else slice(0, 1024)]
            both = dot_nt(x_hi[half, x_rows, :], here)
            value = both[:, :128] + both[:, 128:] + dot_nt(x_lo[half, x_rows, :], here[:128])
            for k in range(value.shape[0] // 192):
                a = cols.start // 192 + k
                into = slice(a * 576 + b * 192, a * 576 + b * 192 + 192)
                if mx == 0 or (mx == 1 and a == 0):
                    wg[into] = value[192 * k : 192 * k + 192]
                else:
                    wg[into] += value[192 * k : 192 * k + 192]

    def add_to(x, half, lanes, value, fresh):
        if fresh:
            o_acc[x, half, :, lanes] = value
        else:
            o_acc[x, half, :, lanes] += value

    def input_terms(mx):
        taps = [a for a in range(3) if 0 <= 2 * mx - 1 + a <= 3]
        top, bottom = taps[0] * 384, taps[-1] * 384 + 384

        def chunk(n, carry):
            here = pl.ds(pl.multiple_of(n * 256, 256), 256)
            first = pl.ds(pl.multiple_of(n * 256, 256), 128)
            second = pl.ds(pl.multiple_of(n * 256 + 128, 128), 128)
            terms = dot(wb[top:bottom, :], g_i[mx, :, here])
            for a in taps:
                x = 2 * mx - 1 + a
                block = terms[a * 384 - top : a * 384 - top + 384]
                add_to(x, 0, here, block[128:256], a > 0)
                add_to(x, 1, first, block[256:384, :128] + block[0:128, 128:], a > 0)
                add_to(x, 1, second, block[256:384, 128:], a > 0)

                @pl.when(n > 0)
                def _(x=x, block=block):
                    before = pl.ds(pl.multiple_of(n * 256 - 128, 128), 128)
                    o_acc[x, 1, :, before] += block[0:128, :128]

            return carry

        lax.fori_loop(0, 4, chunk, 0)

    def input_terms_rim(mx):
        for a in range(3):
            x = 2 * mx - 1 + a
            if 0 <= x <= 3:
                value = dot(wb[a * 384 : a * 384 + 128, :], g_i[mx, :, 1024:1152])
                o_acc[x, 1, :, 896:1024] += value

    def merge(x):
        slot = x % 2
        if x >= 2:
            for copy in copies[2 * (x - 2) : 2 * (x - 2) + 2]:
                copy.wait()
        for half in range(2):
            blocks = [
                jnp.concatenate([o_acc[x, half, 0:64, lanes_of(my)], o_acc[x, half, 64:128, lanes_of(my)]], axis=1)
                for my in range(8)
            ]
            high, low = high_low(jnp.concatenate(blocks, axis=0))
            merged = dot(high, merge_z) + dot(low, merge_z)
            for my in range(8):
                for z in range(2):
                    out_v[slot, z, pl.ds(2 * my + half, 64, stride=16), :] = merged[
                        64 * my : 64 * my + 64, 128 * z : 128 * z + 128
                    ]
        for z in range(2):
            copy = pltpu.make_async_copy(
                out_v.at[slot, z, pl.ds(0, 1024)].reshape(CI, 16, 128),
                gin_out.at[:, x, :, pl.ds(128 * z, 128)],
                out_sem.at[slot, z],
            )
            copy.start()
            copies.append(copy)

    def start_pair(group):
        first, size = GROUPS[group]
        there = wg.at[pl.ds(pl.multiple_of(first + (1 - core) * size, 16), size)]
        copy = remote(there, wg_pair.at[pl.ds(HALVES[group], size)], pair_send.at[group], pair_recv.at[group], pair_device)
        copy.start()
        return copy

    def chip_device(index):
        return (2 * (index // GY) + core, lax.rem(index, GY))

    def slice_of(index):
        return pl.ds(pl.multiple_of(index * 16, 16), 16)

    def share_out(group, copy):
        first, size = GROUPS[group]
        copy.wait()
        here = wg[pl.ds(pl.multiple_of(first + core * size, 16), size)]
        half = slice(HALVES[group], HALVES[group] + size)
        wg_half[half] = here + wg_pair[half]
        low, count = HALVES[group] // 16, size // 16

        def send(k, carry):
            to = low + lax.rem(chip + k + core * (count - 2 * k), count)

            @pl.when(to != chip)
            def _():
                remote(wg_half.at[slice_of(to)], wg_in.at[chip], wr_send, wr_recv, chip_device(to)).start()

            return carry

        lax.fori_loop(0, count, send, 0, unroll=6)

    copies = []
    grad_wait(2)
    from_pair = remote(grad_in.at[pl.ds(0, CO), pl.ds(16, 8)], grad_in.at[pl.ds(0, CO), pl.ds(0, 8)], pair_send.at[5], pair_recv.at[5], pair_device)

    @pl.when(core == 1)
    def _():
        from_pair.start()

    by_y = [(24 + mx, lanes_of(8)) for mx in range(3)]
    place_w(0, rows_of(0))
    for mx in range(3):
        place_w(mx, by_y[mx : mx + 1])
    weight_terms(0)
    for mx in range(3):
        place_i(mx, by_y[mx : mx + 1])
    place_i(0, rows_of(0))
    input_terms(0)
    input_terms_rim(0)
    grad_wait(1)
    place_w(1, rows_of(1))
    weight_terms(1)
    pair_0 = start_pair(0)
    @pl.when(core == 0)
    def _():
        from_pair.wait_recv()

    @pl.when(core == 1)
    def _():
        grad_wait(0)

    place_w(2, rows_of(2))
    weight_terms(2)
    pair_1 = start_pair(1)
    share_out(0, pair_0)
    share_out(1, pair_1)
    place_i(1, rows_of(1))
    input_terms(1)
    input_terms_rim(1)
    place_i(2, rows_of(2))
    input_terms(2)
    input_terms_rim(2)
    own_slice = pl.ds(pl.multiple_of(chip * 16 + jnp.where(chip < CUT, 576 + core * 576, core * 288 - 576), 16), 16)

    @pl.when(chip < OWNERS)
    def _():
        wg_in[pl.ds(chip, 1)] = wg_half[slice_of(chip)][None]
        everyone = wg_in.at[pl.ds(0, N_CHIP - 1)]
        remote(everyone, everyone, wr_send, wr_recv, right).wait_recv()
        gw_out[own_slice] = jnp.sum(wg_in[...], axis=0) * RESCALE

    for group in range(2):

        @pl.when((chip < CUT) if group == 0 else (chip >= CUT) & (chip < OWNERS))
        def _(group=group):
            def send_slice(k, carry):
                src = gw_out.at[own_slice]
                to = chip_device(lax.rem(chip + k + core * (N_CHIP - 2 * k), N_CHIP))
                remote(src, src, wa_send, wa_recv.at[group], to).start()
                return carry

            lax.fori_loop(1, N_CHIP, send_slice, 0, unroll=7)

    for x in range(4):
        merge(x)
    @pl.when(chip < OWNERS)
    def _():
        some = wg_half.at[pl.ds(0, 16 * (OWNERS - 1))]
        remote(some, some, wr_send, wr_recv, right).wait_send()
        everyone = wg_in.at[pl.ds(0, N_CHIP - 1)]
        remote(everyone, everyone, wa_send, wa_recv.at[0], right).wait_send()

    @pl.when(chip >= OWNERS)
    def _():
        remote(wg_half, wg_half, wr_send, wr_recv, right).wait_send()

    last = []
    for group, (low, high) in enumerate(((0, CUT), (CUT, OWNERS))):
        inside = (chip >= low) & (chip < high)
        for missing in range(2):

            @pl.when(inside if missing else jnp.logical_not(inside))
            def _(group=group, rows=(high - low - missing) * 16):
                some = gw_out.at[pl.ds(0, rows)]
                remote(some, some, wa_send, wa_recv.at[group], right).wait_recv()

        first, size = GROUPS[group]
        done = gw_out.at[pl.ds(pl.multiple_of(first + core * size, 16), size)]
        last.append(remote(done, done, pair_send.at[2 + group], pair_recv.at[2 + group], pair_device))
        last[-1].start()
    for copy in last:
        copy.wait()
    for part in (2, 1):
        sent = grad_out.at[pl.ds(0, N_DEV - 1), pl.ds(0, PARTS[part][1])]
        remote(sent, sent, grad_send.at[part], grad_recv.at[part], right).wait_send()
    for which in range(2):

        @pl.when(core == which)
        def _(which=which):
            sent = grad_out.at[pl.ds(0, N_CHIP - which), pl.ds(0, 8)]
            remote(sent, sent, grad_send.at[0], grad_recv.at[0], right).wait_send()
            if which == 1:
                from_pair.wait_send()

    for copy in copies[4:]:
        copy.wait()


def hand_over(*refs):
    copies = []
    for source, target, pieces in zip(refs[:3], refs[3:6], (2, 8, 1)):
        size = source.shape[0] // pieces
        for piece in range(pieces):
            here = pl.ds(piece * size, size)
            copies.append(pltpu.make_async_copy(source.at[here], target.at[here], refs[6].at[len(copies)]))
    for copy in copies:
        copy.start()
    for copy in copies:
        copy.wait()


def local(fine_input, weights, norm_gain, norm_shift, cotangent):
    any_space = pl.BlockSpec(memory_space=pl.ANY)
    vmem = pl.BlockSpec(memory_space=pltpu.VMEM)
    smem = pl.BlockSpec(memory_space=pltpu.SMEM)
    dma = pltpu.SemaphoreType.DMA
    activated, grad_input, grad_weights, grad_gain, grad_shift = pl.pallas_call(
        kernel,
        out_shape=(
            pltpu.VMEM((32, 64, 128), F32),
            pltpu.VMEM((CI, 4, 16, 256), F32),
            pltpu.VMEM((27 * CI, CO), F32),
            jax.ShapeDtypeStruct((1, 1), F32),
            jax.ShapeDtypeStruct((1, 1), F32),
        ),
        in_specs=[any_space, any_space, smem, smem, any_space],
        out_specs=(vmem,) * 5,
        scratch_shapes=[
            pltpu.VMEM((4, CI, 16, 256), F32),
            pltpu.VMEM((27, CI, CO), F32),
            pltpu.VMEM((32, 64, 128), F32),
            pltpu.VMEM((2, 768, 1024), BF16),
            pltpu.VMEM((2, 768, 1024), BF16),
            pltpu.VMEM((1040, 128), F32),
            pltpu.VMEM((1040, 128), F32),
            pltpu.VMEM((256, 576), BF16),
            pltpu.VMEM((512, 576), BF16),
            pltpu.VMEM((1152, 768), BF16),
            pltpu.VMEM((3, CO, 1152), F32),
            pltpu.VMEM((CO, 1024), F32),
            pltpu.VMEM((N_DEV + 1, 32, 128), F32),
            pltpu.VMEM((N_DEV, 32, 128), F32),
            pltpu.VMEM((32, 64, 128), F32),
            pltpu.VMEM((N_DEV, 32, 128), F32),
            pltpu.VMEM((N_DEV + 1, 32, 128), F32),
            pltpu.VMEM((3, 256, 1152), BF16),
            pltpu.VMEM((3, 768, 1152), BF16),
            pltpu.VMEM((4, 2, 128, 1024), F32),
            pltpu.VMEM((2, 2, 1040, 128), F32),
            pltpu.VMEM((27 * CI, 128), F32),
            pltpu.VMEM((HALF, 128), F32),
            pltpu.VMEM((HALF, 128), F32),
            pltpu.VMEM((N_CHIP, 16, 128), F32),
            dma((8,)),
            dma((2, 2)),
            dma((3,)),
            dma((3,)),
            dma((3,)),
            dma((3,)),
            dma,
            dma,
            dma,
            dma((2,)),
            dma((6,)),
            dma((6,)),
            pltpu.SemaphoreType.REGULAR,
        ],
        compiler_params=pltpu.CompilerParams(
            collective_id=0, has_side_effects=True, vmem_limit_bytes=50 << 20
        ),
    )(fine_input, weights.transpose(0, 2, 1), norm_gain, norm_shift, cotangent)
    activated, grad_input, grad_weights = pl.pallas_call(
        hand_over,
        out_shape=tuple(jax.ShapeDtypeStruct(v.shape, F32) for v in (activated, grad_input, grad_weights)),
        in_specs=[any_space] * 3,
        out_specs=(any_space,) * 3,
        scratch_shapes=[dma((11,))],
        compiler_params=pltpu.CompilerParams(vmem_limit_bytes=1 << 20),
    )(activated, grad_input, grad_weights)
    activated, grad_weights = activated[None], grad_weights.reshape(27, CI, CO).transpose(0, 2, 1)
    return activated, grad_input, grad_weights, grad_gain.reshape(1), grad_shift.reshape(1)


def solution(mesh):
    placed = (
        P(None, "gx", "gy", None),
        P(),
        P(("gx", "gy")),
        P(("gx", "gy")),
        P(("gx", "gy"), None, None, None),
    )
    return jax.shard_map(
        local,
        mesh=mesh,
        in_specs=placed,
        out_specs=(
            P(("gx", "gy"), None, None, None),
            P(None, "gx", "gy", None),
            P(),
            P(("gx", "gy")),
            P(("gx", "gy")),
        ),
        check_vma=False,
    )
```
